128 devices in a mesh: seq: 32 (over z_hi, y, x), head: 4 (over z_lo, core).
Axes of the slice: x: 4, y: 4, z: 4 (z_hi: 2, z_lo: 2; z = z_hi * 2 + z_lo), core: 2. Of those that a mesh axis runs over, the one named last changes fastest.
Arguments:
- tokens: bfloat16 [8192, 2048], P('seq'), may hold values from -6 to 6
- query_weight: bfloat16 [2048, 2048], P('seq', 'head'), may hold values from -0.125 to 0.125
- key_weight: bfloat16 [2048, 1024], P('seq', 'head'), may hold values from -0.125 to 0.125
- value_weight: bfloat16 [2048, 1024], P('seq', 'head'), may hold values from -0.125 to 0.125
- gate_weight: bfloat16 [2048, 2048], P('seq', 'head'), may hold values from -0.125 to 0.125
- out_weight: bfloat16 [2048, 2048], P('head', 'seq'), may hold values from -2 to 2
- norm_gain: bfloat16 [2048], P('seq'), may hold values from 0.5 to 1.5
- query_gain: bfloat16 [128], P('seq'), may hold values from 0.5 to 1.5
- key_gain: bfloat16 [128], P('seq'), may hold values from 0.5 to 1.5
- inner_gate: bfloat16 [2048, 6144], P('seq', 'head'), may hold values from -0.125 to 0.125
- inner_lift: bfloat16 [2048, 6144], P('seq', 'head'), may hold values from -0.125 to 0.125
- inner_down: bfloat16 [6144, 2048], P('head', 'seq'), may hold values from -0.078125 to 0.078125
- inner_gain: bfloat16 [2048], P('seq'), may hold values from 0.5 to 1.5
- out_grad: bfloat16 [8192, 2048], P('seq'), may hold values from -6 to 6
- bucket_len: int32 [2], replicated, may hold values from 2176 to 6016, as said below
- seq_len: int32 [2], replicated, may hold values from 2049 to 6016, as said below
- home_block: int32 [32], replicated, may hold values from 0 to 31, as said below
Outputs:
- result: float32 [8192, 2048], P('seq')
- tokens_grad: float32 [8192, 2048], P('seq')
- query_weight_grad: float32 [2048, 2048], P('seq', 'head')
- key_weight_grad: float32 [2048, 1024], P('seq', 'head')
- value_weight_grad: float32 [2048, 1024], P('seq', 'head')
- gate_weight_grad: float32 [2048, 2048], P('seq', 'head')
- out_weight_grad: float32 [2048, 2048], P('head', 'seq')
- norm_gain_grad: float32 [2048], P('seq')
- query_gain_grad: float32 [128], P('seq')
- key_gain_grad: float32 [128], P('seq')
- inner_gate_grad: float32 [2048, 6144], P('seq', 'head')
- inner_lift_grad: float32 [2048, 6144], P('seq', 'head')
- inner_down_grad: float32 [6144, 2048], P('head', 'seq')
- inner_gain_grad: float32 [2048], P('seq')
The draws below stay inside these ranges and needn't reach their ends.
Inputs may be any that keep to these rules, and one draw needn't show every extreme that they name: `bucket_len`: the 2 buckets are multiples of 128 and fill the 8192 stream positions end to end. Sequence s fills the first seq_len[s] positions of bucket s; fewer than 128 positions of a bucket are padding. `home_block`: A permutation of the 32 stream blocks.
All inputs are finite; a program needn't handle non-finite values.
Results may differ from the reference program's by a relative error of at most 0.035.
Values may be sent and summed in bfloat16 or wider, within the bound.
No kernel may reach another device: no remote copies, remote signals or barrier semaphores. Data moves between devices by JAX's collectives and lax.ppermute only.
A program may use at most 192 MiB of HBM per device.

```python
import jax
import jax.numpy as jnp
from jax import lax

D = 2048
HQ = 16
HK = 8
HD = 128
FF = 6144
TOK_DEV = 256
MIN_LEN = 2048
BUCKET = 128
TOKENS = 8192
SEQS = 2
BLOCKS = 32


def plan_stream(key):
    subkeys = jax.random.split(key, 5)
    unit_least = MIN_LEN // BUCKET + 1
    unit_total = TOKENS // BUCKET
    longest = jax.random.randint(subkeys[0], (), 0, SEQS)
    number = jnp.arange(SEQS, dtype=jnp.int32)
    others = jnp.where(number == longest, 0, unit_least).astype(jnp.int32)
    units = jnp.where(number == longest, unit_total - jnp.sum(others), others).astype(jnp.int32)
    bucket = (units * BUCKET).astype(jnp.int32)
    padding = jnp.where(number == longest, 0, jax.random.randint(subkeys[2], (SEQS,), 0, BUCKET)).astype(jnp.int32)
    length = (bucket - padding).astype(jnp.int32)
    starts = (jnp.cumsum(bucket) - bucket).astype(jnp.int32)
    first_block = (jnp.sum(jnp.where(number == longest, starts, 0)) // TOK_DEV).astype(jnp.int32)
    ordering = jax.random.permutation(subkeys[3], BLOCKS).astype(jnp.int32)
    rotation = jax.random.randint(subkeys[4], (), 0, 3)
    targets = jnp.array([0, BLOCKS - 1, BLOCKS // 2], dtype=jnp.int32)
    for rounds in range(3):
        target = targets[(rounds + rotation) % 3]
        wanted = (first_block + rounds).astype(jnp.int32)
        found = jnp.argmax(ordering == wanted)
        holder = ordering[target]
        ordering = ordering.at[found].set(holder).at[target].set(wanted)
    return (bucket, length, ordering)


def draw_bucket_len(key, part):
    bucket, length, ordering = plan_stream(key)
    return bucket


def draw_seq_len(key, part):
    bucket, length, ordering = plan_stream(key)
    return length


def draw_home_block(key, part):
    bucket, length, ordering = plan_stream(key)
    return ordering


def shard_levels(stream_key, extent, pieces, low, high):
    level = 1.0
    for dim, shards_of in pieces:
        draws = jax.random.uniform(jax.random.fold_in(jax.random.fold_in(stream_key, 6), dim), (shards_of,), jnp.float32, low / len(pieces), high / len(pieces))
        level = level * jnp.repeat(jnp.exp(draws), extent[dim] // shards_of).reshape((-1,) + (1,) * (len(extent) - 1 - dim))
    return level


def centred(stream_key, dims, scale, limit, pieces=(), held_as=jnp.bfloat16):
    loudness = shard_levels(stream_key, dims, pieces, -0.22, 0.18) if pieces else 1.0
    values = jax.random.normal(stream_key, dims, jnp.float32) * scale * loudness
    return jnp.minimum(jnp.maximum(values, -limit), limit).astype(held_as)


def setup_inputs(seed: int = 0) -> dict:
    arg_keys = jax.random.split(jax.random.key(seed), 18)
    return {
        "tokens": centred(arg_keys[0], (TOKENS, D), 1.0, 6.0, ((0, 32),)),
        "query_weight": centred(arg_keys[1], (D, HQ * HD), D ** -0.5, 0.125, ((0, 32), (1, 4))),
        "key_weight": centred(arg_keys[2], (D, HK * HD), D ** -0.5, 0.125, ((0, 32), (1, 4))),
        "value_weight": centred(arg_keys[3], (D, HK * HD), D ** -0.5, 0.125, ((0, 32), (1, 4))),
        "gate_weight": centred(arg_keys[4], (D, HQ * HD), D ** -0.5, 0.125, ((0, 32), (1, 4))),
        "out_weight": centred(arg_keys[5], (HQ * HD, D), 8 ** -0.5, 2.0, ((0, 4), (1, 32))),
        "norm_gain": jnp.clip(1.0 + 0.1 * jax.random.normal(arg_keys[6], (D,), jnp.float32), 0.5, 1.5).astype(jnp.bfloat16),
        "query_gain": jnp.clip(1.0 + 0.1 * jax.random.normal(arg_keys[7], (HD,), jnp.float32), 0.5, 1.5).astype(jnp.bfloat16),
        "key_gain": jnp.clip(1.0 + 0.1 * jax.random.normal(arg_keys[8], (HD,), jnp.float32), 0.5, 1.5).astype(jnp.bfloat16),
        "inner_gate": centred(arg_keys[9], (D, FF), D ** -0.5, 0.125, ((0, 32), (1, 4))),
        "inner_lift": centred(arg_keys[10], (D, FF), D ** -0.5, 0.125, ((0, 32), (1, 4))),
        "inner_down": centred(arg_keys[11], (FF, D), FF ** -0.5, 0.078125, ((0, 4), (1, 32))),
        "inner_gain": jnp.clip(1.0 + 0.1 * jax.random.normal(arg_keys[12], (D,), jnp.float32), 0.5, 1.5).astype(jnp.bfloat16),
        "out_grad": centred(arg_keys[13], (TOKENS, D), 1.0, 6.0, ((0, 32),)),
        "bucket_len": draw_bucket_len(jax.random.fold_in(arg_keys[17], 71), 0),
        "seq_len": draw_seq_len(jax.random.fold_in(arg_keys[17], 71), 0),
        "home_block": draw_home_block(jax.random.fold_in(arg_keys[17], 71), 0),
    }


EPS = 1e-06
THETA = 1000000.0
HIGHEST = lax.Precision.HIGHEST

@jax.custom_vjp
def low(v):
    return lax.optimization_barrier(v.astype(jnp.bfloat16)).astype(jnp.float32)

@jax.custom_vjp
def low_back(v):
    return v

def low_keep(v):
    return (low(v), None)

def low_pass(kept, grad):
    return (grad,)

def back_keep(v):
    return (v, None)

def back_low(kept, grad):
    return (low(grad),)
low.defvjp(low_keep, low_pass)
low_back.defvjp(back_keep, back_low)

def product(left, right):
    return jnp.dot(left, right, precision=HIGHEST, preferred_element_type=jnp.float32)

def stream_info(first, count, block_rows, bucket_len, seq_len, home_block):
    row_ids = first + jnp.arange(count, dtype=jnp.int32)
    device = row_ids // block_rows
    slots = jnp.arange(home_block.shape[0], dtype=jnp.int32)
    block = lax.optimization_barrier(jnp.sum(jnp.where(device[:, None] == slots[None, :], home_block[None, :], 0), axis=1)).astype(jnp.int32)
    place = (block * block_rows + row_ids % block_rows).astype(jnp.int32)
    ends = jnp.cumsum(bucket_len).astype(jnp.int32)
    starts = (ends - bucket_len).astype(jnp.int32)
    inside = (place[:, None] >= starts[None, :]) & (place[:, None] < ends[None, :])
    number = jnp.arange(bucket_len.shape[0], dtype=jnp.int32)
    owner = lax.optimization_barrier(jnp.sum(jnp.where(inside, number[None, :], 0), axis=1)).astype(jnp.int32)
    offset = (place - lax.optimization_barrier(jnp.sum(jnp.where(inside, starts[None, :], 0), axis=1))).astype(jnp.int32)
    valid = offset < lax.optimization_barrier(jnp.sum(jnp.where(inside, seq_len[None, :], 0), axis=1))
    return (place, owner, offset, valid)

def rotary(offset, half):
    freq = jnp.power(THETA, -jnp.arange(half, dtype=jnp.float32) * 2.0 / (2 * half))
    angle = offset.astype(jnp.float32)[:, None] * freq[None, :]
    return (jnp.cos(angle)[:, None, :], jnp.sin(angle)[:, None, :])

def turn(value, cosine, sine):
    half = value.shape[-1] // 2
    first_half = value[..., :half]
    second_half = value[..., half:]
    return jnp.concatenate([first_half * cosine - second_half * sine, second_half * cosine + first_half * sine], axis=-1)

def row_norm(value, gain):
    return value * lax.rsqrt(lax.optimization_barrier(jnp.mean(value * value, axis=-1, keepdims=True)) + EPS) * gain

def attention(query, key_rot, value, place, owner, valid):
    block = min(512, TOKENS)
    scale = HD ** (-0.5)

    def one_block(index):
        start = (index * block).astype(jnp.int32)
        query_rows = lax.dynamic_slice_in_dim(query, start, block, 0)
        query_place = lax.dynamic_slice_in_dim(place, start, block, 0)
        query_owner = lax.dynamic_slice_in_dim(owner, start, block, 0)
        visible = (query_owner[:, None] == owner[None, :]) & (place[None, :] <= query_place[:, None]) & valid[None, :]
        score = low_back(jnp.einsum('qhgd,khd->hgqk', query_rows, key_rot, precision=HIGHEST)) * scale
        masked = jnp.where(visible, score, -1e+30)
        summit = lax.optimization_barrier(jnp.max(masked, axis=-1, keepdims=True))
        weight = jnp.where(visible, jnp.exp(masked - summit), 0.0)
        prob = weight / lax.optimization_barrier(jnp.sum(weight, axis=-1, keepdims=True))
        return jnp.einsum('hgqk,khd->qhgd', low(prob), value, precision=HIGHEST)
    blocks_out = lax.map(jax.checkpoint(one_block), jnp.arange(TOKENS // block, dtype=jnp.int32))
    return blocks_out.reshape(TOKENS, HQ * HD)

def layer(tokens, query_weight, key_weight, value_weight, gate_weight, out_weight, norm_gain, query_gain, key_gain, inner_gate, inner_lift, inner_down, inner_gain, place, owner, offset, valid):
    group = HQ // HK
    cosine, sine = rotary(offset, HD // 2)
    normed = low(row_norm(tokens, norm_gain))
    q_pre = low_back(product(normed, query_weight)).reshape(TOKENS, HQ, HD)
    k_pre = low_back(product(normed, key_weight)).reshape(TOKENS, HK, HD)
    value = low(low_back(product(normed, value_weight))).reshape(TOKENS, HK, HD)
    gate_pre = low_back(product(normed, gate_weight))
    query = low(turn(row_norm(q_pre, query_gain), cosine, sine)).reshape(TOKENS, HK, group, HD)
    key_rot = low(turn(row_norm(k_pre, key_gain), cosine, sine))
    attended = low_back(attention(query, key_rot, value, place, owner, valid))
    gated = low(attended * jax.nn.sigmoid(gate_pre))
    mixed_in = tokens + low_back(product(gated, out_weight))
    normed_two = low(row_norm(mixed_in, inner_gain))
    gate_val = low_back(product(normed_two, inner_gate))
    lift_val = low_back(product(normed_two, inner_lift))
    hidden = low(jax.nn.silu(gate_val) * lift_val)
    return mixed_in + low_back(product(hidden, inner_down))

def reference(tokens, query_weight, key_weight, value_weight, gate_weight, out_weight, norm_gain, query_gain, key_gain, inner_gate, inner_lift, inner_down, inner_gain, out_grad, bucket_len, seq_len, home_block):
    place, owner, offset, valid = stream_info(0, TOKENS, TOK_DEV, bucket_len, seq_len, home_block)

    def forward(tok_in, wq_in, wk_in, wv_in, wg_in, wo_in, gn_in, gq_in, gk_in, wa_in, wb_in, wd_in, gf_in):
        return layer(tok_in, wq_in, wk_in, wv_in, wg_in, wo_in, gn_in, gq_in, gk_in, wa_in, wb_in, wd_in, gf_in, place, owner, offset, valid)
    result, pullback = jax.vjp(forward, tokens.astype(jnp.float32), query_weight.astype(jnp.float32), key_weight.astype(jnp.float32), value_weight.astype(jnp.float32), gate_weight.astype(jnp.float32), out_weight.astype(jnp.float32), norm_gain.astype(jnp.float32), query_gain.astype(jnp.float32), key_gain.astype(jnp.float32), inner_gate.astype(jnp.float32), inner_lift.astype(jnp.float32), inner_down.astype(jnp.float32), inner_gain.astype(jnp.float32))
    grads = pullback(out_grad.astype(jnp.float32))
    return (result, grads[0], grads[1], grads[2], grads[3], grads[4], grads[5], grads[6], grads[7], grads[8], grads[9], grads[10], grads[11], grads[12])
```

```python
import jax
import jax.numpy as jnp
from jax import lax
from jax.experimental import pallas as pl
from jax.experimental.pallas import tpu as pltpu
from jax.sharding import Mesh
from jax.sharding import PartitionSpec as P

HD = 128
BLOCK = 256
EPS = 1e-06
THETA = 1000000.0
LOG2E = 1.4426950408889634
SCALE = HD ** (-0.5)
PLANE = ("y", "x")
bfloat = jnp.bfloat16
single = jnp.float32


def turn(value, cosine, sine):
    half = value.shape[-1] // 2
    first_half = value[..., :half]
    second_half = value[..., half:]
    return jnp.concatenate(
        [first_half * cosine - second_half * sine, second_half * cosine + first_half * sine],
        axis=-1,
    )


def turn_back(grad, cosine, sine):
    half = grad.shape[-1] // 2
    first_half = grad[..., :half]
    second_half = grad[..., half:]
    return jnp.concatenate(
        [first_half * cosine + second_half * sine, second_half * cosine - first_half * sine],
        axis=-1,
    )


def rms_parts(value):
    factor = lax.rsqrt(jnp.mean(value * value, axis=-1, keepdims=True) + EPS)
    return (value * factor, factor)


def rms_back(grad, unit_val, factor, gain):
    scaled = grad * gain
    return factor * (scaled - unit_val * jnp.mean(unit_val * scaled, axis=-1, keepdims=True))


def swap(value, axis):
    return lax.ppermute(value, axis, [(0, 1), (1, 0)])


def swap_both(value):
    return lax.ppermute(value, ("zh", "zl"), [(0, 3), (1, 2), (2, 1), (3, 0)])


def line_sum(near, far):
    here = near + swap(far.astype(bfloat), "c").astype(single)
    sent = here.astype(bfloat)
    one = swap(sent[64:128], "zl").astype(single)
    two = swap(sent[128:192], "zh").astype(single)
    three = swap_both(sent[192:256]).astype(single)
    return (here[:64] + one) + (two + three)


def line_gather(own):
    near = jnp.concatenate([own, swap(own, "zl"), swap(own, "zh"), swap_both(own)], axis=0)
    return jnp.concatenate([near, swap(near, "c")], axis=0)


def small_sum(value):
    value = value + swap(value, "c")
    return (value + swap(value, "zl")) + (swap(value, "zh") + swap_both(value))


def head_gather(own, mine):
    near = jnp.concatenate([own, swap(own, "zl")], axis=0)
    parts = jnp.concatenate([near, swap(near, "c")], axis=0).reshape(4, 64, -1)
    order = (0, 2, 1, 3)
    rows = []
    for place in range(4):
        other = place ^ mine
        slot = (other & 1) * 2 + (other >> 1)
        rows.append(lax.dynamic_index_in_dim(parts, slot, 0, keepdims=False))
    return jnp.concatenate(rows, axis=0).astype(single)


def row_place(index, zl, c):
    core = (index >> 7) & 1
    low = (index >> 6) & 1
    return ((low ^ zl) * 2 + (core ^ c)) * 64 + (index & 63)


def block_range(block, cut, ends):
    first = block * BLOCK
    last = first + BLOCK - 1
    low_least = jnp.where(first >= cut, cut, 0)
    low_most = jnp.where(last >= cut, cut, 0)
    high_least = jnp.minimum(first, jnp.where(first >= cut, ends[1], ends[0]))
    start = low_least // BLOCK
    whole = jnp.minimum((low_most + BLOCK - 1) // BLOCK, block + 1)
    whole_end = jnp.maximum((high_least + 1) // BLOCK, whole)
    return start, whole, whole_end, block + 1


def stacked(ref, half, low):
    near = half * 128
    return jnp.concatenate(
        [
            ref[near : near + 128, 0:HD],
            ref[256 + near : 384 + near, 0:HD],
            ref[near : near + 128, HD : 2 * HD],
            ref[256 + near : 384 + near, HD : 2 * HD],
        ],
        axis=0,
    )


def unstack(ref, half, value):
    near = half * 128
    ref[near : near + 128, 0:HD] = value[0:128]
    ref[256 + near : 384 + near, 0:HD] = value[128:256]
    ref[near : near + 128, HD : 2 * HD] = value[256:384]
    ref[256 + near : 384 + near, HD : 2 * HD] = value[384:512]


def key_rows(ref, plane, half, column):
    near = pl.multiple_of(half * 128, 128)
    far = pl.multiple_of(256 + half * 128, 128)
    columns = slice(column * HD, (column + 1) * HD)
    return jnp.concatenate(
        [ref[plane, pl.ds(near, 128), columns], ref[plane, pl.ds(far, 128), columns]], axis=0
    )


def dot_nt(left, right):
    return lax.dot_general(left, right, (((1,), (1,)), ((), ())), preferred_element_type=single)


def dot_tn(left, right):
    return lax.dot_general(left, right, (((0,), (0,)), ((), ())), preferred_element_type=single)


def find_blocks(home, where):
    for slot in range(32):
        where[home[slot]] = slot


def tile_limits(info, half):
    zl, c, cut = info[2], info[3], info[5]
    ends = (info[6] - 1, cut + info[7] - 1)
    block = info[half]
    place = block * BLOCK + row_place(lax.broadcasted_iota(jnp.int32, (1, 512), 1), zl, c)
    second = place >= cut
    low = jnp.where(second, cut, 0)
    high = jnp.minimum(place, jnp.where(second, ends[1], ends[0]))
    return low, high, block_range(block, cut, ends)


def over_blocks(limits, step):
    start, whole, whole_end, stop = limits
    lax.fori_loop(start, whole, lambda block, _: step(block, True), None)
    lax.fori_loop(whole, whole_end, lambda block, _: step(block, False), None)
    lax.fori_loop(whole_end, stop, lambda block, _: step(block, True), None)


def attend_kernel(info, home, query, pairs, out, logs, where, accum, total):
    find_blocks(home, where)
    zh = info[4]
    key_place = row_place(lax.broadcasted_iota(jnp.int32, (256, 512), 0), info[2], info[3])
    for half in range(2):
        low, high, limits = tile_limits(info, half)
        rows = stacked(query, half, None)
        accum[...] = jnp.zeros_like(accum)
        total[...] = jnp.zeros_like(total)

        def step(block, masked):
            slot = where[block]
            plane = slot & 15
            side = (slot >> 4) ^ zh
            score = dot_nt(key_rows(pairs, plane, side, 0), rows)
            weight = jnp.exp2(score * (SCALE * LOG2E))
            if masked:
                place = key_place + block * BLOCK
                weight = jnp.where((place >= low) & (place <= high), weight, 0.0)
            total[...] += jnp.sum(weight, axis=0, keepdims=True)
            accum[...] += dot_tn(key_rows(pairs, plane, side, 1), weight.astype(bfloat))

        over_blocks(limits, step)
        logs[half] = jnp.log2(total[...])
        unstack(out, half, jnp.transpose(accum[...] / total[...]))


def attend_back_kernel(
    info, home, query, d_out, out, pairs, logs, d_query, d_pairs, where, accum, d_rows
):
    find_blocks(home, where)
    zh = info[4]
    key_place = row_place(lax.broadcasted_iota(jnp.int32, (256, 512), 0), info[2], info[3])

    def clear(index, _):
        accum[index] = jnp.zeros(accum.shape[1:], single)

    lax.fori_loop(0, accum.shape[0], clear, None)
    for half in range(2):
        low, high, limits = tile_limits(info, half)
        rows = stacked(query, half, None)
        grads = stacked(d_out, half, None)
        delta = jnp.sum(
            jnp.transpose(grads.astype(single) * stacked(out, half, None)), axis=0, keepdims=True
        )
        log = logs[half]
        d_rows[...] = jnp.zeros_like(d_rows)

        def step(block, masked):
            slot = where[block]
            plane = slot & 15
            side = (slot >> 4) ^ zh
            keys = key_rows(pairs, plane, side, 0)
            values = key_rows(pairs, plane, side, 1)
            prob = jnp.exp2(dot_nt(keys, rows) * (SCALE * LOG2E) - log)
            if masked:
                place = key_place + block * BLOCK
                prob = jnp.where((place >= low) & (place <= high), prob, 0.0)
            d_score = (prob * (dot_nt(values, grads) - delta)).astype(bfloat)
            d_value = jnp.dot(prob.astype(bfloat), grads, preferred_element_type=single)
            d_key = jnp.dot(d_score, rows, preferred_element_type=single)
            d_rows[...] += dot_tn(keys, d_score)
            near = pl.multiple_of(side * 128, 128)
            far = pl.multiple_of(256 + side * 128, 128)
            accum[plane, pl.ds(near, 128), 0:HD] += d_key[0:128]
            accum[plane, pl.ds(far, 128), 0:HD] += d_key[128:256]
            accum[plane, pl.ds(near, 128), HD : 2 * HD] += d_value[0:128]
            accum[plane, pl.ds(far, 128), HD : 2 * HD] += d_value[128:256]

        over_blocks(limits, step)
        unstack(d_query, half, jnp.transpose(d_rows[...]) * SCALE)

    def finish(index, _):
        d_pairs[index, :, 0:HD] = (accum[index, :, 0:HD] * SCALE).astype(bfloat)
        d_pairs[index, :, HD : 2 * HD] = accum[index, :, HD : 2 * HD].astype(bfloat)

    lax.fori_loop(0, accum.shape[0], finish, None)


VMEM = pl.BlockSpec(memory_space=pltpu.VMEM)
SMEM = pl.BlockSpec(memory_space=pltpu.SMEM)


def attend(info, home, query, pairs):
    return pl.pallas_call(
        attend_kernel,
        out_shape=(
            jax.ShapeDtypeStruct((512, 2 * HD), single),
            jax.ShapeDtypeStruct((2, 1, 512), single),
        ),
        in_specs=[SMEM, SMEM, VMEM, VMEM],
        out_specs=(VMEM, VMEM),
        scratch_shapes=[
            pltpu.SMEM((32,), jnp.int32),
            pltpu.VMEM((HD, 512), single),
            pltpu.VMEM((1, 512), single),
        ],
        compiler_params=pltpu.CompilerParams(vmem_limit_bytes=32 * 2**20),
        cost_estimate=pl.CostEstimate(
            flops=4 * 2**30, bytes_accessed=6 * 2**20, transcendentals=4 * 2**20
        ),
        name="attend",
    )(info, home, query, pairs)


def attend_back(info, home, query, d_out, out, pairs, logs):
    return pl.pallas_call(
        attend_back_kernel,
        out_shape=(
            jax.ShapeDtypeStruct((512, 2 * HD), single),
            jax.ShapeDtypeStruct(pairs.shape, bfloat),
        ),
        in_specs=[SMEM, SMEM, VMEM, VMEM, VMEM, VMEM, VMEM],
        out_specs=(VMEM, VMEM),
        scratch_shapes=[
            pltpu.SMEM((32,), jnp.int32),
            pltpu.VMEM(pairs.shape, single),
            pltpu.VMEM((HD, 512), single),
        ],
        compiler_params=pltpu.CompilerParams(vmem_limit_bytes=40 * 2**20),
        cost_estimate=pl.CostEstimate(
            flops=10 * 2**30, bytes_accessed=12 * 2**20, transcendentals=4 * 2**20
        ),
        name="attend_back",
    )(info, home, query, d_out, out, pairs, logs)


def columns_of(weight, side, width):
    return lax.dynamic_slice_in_dim(weight, side * width, width, 1)


def rows_of(weight, side, width):
    return lax.dynamic_slice_in_dim(weight, side * width, width, 0)


def in_order(zh, own, other, axis):
    first = jnp.where(zh == 0, own, other)
    second = jnp.where(zh == 0, other, own)
    return jnp.concatenate([first, second], axis=axis)


def gather_plane(block):
    whole = lax.all_gather(block, PLANE, axis=1, tiled=True)
    return whole.reshape(-1, block.shape[-1])


def per_device(
    tokens,
    query_weight,
    key_weight,
    value_weight,
    gate_weight,
    out_weight,
    norm_gain,
    query_gain,
    key_gain,
    inner_gate,
    inner_lift,
    inner_down,
    inner_gain,
    out_grad,
    bucket_len,
    seq_len,
    home_block,
):
    zh = lax.axis_index("zh")
    zl = lax.axis_index("zl")
    c = lax.axis_index("c")
    mine = zl * 2 + c
    width = tokens.shape[1]
    seq_index = zh * 16 + lax.axis_index("y") * 4 + lax.axis_index("x")
    block_own = lax.dynamic_index_in_dim(home_block, seq_index, 0, keepdims=False)
    block_other = lax.dynamic_index_in_dim(home_block, seq_index ^ 16, 0, keepdims=False)
    info = jnp.stack(
        [block_own, block_other, zl, c, zh, bucket_len[0], seq_len[0], seq_len[1]]
    ).astype(jnp.int32)

    def column(vector):
        return jnp.pad(vector, (0, 64 - vector.shape[0]))[:, None]

    gain_columns = jnp.pad(
        jnp.concatenate(
            [column(norm_gain), column(inner_gain), column(query_gain), column(key_gain)], axis=1
        ),
        ((0, 0), (0, 124)),
    )

    def outer_pack(side):
        return jnp.concatenate(
            [
                columns_of(query_weight, side, 256),
                columns_of(key_weight, side, 128),
                columns_of(value_weight, side, 128),
                columns_of(gate_weight, side, 256),
                rows_of(out_weight, side, 256).T,
                gain_columns,
            ],
            axis=1,
        )

    def inner_pack(side):
        return jnp.concatenate(
            [
                columns_of(inner_gate, side, 768),
                columns_of(inner_lift, side, 768),
                rows_of(inner_down, side, 768).T,
            ],
            axis=1,
        )

    def pair_up(pack):
        own = pack(zh)
        other = swap(pack(1 - zh), "zh")
        return in_order(zh, own[None], other[None], 0)

    outer = gather_plane(pair_up(outer_pack))
    inner = gather_plane(pair_up(inner_pack))

    def line_rows(rows):
        other = swap(rows, "zh")
        pieces = []
        for core in range(2):
            for source in (rows, other):
                for low in range(2):
                    pieces.append(rows_of(source, mine ^ (low * 2 + core), 64))
        return jnp.concatenate(pieces, axis=0)

    rows_in = line_rows(tokens)
    rows_grad = line_rows(out_grad)

    gains = outer[:, 1024:1028].astype(single).T
    gain_norm = gains[0:1]
    gain_inner = gains[1:2]
    gain_query = gains[2].reshape(32, 64)[:, :4].reshape(HD)
    gain_key = gains[3].reshape(32, 64)[:, :4].reshape(HD)
    w_outer = outer[:, :768]
    w_out = outer[:, 768:1024]
    w_gate_lift = inner[:, :1536]
    w_down = inner[:, 1536:]

    index = jnp.arange(512, dtype=jnp.int32)
    half_of = (index >> 7) & 1
    place = jnp.where(half_of == 0, block_own, block_other) * BLOCK + row_place(
        ((index >> 8) << 7) | (index & 127), zl, c
    )
    offset = jnp.where(place >= bucket_len[0], place - bucket_len[0], place)
    freq = jnp.power(THETA, -jnp.arange(HD // 2, dtype=single) * 2.0 / HD)
    angle = offset.astype(single)[:, None] * freq[None, :]
    cosine = jnp.cos(angle)[:, None, :]
    sine = jnp.sin(angle)[:, None, :]

    inputs = rows_in.astype(single)
    unit_in, factor_in = rms_parts(inputs)
    normed = (unit_in * gain_norm).astype(bfloat)
    pre = jnp.dot(normed, w_outer, preferred_element_type=single)
    q_unit, q_factor = rms_parts(pre[:, :256].reshape(512, 2, HD))
    k_unit, k_factor = rms_parts(pre[:, 256:384].reshape(512, 1, HD))
    gate_sig = jax.nn.sigmoid(pre[:, 512:768])
    query = turn(q_unit * gain_query, cosine, sine).astype(bfloat).reshape(512, 256)
    key_rot = turn(k_unit * gain_key, cosine, sine).astype(bfloat).reshape(512, HD)
    pairs = lax.all_gather(
        jnp.concatenate([key_rot, pre[:, 384:512].astype(bfloat)], axis=1), PLANE, axis=0
    )
    attended, logs = attend(info, home_block, query, pairs)
    gated = (attended * gate_sig).astype(bfloat)

    def line_product(left, right):
        return line_sum(dot_nt(left[:256], right), dot_nt(left[256:], right))

    mixed_in = inputs[:64] + line_product(gated, w_out)
    unit_two, factor_two = rms_parts(mixed_in)
    normed_two = line_gather((unit_two * gain_inner).astype(bfloat))
    d_hidden = jnp.dot(rows_grad, w_down, preferred_element_type=single)
    gate_lift = jnp.dot(normed_two, w_gate_lift, preferred_element_type=single)
    gate_val = gate_lift[:, :768]
    lift_val = gate_lift[:, 768:]
    gate_act = jax.nn.sigmoid(gate_val)
    hidden = (gate_val * gate_act * lift_val).astype(bfloat)
    d_gate = (d_hidden * lift_val * gate_act * (1.0 + gate_val * (1.0 - gate_act))).astype(bfloat)
    d_lift = (d_hidden * gate_val * gate_act).astype(bfloat)
    d_gate_lift = jnp.concatenate([d_gate, d_lift], axis=1)
    d_normed_two = line_product(d_gate_lift, w_gate_lift)
    grad_inner = jnp.concatenate(
        [
            dot_tn(normed_two, d_gate_lift).astype(bfloat),
            dot_tn(rows_grad, hidden).astype(bfloat),
        ],
        axis=1,
    )

    def scatter_plane(grad):
        return lax.psum_scatter(
            grad.reshape(2, -1, grad.shape[-1]), PLANE, scatter_dimension=1, tiled=True
        )

    inner_part = scatter_plane(grad_inner)
    result_rows = mixed_in + line_product(hidden, w_down)
    d_mixed = rows_grad[:64].astype(single) + rms_back(
        d_normed_two, unit_two, factor_two, gain_inner
    )
    d_attn = line_gather(d_mixed.astype(bfloat))
    d_gated = jnp.dot(d_attn, w_out, preferred_element_type=single)
    d_attended = (d_gated * gate_sig).astype(bfloat)
    d_gate_pre = (d_gated * attended * gate_sig * (1.0 - gate_sig)).astype(bfloat)
    d_query, d_pairs = attend_back(info, home_block, query, d_attended, attended, pairs, logs)
    received = lax.all_to_all(d_pairs, PLANE, 0, 0, tiled=True)
    d_pair = jnp.sum(received.astype(single), axis=0)
    d_q_turned = turn_back(d_query.reshape(512, 2, HD), cosine, sine)
    d_k_turned = turn_back(d_pair[:, None, :HD], cosine, sine)
    query_gain_part = jnp.sum(d_q_turned * q_unit, axis=(0, 1))
    key_gain_part = jnp.sum(d_k_turned * k_unit, axis=(0, 1))
    d_q_pre = rms_back(d_q_turned, q_unit, q_factor, gain_query).astype(bfloat).reshape(512, 256)
    d_k_pre = rms_back(d_k_turned, k_unit, k_factor, gain_key).astype(bfloat).reshape(512, HD)
    d_kv_pre = jnp.concatenate([d_k_pre, d_pair[:, HD:].astype(bfloat)], axis=1)
    outer_part = scatter_plane(
        jnp.concatenate(
            [
                dot_tn(normed, jnp.concatenate([d_q_pre, d_gate_pre], axis=1)).astype(bfloat),
                dot_tn(d_attn, gated).astype(bfloat),
            ],
            axis=1,
        )
    )
    grad_pairs = dot_tn(normed, d_kv_pre).astype(bfloat)

    def by_plane(vector):
        return jnp.transpose(vector.reshape(2, 16, 4), (1, 0, 2)).reshape(16, 8)

    gain_rows = jnp.concatenate([by_plane(query_gain_part), by_plane(key_gain_part)], axis=1)
    gain_rows = jnp.pad(gain_rows.astype(bfloat)[:, None, :], ((0, 0), (0, 15), (0, 240)))
    pairs_sent = jnp.concatenate(
        [
            jnp.transpose(grad_pairs.reshape(2, 16, 64, 256), (1, 0, 2, 3)).reshape(16, 128, 256),
            gain_rows,
        ],
        axis=1,
    )
    pairs_got = lax.all_to_all(pairs_sent, PLANE, 0, 0, tiled=True)
    pairs_sum = jnp.sum(pairs_got.astype(single), axis=0)
    pair_part = pairs_sum[:128].reshape(2, 64, 256)
    gain_part = pairs_sum[128, :16].reshape(2, 2, 4)

    d_pre = jnp.concatenate([d_q_pre, d_kv_pre, d_gate_pre], axis=1)
    d_normed = line_product(d_pre, w_outer)
    token_rows = d_mixed + rms_back(d_normed, unit_in[:64], factor_in[:64], gain_norm)

    def both_sides(part):
        own = lax.dynamic_index_in_dim(part, zh, 0, keepdims=False).astype(single)
        sent = lax.dynamic_index_in_dim(part, 1 - zh, 0, keepdims=False)
        return own, swap(sent.astype(bfloat), "zh").astype(single)

    inner_own, inner_got = both_sides(inner_part)
    outer_own, outer_got = both_sides(outer_part)
    pair_own, pair_got = both_sides(pair_part)

    def shard(own, got, start, count):
        return in_order(zh, own[:, start : start + count], got[:, start : start + count], 1)

    shard_igate = shard(inner_own, inner_got, 0, 768)
    shard_ilift = shard(inner_own, inner_got, 768, 768)
    shard_idown = shard(inner_own, inner_got, 1536, 768).T
    shard_query = shard(outer_own, outer_got, 0, 256)
    shard_gate = shard(outer_own, outer_got, 256, 256)
    shard_out = shard(outer_own, outer_got, 512, 256).T
    shard_key = shard(pair_own, pair_got, 0, 128)
    shard_value = shard(pair_own, pair_got, 128, 128)

    def weighted(weight, grad):
        return jnp.sum(weight.astype(single) * grad, axis=1)

    norm_part = (
        weighted(query_weight, shard_query)
        + weighted(key_weight, shard_key)
        + weighted(value_weight, shard_value)
        + weighted(gate_weight, shard_gate)
    ) / norm_gain.astype(single)
    inner_gain_part = (
        weighted(inner_gate, shard_igate) + weighted(inner_lift, shard_ilift)
    ) / inner_gain.astype(single)
    both = jnp.concatenate([norm_part, inner_gain_part])
    gain_line = jnp.concatenate(
        [
            jnp.where(zh == 0, both, 0.0),
            jnp.where(zh == 1, both, 0.0),
            gain_part.reshape(16),
            jnp.zeros((112,), single),
        ]
    ).reshape(3, HD)
    gain_line = small_sum(gain_line)
    gain_own = lax.dynamic_index_in_dim(gain_line, zh, 0, keepdims=False)
    gain_sides = lax.dynamic_index_in_dim(
        gain_line[2, :16].reshape(2, 2, 4), zh, 1, keepdims=False
    )

    def rounded(rows):
        return lax.reduce_precision(rows, 8, 7).astype(bfloat)

    result = head_gather(rounded(result_rows), mine)
    tokens_grad = head_gather(rounded(token_rows), mine)
    return (
        result,
        tokens_grad,
        shard_query,
        shard_key,
        shard_value,
        shard_gate,
        shard_out,
        gain_own[:64],
        gain_sides[0],
        gain_sides[1],
        shard_igate,
        shard_ilift,
        shard_idown,
        gain_own[64:],
    )


def solution(mesh):
    fine = Mesh(mesh.devices.reshape(2, 4, 4, 2, 2), ("zh", "y", "x", "zl", "c"))
    seq = ("zh", "y", "x")
    head = ("zl", "c")
    in_specs = (
        P(seq, None),
        P(seq, head),
        P(seq, head),
        P(seq, head),
        P(seq, head),
        P(head, seq),
        P(seq),
        P(seq),
        P(seq),
        P(seq, head),
        P(seq, head),
        P(head, seq),
        P(seq),
        P(seq, None),
        P(),
        P(),
        P(),
    )
    out_specs = (
        P(seq, None),
        P(seq, None),
        P(seq, head),
        P(seq, head),
        P(seq, head),
        P(seq, head),
        P(head, seq),
        P(seq),
        P(seq),
        P(seq),
        P(seq, head),
        P(seq, head),
        P(head, seq),
        P(seq),
    )
    return jax.shard_map(
        per_device, mesh=fine, in_specs=in_specs, out_specs=out_specs, check_vma=False
    )
```

```python
import jax
import jax.numpy as jnp
from jax import lax
from jax.experimental import pallas as pl
from jax.experimental.pallas import tpu as pltpu
from jax.sharding import Mesh
from jax.sharding import PartitionSpec as P

HD = 128
BLOCK = 256
EPS = 1e-06
THETA = 1000000.0
LOG2E = 1.4426950408889634
SCALE = HD ** (-0.5)
PLANE = ("y", "x")
bfloat = jnp.bfloat16
single = jnp.float32


def turn(value, cosine, sine):
    half = value.shape[-1] // 2
    first_half = value[..., :half]
    second_half = value[..., half:]
    return jnp.concatenate(
        [first_half * cosine - second_half * sine, second_half * cosine + first_half * sine],
        axis=-1,
    )


def turn_back(grad, cosine, sine):
    half = grad.shape[-1] // 2
    first_half = grad[..., :half]
    second_half = grad[..., half:]
    return jnp.concatenate(
        [first_half * cosine + second_half * sine, second_half * cosine - first_half * sine],
        axis=-1,
    )


def rms_parts(value):
    factor = lax.rsqrt(jnp.mean(value * value, axis=-1, keepdims=True) + EPS)
    return (value * factor, factor)


def rms_back(grad, unit_val, factor, gain):
    scaled = grad * gain
    return factor * (scaled - unit_val * jnp.mean(unit_val * scaled, axis=-1, keepdims=True))


def swap(value, axis):
    return lax.ppermute(value, axis, [(0, 1), (1, 0)])


def swap_both(value):
    return lax.ppermute(value, ("zh", "zl"), [(0, 3), (1, 2), (2, 1), (3, 0)])


def line_sum(near, far, beside=None, needs=None):
    here = near + swap(far.astype(bfloat), "c").astype(single)
    if beside is not None:
        here, needs = lax.optimization_barrier((here, needs))
        made = beside(needs)
    sent = here.astype(bfloat)
    got = (swap(sent[64:128], "zl"), swap(sent[128:192], "zh"), swap_both(sent[192:256]))
    if beside is not None:
        got, made = lax.optimization_barrier((got, made))
    one, two, three = (piece.astype(single) for piece in got)
    total = (here[:64] + one) + (two + three)
    return total if beside is None else (total, made)


def shift(value, axis, step):
    return lax.ppermute(value, axis, [(i, (i + step) % 4) for i in range(4)])


def plane_sum(one, two, later=None):
    for axes in (("x", "y"), ("y", "x")):
        got = [[shift(v[step], axis, step) for step in range(1, 4)] for v, axis in zip((one, two), axes)]
        if later is not None and axes[0] == "x":
            got, later = lax.optimization_barrier((got, later))
        else:
            got = lax.optimization_barrier(got)
        one, two = (
            (v[0].astype(single) + parts[0].astype(single))
            + (parts[1].astype(single) + parts[2].astype(single))
            for v, parts in zip((one, two), got)
        )
        if axes[0] == "x":
            one, two = (
                [v[0]] + [v[step].astype(bfloat) for step in range(1, 4)] for v in (one, two)
            )
    return (one, two) if later is None else (one, two, later)


def line_gather(own):
    near = jnp.concatenate([own, swap(own, "zl"), swap(own, "zh"), swap_both(own)], axis=0)
    return jnp.concatenate([near, swap(near, "c")], axis=0)


def small_sum(value):
    value = value + swap(value, "c")
    return (value + swap(value, "zl")) + (swap(value, "zh") + swap_both(value))


def head_gather(own, mine):
    near = jnp.concatenate([own, swap(own, "zl")], axis=0)
    parts = jnp.concatenate([near, swap(near, "c")], axis=0).reshape(4, 64, -1)
    order = (0, 2, 1, 3)
    rows = []
    for place in range(4):
        other = place ^ mine
        slot = (other & 1) * 2 + (other >> 1)
        rows.append(lax.dynamic_index_in_dim(parts, slot, 0, keepdims=False))
    return jnp.concatenate(rows, axis=0).astype(single)


def row_place(index, zl, c):
    core = (index >> 7) & 1
    low = (index >> 6) & 1
    return ((low ^ zl) * 2 + (core ^ c)) * 64 + (index & 63)


def block_range(block, cut, ends):
    first = block * BLOCK
    last = first + BLOCK - 1
    low_least = jnp.where(first >= cut, cut, 0)
    low_most = jnp.where(last >= cut, cut, 0)
    high_least = jnp.minimum(first, jnp.where(first >= cut, ends[1], ends[0]))
    start = low_least // BLOCK
    whole = jnp.minimum((low_most + BLOCK - 1) // BLOCK, block + 1)
    whole_end = jnp.maximum((high_least + 1) // BLOCK, whole)
    return start, whole, whole_end, block + 1


def stacked(ref, half, low):
    near = half * 128
    return jnp.concatenate(
        [
            ref[near : near + 128, 0:HD],
            ref[256 + near : 384 + near, 0:HD],
            ref[near : near + 128, HD : 2 * HD],
            ref[256 + near : 384 + near, HD : 2 * HD],
        ],
        axis=0,
    )


def unstack(ref, half, value):
    near = half * 128
    ref[near : near + 128, 0:HD] = value[0:128]
    ref[256 + near : 384 + near, 0:HD] = value[128:256]
    ref[near : near + 128, HD : 2 * HD] = value[256:384]
    ref[256 + near : 384 + near, HD : 2 * HD] = value[384:512]


def key_rows(ref, plane, half, column):
    near = pl.multiple_of(half * 128, 128)
    far = pl.multiple_of(256 + half * 128, 128)
    columns = slice(column * HD, (column + 1) * HD)
    return jnp.concatenate(
        [ref[plane, pl.ds(near, 128), columns], ref[plane, pl.ds(far, 128), columns]], axis=0
    )


def find_slot(info, where, block):
    slot = where[block]
    return slot & 15, (slot >> 4) ^ info[4]


def dot_nt(left, right):
    return lax.dot_general(left, right, (((1,), (1,)), ((), ())), preferred_element_type=single)


def dot_tn(left, right):
    return lax.dot_general(left, right, (((0,), (0,)), ((), ())), preferred_element_type=single)


def find_blocks(home, where):
    for slot in range(32):
        where[home[slot]] = slot


def tile_limits(info, half):
    zl, c, cut = info[2], info[3], info[5]
    ends = (info[6] - 1, cut + info[7] - 1)
    block = info[half]
    place = block * BLOCK + row_place(lax.broadcasted_iota(jnp.int32, (1, 512), 1), zl, c)
    second = place >= cut
    low = jnp.where(second, cut, 0)
    high = jnp.minimum(place, jnp.where(second, ends[1], ends[0]))
    return low, high, block_range(block, cut, ends)


def over_blocks(limits, step):
    start, whole, whole_end, stop = limits
    lax.fori_loop(start, whole, lambda block, _: step(block, True), None)
    lax.fori_loop(whole, whole_end, lambda block, _: step(block, False), None)
    lax.fori_loop(whole_end, stop, lambda block, _: step(block, True), None)


def attend_kernel(info, home, query, pairs, out, logs, where, accum, total):
    find_blocks(home, where)
    key_place = row_place(lax.broadcasted_iota(jnp.int32, (256, 512), 0), info[2], info[3])
    for half in range(2):
        low, high, limits = tile_limits(info, half)
        rows = stacked(query, half, None)
        accum[...] = jnp.zeros_like(accum)
        total[...] = jnp.zeros_like(total)

        def step(block, masked):
            plane, side = find_slot(info, where, block)
            score = dot_nt(key_rows(pairs, plane, side, 0), rows)
            weight = jnp.exp2(score * (SCALE * LOG2E))
            if masked:
                place = key_place + block * BLOCK
                weight = jnp.where((place >= low) & (place <= high), weight, 0.0)
            total[...] += jnp.sum(weight, axis=0, keepdims=True)
            values = key_rows(pairs, plane, side, 1)
            accum[...] += dot_tn(values, weight.astype(bfloat))

        over_blocks(limits, step)
        logs[half] = jnp.log2(total[...])
        unstack(out, half, jnp.transpose(accum[...] / total[...]))


def attend_back_kernel(info, home, query, d_out, out, pairs, logs, *refs):
    d_query, d_keys, d_values = refs[0], refs[1:5], refs[5:9]
    where, key_sum, value_sum, d_rows = refs[9:]
    find_blocks(home, where)
    key_place = row_place(lax.broadcasted_iota(jnp.int32, (256, 512), 0), info[2], info[3])

    def clear(index, _):
        for accum in (key_sum, value_sum):
            accum[index] = jnp.zeros(accum.shape[1:], single)

    lax.fori_loop(0, 16, clear, None)
    for half in range(2):
        low, high, limits = tile_limits(info, half)
        rows = stacked(query, half, None)
        grads = stacked(d_out, half, None)
        delta = jnp.sum(
            jnp.transpose(grads.astype(single) * stacked(out, half, None)), axis=0, keepdims=True
        )
        log = logs[half]
        d_rows[...] = jnp.zeros_like(d_rows)

        def step(block, masked):
            plane, side = find_slot(info, where, block)
            keys = key_rows(pairs, plane, side, 0)
            values = key_rows(pairs, plane, side, 1)
            prob = jnp.exp2(dot_nt(keys, rows) * (SCALE * LOG2E) - log)
            if masked:
                place = key_place + block * BLOCK
                prob = jnp.where((place >= low) & (place <= high), prob, 0.0)
            d_score = (prob * (dot_nt(values, grads) - delta)).astype(bfloat)
            d_value = jnp.dot(prob.astype(bfloat), grads, preferred_element_type=single)
            d_key = jnp.dot(d_score, rows, preferred_element_type=single)
            d_rows[...] += dot_tn(keys, d_score)
            near = pl.multiple_of(side * 128, 128)
            far = pl.multiple_of(256 + side * 128, 128)
            down = ((plane >> 2) - info[8]) & 3
            across = (plane - info[9]) & 3
            for accum, slot, grad in (
                (key_sum, across * 4 + down, d_key),
                (value_sum, down * 4 + across, d_value),
            ):
                accum[slot, pl.ds(near, 128), :] += grad[0:128]
                accum[slot, pl.ds(far, 128), :] += grad[128:256]

        over_blocks(limits, step)
        unstack(d_query, half, jnp.transpose(d_rows[...]) * SCALE)
    for one in range(4):
        for two in range(4):
            d_keys[one][two] = (key_sum[one * 4 + two] * SCALE).astype(bfloat)
            d_values[one][two] = value_sum[one * 4 + two].astype(bfloat)


VMEM = pl.BlockSpec(memory_space=pltpu.VMEM)
SMEM = pl.BlockSpec(memory_space=pltpu.SMEM)


def attend(info, home, query, pairs):
    return pl.pallas_call(
        attend_kernel,
        out_shape=(
            jax.ShapeDtypeStruct((512, 2 * HD), single),
            jax.ShapeDtypeStruct((2, 1, 512), single),
        ),
        in_specs=[SMEM, SMEM, VMEM, VMEM],
        out_specs=(VMEM, VMEM),
        scratch_shapes=[
            pltpu.SMEM((32,), jnp.int32),
            pltpu.VMEM((HD, 512), single),
            pltpu.VMEM((1, 512), single),
        ],
        compiler_params=pltpu.CompilerParams(vmem_limit_bytes=32 * 2**20),
        cost_estimate=pl.CostEstimate(
            flops=4 * 2**30, bytes_accessed=6 * 2**20, transcendentals=4 * 2**20
        ),
        name="attend",
    )(info, home, query, pairs)


def attend_back(info, home, query, d_out, out, pairs, logs):
    outs = pl.pallas_call(
        attend_back_kernel,
        out_shape=[jax.ShapeDtypeStruct((512, 2 * HD), single)]
        + [jax.ShapeDtypeStruct((4, 512, HD), bfloat)] * 8,
        in_specs=[SMEM, SMEM, VMEM, VMEM, VMEM, VMEM, VMEM],
        out_specs=[VMEM] * 9,
        scratch_shapes=[
            pltpu.SMEM((32,), jnp.int32),
            pltpu.VMEM((16, 512, HD), single),
            pltpu.VMEM((16, 512, HD), single),
            pltpu.VMEM((HD, 512), single),
        ],
        compiler_params=pltpu.CompilerParams(vmem_limit_bytes=40 * 2**20),
        cost_estimate=pl.CostEstimate(
            flops=10 * 2**30, bytes_accessed=12 * 2**20, transcendentals=4 * 2**20
        ),
        name="attend_back",
    )(info, home, query, d_out, out, pairs, logs)
    return outs[0], outs[1:5], outs[5:9]


def plane_grads(lefts, rights, tile, info=None):
    starts = []
    count = 0
    for _, right in rights:
        starts.append(count)
        count += right.shape[1] // tile
    spans = list(zip(starts, starts[1:] + [count]))
    depth, height = lefts[0].shape
    flips = {}
    for (number, _), start in zip(rights, starts):
        flips.setdefault(number, start)
    half = count // 2

    def flip(info_ref, left, flipped):
        for group in range(8):
            side, y = group // 4, group % 4
            turned = jnp.transpose(left[:, group * 256 : group * 256 + 256])
            for x in range(4):
                rows = turned[x * 64 : x * 64 + 64]
                if info_ref is None:
                    first = ((y * 4 + x) * 2 + side) * 64
                    flipped[first : first + 64, :] = rows
                else:
                    slot = ((x - info_ref[9]) & 3) * 4 + ((y - info_ref[8]) & 3)
                    first = pl.multiple_of((slot * 2 + side) * 64, 64)
                    flipped[pl.ds(first, 64), :] = rows

    def kernel(*refs):
        info_ref = None
        if info is not None:
            info_ref, refs = refs[0], refs[1:]
        left_refs = refs[: len(lefts)]
        right_refs = refs[len(lefts) : len(lefts) + len(rights)]
        outs, flipped = refs[len(lefts) + len(rights) : -1], refs[-1]
        step = pl.program_id(0)
        for number, start in flips.items():

            @pl.when(step == start)
            def _():
                flip(info_ref, left_refs[number], flipped)

        def product(right, store):
            for one in range(4):
                rows = flipped[one * 512 : one * 512 + 512, :]
                part = jnp.dot(rows, right, preferred_element_type=single).astype(bfloat)
                store(one, part.reshape(4, 128, tile))

        def store_whole(one, part):
            outs[0][one * 4 : one * 4 + 4] = part

        def store_first(one, part):
            outs[one][...] = part

        def store_second(one, part):
            for two in range(4):
                outs[4 + two][one] = part[two]

        for ref, (start, stop) in zip(right_refs, spans):
            if info is None:
                stores = [(start, stop, store_whole)]
            else:
                stores = [
                    (start, min(stop, half), store_first),
                    (max(start, half), stop, store_second),
                ]
            for begin, end, store in stores:
                if begin < end:
                    pl.when((step >= begin) & (step < end))(
                        lambda ref=ref, store=store: product(ref[...], store)
                    )

    def right_spec(start, stop):
        return pl.BlockSpec(
            (depth, tile), lambda i: (0, jnp.minimum(jnp.maximum(i - start, 0), stop - start - 1))
        )

    in_specs = [pl.BlockSpec((depth, height), lambda i: (0, 0)) for _ in lefts]
    in_specs += [right_spec(*span) for span in spans]
    operands = list(lefts) + [right for _, right in rights]
    if info is None:
        out_specs = [pl.BlockSpec((16, 128, tile), lambda i: (0, 0, i))]
        out_shape = [jax.ShapeDtypeStruct((16, 128, count * tile), bfloat)]
    else:
        in_specs = [SMEM] + in_specs
        operands = [info] + operands
        first = pl.BlockSpec((4, 128, tile), lambda i: (0, 0, jnp.minimum(i, half - 1)))
        second = pl.BlockSpec((4, 128, tile), lambda i: (0, 0, jnp.maximum(i - half, 0)))
        out_specs = [first] * 4 + [second] * 4
        out_shape = [jax.ShapeDtypeStruct((4, 128, half * tile), bfloat)] * 8
    outs = pl.pallas_call(
        kernel,
        grid=(count,),
        in_specs=in_specs,
        out_specs=out_specs,
        out_shape=out_shape,
        scratch_shapes=[pltpu.VMEM((height, depth), bfloat)],
        compiler_params=pltpu.CompilerParams(
            vmem_limit_bytes=32 * 2**20, dimension_semantics=("arbitrary",)
        ),
        cost_estimate=pl.CostEstimate(
            flops=2 * depth * height * count * tile,
            bytes_accessed=2 * (depth + height) * count * tile + 2 * depth * height,
            transcendentals=0,
        ),
        name="plane_grads",
    )(*operands)
    return outs[0] if info is None else (outs[:4], outs[4:])


def columns_of(weight, side, width):
    return lax.dynamic_slice_in_dim(weight, side * width, width, 1)


def rows_of(weight, side, width):
    return lax.dynamic_slice_in_dim(weight, side * width, width, 0)


def in_order(zh, own, other, axis):
    first = jnp.where(zh == 0, own, other)
    second = jnp.where(zh == 0, other, own)
    return jnp.concatenate([first, second], axis=axis)


def gather_plane(block):
    whole = lax.all_gather(block, PLANE, axis=1, tiled=True)
    return whole.reshape(-1, block.shape[-1])


def per_device(
    tokens,
    query_weight,
    key_weight,
    value_weight,
    gate_weight,
    out_weight,
    norm_gain,
    query_gain,
    key_gain,
    inner_gate,
    inner_lift,
    inner_down,
    inner_gain,
    out_grad,
    bucket_len,
    seq_len,
    home_block,
):
    zh = lax.axis_index("zh")
    zl = lax.axis_index("zl")
    c = lax.axis_index("c")
    mine = zl * 2 + c
    width = tokens.shape[1]
    seq_index = zh * 16 + lax.axis_index("y") * 4 + lax.axis_index("x")
    block_own = lax.dynamic_index_in_dim(home_block, seq_index, 0, keepdims=False)
    block_other = lax.dynamic_index_in_dim(home_block, seq_index ^ 16, 0, keepdims=False)
    info = jnp.stack(
        [
            block_own,
            block_other,
            zl,
            c,
            zh,
            bucket_len[0],
            seq_len[0],
            seq_len[1],
            lax.axis_index("y"),
            lax.axis_index("x"),
        ]
    ).astype(jnp.int32)

    def column(vector):
        return jnp.pad(vector, (0, 64 - vector.shape[0]))[:, None]

    gain_columns = jnp.pad(
        jnp.concatenate(
            [column(norm_gain), column(inner_gain), column(query_gain), column(key_gain)], axis=1
        ),
        ((0, 0), (0, 124)),
    )

    def outer_pack(side):
        return jnp.concatenate(
            [
                columns_of(query_weight, side, 256),
                columns_of(key_weight, side, 128),
                columns_of(value_weight, side, 128),
                columns_of(gate_weight, side, 256),
                rows_of(out_weight, side, 256).T,
                gain_columns,
            ],
            axis=1,
        )

    def inner_pack(side):
        return jnp.concatenate(
            [
                columns_of(inner_gate, side, 768),
                columns_of(inner_lift, side, 768),
                rows_of(inner_down, side, 768).T,
            ],
            axis=1,
        )

    def pair_up(pack):
        own = pack(zh)
        other = swap(pack(1 - zh), "zh")
        return in_order(zh, own[None], other[None], 0)

    outer_block = pair_up(outer_pack)
    inner_block = pair_up(inner_pack)
    outer = gather_plane(outer_block)

    def line_rows(rows):
        other = swap(rows, "zh")
        pieces = []
        for core in range(2):
            for source in (rows, other):
                for low in range(2):
                    pieces.append(rows_of(source, mine ^ (low * 2 + core), 64))
        return jnp.concatenate(pieces, axis=0)

    rows_in = line_rows(tokens)
    out_grad, rows_in = lax.optimization_barrier((out_grad, rows_in))
    rows_grad = line_rows(out_grad)

    index = jnp.arange(512, dtype=jnp.int32)
    half_of = (index >> 7) & 1
    place = jnp.where(half_of == 0, block_own, block_other) * BLOCK + row_place(
        ((index >> 8) << 7) | (index & 127), zl, c
    )
    offset = jnp.where(place >= bucket_len[0], place - bucket_len[0], place)
    freq = jnp.power(THETA, -jnp.arange(HD // 2, dtype=single) * 2.0 / HD)
    angle = offset.astype(single)[:, None] * freq[None, :]
    cosine = jnp.cos(angle)[:, None, :]
    sine = jnp.sin(angle)[:, None, :]

    inputs = rows_in.astype(single)
    unit_in, factor_in = rms_parts(inputs)
    unit_in, rows_grad = lax.optimization_barrier((unit_in, rows_grad))
    gains = outer[:, 1024:1028].astype(single).T
    gain_norm = gains[0:1]
    gain_inner = gains[1:2]
    gain_query = gains[2].reshape(32, 64)[:, :4].reshape(HD)
    gain_key = gains[3].reshape(32, 64)[:, :4].reshape(HD)
    w_outer = outer[:, :768]
    w_out = outer[:, 768:1024]
    normed = (unit_in * gain_norm).astype(bfloat)
    pre = jnp.dot(normed, w_outer, preferred_element_type=single)
    q_unit, q_factor = rms_parts(pre[:, :256].reshape(512, 2, HD))
    k_unit, k_factor = rms_parts(pre[:, 256:384].reshape(512, 1, HD))
    gate_sig = jax.nn.sigmoid(pre[:, 512:768])
    query = turn(q_unit * gain_query, cosine, sine).astype(bfloat).reshape(512, 256)
    key_rot = turn(k_unit * gain_key, cosine, sine).astype(bfloat).reshape(512, HD)
    pairs = lax.all_gather(
        jnp.concatenate([key_rot, pre[:, 384:512].astype(bfloat)], axis=1), PLANE, axis=0
    )
    pairs, inner_sent = lax.optimization_barrier((pairs, inner_block))
    inner = gather_plane(inner_sent)
    w_gate_lift = inner[:, :1536]
    w_down = inner[:, 1536:]
    attended, logs = attend(info, home_block, query, pairs)
    gated = (attended * gate_sig).astype(bfloat)

    def line_product(left, right, *beside):
        return line_sum(dot_nt(left[:256], right), dot_nt(left[256:], right), *beside)

    mixed_in = inputs[:64] + line_product(gated, w_out)
    unit_two, factor_two = rms_parts(mixed_in)
    normed_two = line_gather((unit_two * gain_inner).astype(bfloat))
    d_hidden = jnp.dot(rows_grad, w_down, preferred_element_type=single)
    gate_lift = jnp.dot(normed_two, w_gate_lift, preferred_element_type=single)
    gate_val = gate_lift[:, :768]
    lift_val = gate_lift[:, 768:]
    gate_act = jax.nn.sigmoid(gate_val)
    hidden = (gate_val * gate_act * lift_val).astype(bfloat)
    d_gate = (d_hidden * lift_val * gate_act * (1.0 + gate_val * (1.0 - gate_act))).astype(bfloat)
    d_lift = (d_hidden * gate_val * gate_act).astype(bfloat)
    d_gate_lift = jnp.concatenate([d_gate, d_lift], axis=1)

    def inner_grads(needs):
        return plane_grads(
            [normed_two, rows_grad], [(0, needs[0]), (0, needs[1]), (1, needs[2])], 384
        )

    d_normed_two, grad_inner = line_product(
        d_gate_lift, w_gate_lift, inner_grads, (d_gate, d_lift, hidden)
    )

    def scatter_plane(grad):
        part = lax.psum_scatter(grad, PLANE, scatter_dimension=0, tiled=False)
        return part.reshape(2, 64, -1)

    inner_part = scatter_plane(grad_inner)
    result_rows = mixed_in + line_product(hidden, w_down)
    d_mixed = rows_grad[:64].astype(single) + rms_back(
        d_normed_two, unit_two, factor_two, gain_inner
    )
    d_attn = line_gather(d_mixed.astype(bfloat))
    d_gated = jnp.dot(d_attn, w_out, preferred_element_type=single)
    d_attended = (d_gated * gate_sig).astype(bfloat)
    d_gate_pre = (d_gated * attended * gate_sig * (1.0 - gate_sig)).astype(bfloat)
    d_query, d_keys, d_values = attend_back(
        info, home_block, query, d_attended, attended, pairs, logs
    )
    d_q_turned = turn_back(d_query.reshape(512, 2, HD), cosine, sine)
    query_gain_part = jnp.sum(d_q_turned * q_unit, axis=(0, 1))
    d_q_pre = rms_back(d_q_turned, q_unit, q_factor, gain_query).astype(bfloat).reshape(512, 256)
    grad_outer = plane_grads(
        [normed, d_attn], [(0, d_q_pre), (0, d_gate_pre), (1, gated)], 128, info
    )
    d_key, d_value, grad_outer = plane_sum(d_keys, d_values, grad_outer)
    d_k_turned = turn_back(d_key[:, None, :], cosine, sine)
    key_gain_part = jnp.sum(d_k_turned * k_unit, axis=(0, 1))
    d_k_pre = rms_back(d_k_turned, k_unit, k_factor, gain_key).astype(bfloat).reshape(512, HD)
    d_kv_pre = jnp.concatenate([d_k_pre, d_value.astype(bfloat)], axis=1)
    outer_part = plane_sum(*grad_outer)
    outer_part = jnp.concatenate(outer_part, axis=1).reshape(2, 64, -1)
    grad_pairs = plane_grads([normed], [(0, d_kv_pre)], 256)

    def by_plane(vector):
        return jnp.transpose(vector.reshape(2, 16, 4), (1, 0, 2)).reshape(16, 8)

    gain_rows = jnp.concatenate([by_plane(query_gain_part), by_plane(key_gain_part)], axis=1)
    gain_rows = jnp.pad(gain_rows.astype(bfloat)[:, None, :], ((0, 0), (0, 15), (0, 240)))
    pairs_sent = jnp.concatenate(
        [grad_pairs, gain_rows],
        axis=1,
    )
    pairs_got = lax.all_to_all(pairs_sent, PLANE, 0, 0, tiled=True)
    pairs_sum = jnp.sum(pairs_got.astype(single), axis=0)
    pair_part = pairs_sum[:128].reshape(2, 64, 256)
    gain_part = pairs_sum[128, :16].reshape(2, 2, 4)

    d_pre = jnp.concatenate([d_q_pre, d_kv_pre, d_gate_pre], axis=1)
    d_normed = line_product(d_pre, w_outer)
    token_rows = d_mixed + rms_back(d_normed, unit_in[:64], factor_in[:64], gain_norm)

    def both_sides(part):
        own = lax.dynamic_index_in_dim(part, zh, 0, keepdims=False).astype(single)
        sent = lax.dynamic_index_in_dim(part, 1 - zh, 0, keepdims=False)
        return own, swap(sent.astype(bfloat), "zh").astype(single)

    inner_own, inner_got = both_sides(inner_part)
    outer_own, outer_got = both_sides(outer_part)
    pair_own, pair_got = both_sides(pair_part)

    def shard(own, got, start, count):
        return in_order(zh, own[:, start : start + count], got[:, start : start + count], 1)

    shard_igate = shard(inner_own, inner_got, 0, 768)
    shard_ilift = shard(inner_own, inner_got, 768, 768)
    shard_idown = shard(inner_own, inner_got, 1536, 768).T
    shard_query = shard(outer_own, outer_got, 0, 256)
    shard_gate = shard(outer_own, outer_got, 256, 256)
    shard_out = shard(outer_own, outer_got, 512, 256).T
    shard_key = shard(pair_own, pair_got, 0, 128)
    shard_value = shard(pair_own, pair_got, 128, 128)

    def weighted(block, part):
        return jnp.sum(block.astype(single) * part.astype(single), axis=2)

    norm_part = (
        weighted(outer_block[:, :, :256], outer_part[:, :, :256])
        + weighted(outer_block[:, :, 256:512], pair_part)
        + weighted(outer_block[:, :, 512:768], outer_part[:, :, 256:512])
    ) / outer_block[:, :, 1024].astype(single)
    inner_gain_part = weighted(inner_block[:, :, :1536], inner_part[:, :, :1536]) / outer_block[
        :, :, 1025
    ].astype(single)
    gain_line = jnp.concatenate(
        [
            norm_part.reshape(HD),
            inner_gain_part.reshape(HD),
            gain_part.reshape(16),
            jnp.zeros((112,), single),
        ]
    ).reshape(3, HD)
    gain_line = small_sum(gain_line)
    gain_own = lax.dynamic_index_in_dim(gain_line[:2].reshape(2, 2, 64), zh, 1, keepdims=False)
    gain_sides = lax.dynamic_index_in_dim(
        gain_line[2, :16].reshape(2, 2, 4), zh, 1, keepdims=False
    )

    def rounded(rows):
        return lax.reduce_precision(rows, 8, 7).astype(bfloat)

    result = head_gather(rounded(result_rows), mine)
    tokens_grad = head_gather(rounded(token_rows), mine)
    return (
        result,
        tokens_grad,
        shard_query,
        shard_key,
        shard_value,
        shard_gate,
        shard_out,
        gain_own[0],
        gain_sides[0],
        gain_sides[1],
        shard_igate,
        shard_ilift,
        shard_idown,
        gain_own[1],
    )


def solution(mesh):
    fine = Mesh(mesh.devices.reshape(2, 4, 4, 2, 2), ("zh", "y", "x", "zl", "c"))
    seq = ("zh", "y", "x")
    head = ("zl", "c")
    in_specs = (
        P(seq, None),
        P(seq, head),
        P(seq, head),
        P(seq, head),
        P(seq, head),
        P(head, seq),
        P(seq),
        P(seq),
        P(seq),
        P(seq, head),
        P(seq, head),
        P(head, seq),
        P(seq),
        P(seq, None),
        P(),
        P(),
        P(),
    )
    out_specs = (
        P(seq, None),
        P(seq, None),
        P(seq, head),
        P(seq, head),
        P(seq, head),
        P(seq, head),
        P(head, seq),
        P(seq),
        P(seq),
        P(seq),
        P(seq, head),
        P(seq, head),
        P(head, seq),
        P(seq),
    )
    return jax.shard_map(
        per_device, mesh=fine, in_specs=in_specs, out_specs=out_specs, check_vma=False
    )
```

```python
import jax
import jax.numpy as jnp
from jax import lax
from jax.experimental import pallas as pl
from jax.experimental.pallas import tpu as pltpu
from jax.sharding import Mesh
from jax.sharding import PartitionSpec as P

HD = 128
BLOCK = 256
EPS = 1e-06
THETA = 1000000.0
LOG2E = 1.4426950408889634
SCALE = HD ** (-0.5)
PLANE = ("y", "x")
bfloat = jnp.bfloat16
single = jnp.float32


def rms_parts(value):
    factor = lax.rsqrt(jnp.mean(value * value, axis=-1, keepdims=True) + EPS)
    return (value * factor, factor)


def rms_back(grad, unit_val, factor, gain):
    scaled = grad * gain
    return factor * (scaled - unit_val * jnp.mean(unit_val * scaled, axis=-1, keepdims=True))


def swap(value, axis):
    return lax.ppermute(value, axis, [(0, 1), (1, 0)])


def swap_both(value):
    return lax.ppermute(value, ("zh", "zl"), [(0, 3), (1, 2), (2, 1), (3, 0)])


def line_sum(near, far):
    return line_sum_end(line_sum_middle(near, far))


def line_sum_middle(near, far):
    return near + swap(far.astype(bfloat), "c").astype(single)


def line_sum_end(here, beside=None):
    made = None
    if beside is not None:
        here, needs = lax.optimization_barrier((here, beside[1]))
        made = beside[0](needs)
    sent = here.astype(bfloat)
    got = (swap(sent[64:128], "zl"), swap(sent[128:192], "zh"), swap_both(sent[192:256]))
    if beside is not None:
        got, made = lax.optimization_barrier((got, made))
    one, two, three = (piece.astype(single) for piece in got)
    total = (here[:64] + one) + (two + three)
    return total if beside is None else (total, made)


def shift(value, axis, step):
    return lax.ppermute(value, axis, [(i, (i + step) % 4) for i in range(4)])


def plane_gather(one, two, later, ring):
    got = [
        [shift(value, axis, -step) for step in range(1, 4)]
        for value, axis in ((one, "x"), (two, "y"))
    ]
    got, later = lax.optimization_barrier((got, later))
    lines = [jnp.stack([v] + parts, axis=0) for v, parts in zip((one, two), got)]
    if not ring:
        pieces = [
            [line] + [shift(line, axis, -step) for step in range(1, 4)]
            for line, axis in zip(lines, ("y", "x"))
        ]
        return pieces, later
    next_to = [(shift(line, axis, -1), shift(line, axis, 1)) for line, axis in zip(lines, ("y", "x"))]
    next_to = lax.optimization_barrier(next_to)
    return [
        [line, up, shift(up[:2], axis, -1), shift(down[2:], axis, 1), down]
        for line, (up, down), axis in zip(lines, next_to, ("y", "x"))
    ], later


def plane_sum(one, two, beside):
    both = list(zip((one, two), ("x", "y")))
    across = [(shift(v[2], axis, 1), shift(v[3], axis, -1)) for v, axis in both]
    across, start = lax.optimization_barrier((across, beside[0]))
    got = []
    for (v, axis), (up, down) in zip(both, across):
        up = jnp.concatenate([(v[1][:2].astype(single) + up.astype(single)).astype(bfloat), v[1][2:]])
        down = jnp.concatenate(
            [v[4][:2], (v[4][2:].astype(single) + down.astype(single)).astype(bfloat)]
        )
        got.append((shift(up, axis, 1), shift(down, axis, -1)))
    got, first = lax.optimization_barrier((got, beside[1]))
    sums = [
        v[0].astype(single) + (up.astype(single) + down.astype(single))
        for (v, _), (up, down) in zip(both, got)
    ]
    got = [
        [shift(v[step].astype(bfloat), axis, step) for step in range(1, 4)]
        for v, axis in zip(sums, ("y", "x"))
    ]
    got, second = lax.optimization_barrier((got, beside[2]))
    sums = [
        (v[0] + parts[0].astype(single)) + (parts[1].astype(single) + parts[2].astype(single))
        for v, parts in zip(sums, got)
    ]
    return sums[0], sums[1], (start, first, second)


def line_gather(own):
    near = jnp.concatenate([own, swap(own, "zl"), swap(own, "zh"), swap_both(own)], axis=0)
    return jnp.concatenate([near, swap(near, "c")], axis=0)


def small_sum(value):
    value = value + swap(value, "c")
    return (value + swap(value, "zl")) + (swap(value, "zh") + swap_both(value))


def head_gather(own, mine):
    near = jnp.concatenate([own, swap(own, "zl")], axis=0)
    parts = jnp.concatenate([near, swap(near, "c")], axis=0).reshape(4, 64, -1)
    order = (0, 2, 1, 3)
    rows = []
    for place in range(4):
        other = place ^ mine
        slot = (other & 1) * 2 + (other >> 1)
        rows.append(lax.dynamic_index_in_dim(parts, slot, 0, keepdims=False))
    return jnp.concatenate(rows, axis=0).astype(single)


def row_place(index, zl, c):
    core = (index >> 7) & 1
    low = (index >> 6) & 1
    return ((low ^ zl) * 2 + (core ^ c)) * 64 + (index & 63)


def block_range(block, cut, ends):
    first = block * BLOCK
    last = first + BLOCK - 1
    low_least = jnp.where(first >= cut, cut, 0)
    low_most = jnp.where(last >= cut, cut, 0)
    high_least = jnp.minimum(first, jnp.where(first >= cut, ends[1], ends[0]))
    start = low_least // BLOCK
    whole = jnp.minimum((low_most + BLOCK - 1) // BLOCK, block + 1)
    whole_end = jnp.maximum((high_least + 1) // BLOCK, whole)
    return start, whole, whole_end, block + 1


def stacked(ref, half):
    near = half * 128
    return jnp.concatenate(
        [
            ref[near : near + 128, 0:HD],
            ref[256 + near : 384 + near, 0:HD],
            ref[near : near + 128, HD : 2 * HD],
            ref[256 + near : 384 + near, HD : 2 * HD],
        ],
        axis=0,
    )


def unstack(ref, half, value):
    near = half * 128
    ref[near : near + 128, 0:HD] = value[0:128]
    ref[256 + near : 384 + near, 0:HD] = value[128:256]
    ref[near : near + 128, HD : 2 * HD] = value[256:384]
    ref[256 + near : 384 + near, HD : 2 * HD] = value[384:512]


def key_rows(ref, one, two, half):
    near = pl.multiple_of(half * 128, 128)
    far = pl.multiple_of(256 + half * 128, 128)
    return jnp.concatenate(
        [ref[one, two, pl.ds(near, 128), :], ref[one, two, pl.ds(far, 128), :]], axis=0
    )


def find_slot(info, where, block):
    slot = where[block]
    down = ((slot >> 2) - info[8]) & 3
    across = (slot - info[9]) & 3
    return down, across, (slot >> 4) ^ info[4]


def fetch(pieces, buffers, sems):
    copies = []
    for buffer, parts in zip(buffers, (pieces[:5], pieces[5:])):
        targets = (
            buffer.at[0],
            buffer.at[1],
            buffer.at[2, pl.ds(0, 2)],
            buffer.at[2, pl.ds(2, 2)],
            buffer.at[3],
        )
        for part, target in zip(parts, targets):
            copies.append(pltpu.make_async_copy(part, target, sems.at[len(copies)]))
    for copy in copies:
        copy.start()
    for copy in copies:
        copy.wait()


def turned(value, cosine, sine):
    return value * cosine + pltpu.roll(value, HD // 2, 1) * sine


def unit_of(value):
    factor = lax.rsqrt(jnp.mean(value * value, axis=-1, keepdims=True) + EPS)
    return value * factor, factor


def dot_nt(left, right):
    return lax.dot_general(left, right, (((1,), (1,)), ((), ())), preferred_element_type=single)


def dot_tn(left, right):
    return lax.dot_general(left, right, (((0,), (0,)), ((), ())), preferred_element_type=single)


def find_blocks(home, where):
    for slot in range(32):
        where[home[slot]] = slot


def tile_limits(info, half):
    zl, c, cut = info[2], info[3], info[5]
    ends = (info[6] - 1, cut + info[7] - 1)
    block = info[half]
    place = block * BLOCK + row_place(lax.broadcasted_iota(jnp.int32, (1, 512), 1), zl, c)
    second = place >= cut
    low = jnp.where(second, cut, 0)
    high = jnp.minimum(place, jnp.where(second, ends[1], ends[0]))
    return low, high, block_range(block, cut, ends)


def over_blocks(limits, step):
    start, whole, whole_end, stop = limits
    lax.fori_loop(start, whole, lambda block, _: step(block, True), None)
    lax.fori_loop(whole, whole_end, lambda block, _: step(block, False), None)
    lax.fori_loop(whole_end, stop, lambda block, _: step(block, True), None)


def attend_kernel(info, home, query, *refs):
    pieces, (out, logs) = refs[:10], refs[10:12]
    keys, values, where, accum, total, sems = refs[12:]
    find_blocks(home, where)
    fetch(pieces, (keys, values), sems)
    key_place = row_place(lax.broadcasted_iota(jnp.int32, (256, 512), 0), info[2], info[3])
    for half in range(2):
        low, high, limits = tile_limits(info, half)
        rows = stacked(query, half)
        accum[...] = jnp.zeros_like(accum)
        total[...] = jnp.zeros_like(total)

        def step(block, masked):
            down, across, side = find_slot(info, where, block)
            score = dot_nt(key_rows(keys, down, across, side), rows)
            weight = jnp.exp2(score * (SCALE * LOG2E))
            if masked:
                place = key_place + block * BLOCK
                weight = jnp.where((place >= low) & (place <= high), weight, 0.0)
            total[...] += jnp.sum(weight, axis=0, keepdims=True)
            accum[...] += dot_tn(key_rows(values, across, down, side), weight.astype(bfloat))

        over_blocks(limits, step)
        logs[half] = jnp.log2(total[...])
        unstack(out, half, jnp.transpose(accum[...] / total[...]))


def attend_back_kernel(info, home, query, d_out, out, logs, pre, cosine, sine, gains, *refs):
    pieces, (d_pre, gain_grad) = refs[:10], refs[10:12]
    d_keys, d_values = refs[12:17], refs[17:22]
    keys, values, where, key_sum, value_sum, d_rows, d_query, sems = refs[22:]
    find_blocks(home, where)
    fetch(pieces, (keys, values), sems)
    key_place = row_place(lax.broadcasted_iota(jnp.int32, (256, 512), 0), info[2], info[3])

    def clear(index, _):
        for accum in (key_sum, value_sum):
            accum[index] = jnp.zeros(accum.shape[1:], single)

    lax.fori_loop(0, 16, clear, None)
    for half in range(2):
        low, high, limits = tile_limits(info, half)
        rows = stacked(query, half)
        grads = stacked(d_out, half)
        delta = jnp.sum(
            jnp.transpose(grads.astype(single) * stacked(out, half)), axis=0, keepdims=True
        )
        log = logs[half]
        d_rows[...] = jnp.zeros_like(d_rows)

        def step(block, masked):
            down, across, side = find_slot(info, where, block)
            key = key_rows(keys, down, across, side)
            prob = jnp.exp2(dot_nt(key, rows) * (SCALE * LOG2E) - log)
            if masked:
                place = key_place + block * BLOCK
                prob = jnp.where((place >= low) & (place <= high), prob, 0.0)
            d_prob = dot_nt(key_rows(values, across, down, side), grads)
            d_score = (prob * (d_prob - delta)).astype(bfloat)
            d_value = jnp.dot(prob.astype(bfloat), grads, preferred_element_type=single)
            d_key = jnp.dot(d_score, rows, preferred_element_type=single)
            d_rows[...] += dot_tn(key, d_score)
            near = pl.multiple_of(side * 128, 128)
            far = pl.multiple_of(256 + side * 128, 128)
            for accum, slot, grad in (
                (key_sum, across * 4 + down, d_key),
                (value_sum, down * 4 + across, d_value),
            ):
                accum[slot, pl.ds(near, 128), :] += grad[0:128]
                accum[slot, pl.ds(far, 128), :] += grad[128:256]

        over_blocks(limits, step)
        unstack(d_query, half, jnp.transpose(d_rows[...]) * SCALE)
    for one in range(4):
        for two in range(4):
            number, place = (one, two) if one < 2 else (4, two) if one == 3 else (2 + two // 2, two % 2)
            d_keys[number][place] = (key_sum[one * 4 + two] * SCALE).astype(bfloat)
            d_values[number][place] = value_sum[one * 4 + two].astype(bfloat)
    gain = gains[0:1]
    total = jnp.zeros((1, HD), single)
    for head in range(2):
        columns = slice(head * HD, (head + 1) * HD)
        d_turned = turned(d_query[:, columns], cosine[...], -sine[...])
        unit, factor = unit_of(pre[:, columns])
        total += jnp.sum(d_turned * unit, axis=0, keepdims=True)
        d_pre[:, columns] = rms_back(d_turned, unit, factor, gain).astype(bfloat)
    gain_grad[...] = total


def line_order(info):
    for core in range(2):
        for source in range(2):
            for low in range(2):
                there = ((low ^ info[2]) * 2 + (core ^ info[3])) * 64
                yield core * 4 + source * 2 + low, source, pl.multiple_of(there, 64)


def arrange_kernel(info, own, other, out):
    for place, source, there in line_order(info):
        out[place * 64 : place * 64 + 64, :] = (own, other)[source][pl.ds(there, 64), :]


def project_pairs_kernel(info, own, other, cosine, sine, *refs):
    normed, key, value, pre, weights, gains, small, extra, came, sems = refs[8:]
    copies = [
        pltpu.make_async_copy(piece, came.at[i], sems.at[i]) for i, piece in enumerate(refs[:8])
    ]
    for copy in copies:
        copy.start()
    for copy in copies:
        copy.wait()
    for one in range(4):
        for two in range(4):
            for number, y, x, column in ((one, one, two, 0), (4 + one, two, one, HD)):
                plane = ((y + info[8]) & 3) * 4 + ((x + info[9]) & 3)
                for side in range(2):
                    to = pl.ds(pl.multiple_of(side * 1024 + plane * 64, 64), 64)
                    block = came[number, two, side * 64 : side * 64 + 64, :]
                    weights[to, column : column + HD] = block[:, :HD]
                    extra[to, column : column + HD] = block[:, HD:]
    gains[...] = jnp.transpose(extra[:, 0:HD].astype(single))[0:8]
    total = jnp.zeros((16, HD), single)
    for block in range(32):
        total += extra[block * 64 : block * 64 + 16, HD : 2 * HD].astype(single)
    small[...] = total[0:8]
    gain = gains[0:1]
    for place, source, there in line_order(info):
        unit, _ = unit_of((own, other)[source][pl.ds(there, 64), :].astype(single))
        normed[place * 64 : place * 64 + 64, :] = (unit * gain).astype(bfloat)
    both = jnp.dot(normed[...], weights[...], preferred_element_type=single)
    pre[...] = both[:, :HD]
    unit, _ = unit_of(both[:, :HD])
    key[...] = turned(unit * small[1:2], cosine[...], sine[...]).astype(bfloat)
    value[...] = both[:, HD:].astype(bfloat)


def project_query_kernel(normed, weights, cosine, sine, gains, query, pre, gate_act):
    both = jnp.dot(normed[...], weights[:, 0 : 4 * HD], preferred_element_type=single)
    for head in range(2):
        columns = slice(head * HD, (head + 1) * HD)
        pre[:, columns] = both[:, columns]
        unit, _ = unit_of(both[:, columns])
        query[:, columns] = turned(unit * gains[0:1], cosine[...], sine[...]).astype(bfloat)
    gate_act[...] = jax.nn.sigmoid(both[:, 2 * HD : 4 * HD])


VMEM = pl.BlockSpec(memory_space=pltpu.VMEM)
SMEM = pl.BlockSpec(memory_space=pltpu.SMEM)
ANY = pl.BlockSpec(memory_space=pl.ANY)


def shaped(dtype, *shape):
    return jax.ShapeDtypeStruct(shape, dtype)


def arrange(info, own, other):
    return pl.pallas_call(
        arrange_kernel,
        out_shape=shaped(own.dtype, 512, own.shape[1]),
        in_specs=[SMEM, VMEM, VMEM],
        out_specs=VMEM,
        cost_estimate=pl.CostEstimate(flops=0, bytes_accessed=4 * 2**20, transcendentals=0),
        name="arrange",
    )(info, own, other)


def project_pairs(info, own, other, cosine, sine, pieces):
    width = own.shape[1]
    return pl.pallas_call(
        project_pairs_kernel,
        out_shape=(
            shaped(bfloat, 512, width),
            shaped(bfloat, 512, HD),
            shaped(bfloat, 512, HD),
            shaped(single, 512, HD),
            shaped(bfloat, width, 2 * HD),
            shaped(single, 8, width),
            shaped(single, 8, HD),
        ),
        in_specs=[SMEM] + [VMEM] * 4 + [ANY] * 8,
        out_specs=[VMEM] * 7,
        scratch_shapes=[
            pltpu.VMEM((width, 2 * HD), bfloat),
            pltpu.VMEM((8, 4, HD, 2 * HD), bfloat),
            pltpu.SemaphoreType.DMA((8,)),
        ],
        compiler_params=pltpu.CompilerParams(vmem_limit_bytes=32 * 2**20),
        cost_estimate=pl.CostEstimate(
            flops=2**30, bytes_accessed=8 * 2**20, transcendentals=2**10
        ),
        name="project_pairs",
    )(info, own, other, cosine, sine, *pieces[0], *pieces[1])


def project_query(normed, weights, cosine, sine, gains):
    return pl.pallas_call(
        project_query_kernel,
        out_shape=(
            shaped(bfloat, 512, 2 * HD),
            shaped(single, 512, 2 * HD),
            shaped(single, 512, 2 * HD),
        ),
        in_specs=[VMEM] * 5,
        out_specs=[VMEM] * 3,
        compiler_params=pltpu.CompilerParams(vmem_limit_bytes=32 * 2**20),
        cost_estimate=pl.CostEstimate(
            flops=2**30, bytes_accessed=8 * 2**20, transcendentals=2**17
        ),
        name="project_query",
    )(normed, weights, cosine, sine, gains)


def attend(info, home, query, pieces):
    return pl.pallas_call(
        attend_kernel,
        out_shape=(shaped(single, 512, 2 * HD), shaped(single, 2, 1, 512)),
        in_specs=[SMEM, SMEM, VMEM] + [ANY] * 10,
        out_specs=(VMEM, VMEM),
        scratch_shapes=[
            pltpu.VMEM((4, 4, 512, HD), bfloat),
            pltpu.VMEM((4, 4, 512, HD), bfloat),
            pltpu.SMEM((32,), jnp.int32),
            pltpu.VMEM((HD, 512), single),
            pltpu.VMEM((1, 512), single),
            pltpu.SemaphoreType.DMA((10,)),
        ],
        compiler_params=pltpu.CompilerParams(vmem_limit_bytes=32 * 2**20),
        cost_estimate=pl.CostEstimate(
            flops=4 * 2**30, bytes_accessed=6 * 2**20, transcendentals=4 * 2**20
        ),
        name="attend",
    )(info, home, query, *pieces[0], *pieces[1])


def attend_back(info, home, query, d_out, out, logs, pre, cosine, sine, gains, pieces):
    outs = pl.pallas_call(
        attend_back_kernel,
        out_shape=[shaped(bfloat, 512, 2 * HD), shaped(single, 1, HD)]
        + [pltpu.HBM((count, 512, HD), bfloat) for count in (4, 4, 2, 2, 4)] * 2,
        in_specs=[SMEM, SMEM] + [VMEM] * 8 + [ANY] * 10,
        out_specs=[VMEM] * 12,
        scratch_shapes=[
            pltpu.VMEM((4, 4, 512, HD), bfloat),
            pltpu.VMEM((4, 4, 512, HD), bfloat),
            pltpu.SMEM((32,), jnp.int32),
            pltpu.VMEM((16, 512, HD), single),
            pltpu.VMEM((16, 512, HD), single),
            pltpu.VMEM((HD, 512), single),
            pltpu.VMEM((512, 2 * HD), single),
            pltpu.SemaphoreType.DMA((10,)),
        ],
        compiler_params=pltpu.CompilerParams(vmem_limit_bytes=44 * 2**20),
        cost_estimate=pl.CostEstimate(
            flops=10 * 2**30, bytes_accessed=12 * 2**20, transcendentals=4 * 2**20
        ),
        name="attend_back",
    )(info, home, query, d_out, out, logs, pre, cosine, sine, gains, *pieces[0], *pieces[1])
    return outs[0], outs[1], outs[2:7], outs[7:12]


def plane_grads(lefts, rights, tile, rows=128, columns=None, into=None, extras=()):
    starts = []
    count = 0
    for _, right in rights:
        starts.append(count)
        count += right.shape[1] // tile
    spans = list(zip(starts, starts[1:] + [count]))
    depth, height = lefts[0].shape
    columns = columns or count * tile
    shift_by = 0 if into is None else columns // tile - count
    flips = {}
    for (number, _), start in zip(rights, starts):
        flips.setdefault(number, start)

    def kernel(*refs):
        left_refs, right_refs = refs[: len(lefts)], refs[len(lefts) : len(lefts) + len(rights)]
        extra_refs = refs[len(lefts) + len(rights) : len(lefts) + len(rights) + len(extras)]
        out, flipped = refs[-2:]
        step = pl.program_id(0)

        def flip(left):
            for group in range(8):
                side, y = group // 4, group % 4
                turned = jnp.transpose(left[:, group * 256 : group * 256 + 256])
                for x in range(4):
                    first = ((y * 4 + x) * 2 + side) * 64
                    flipped[first : first + 64, :] = turned[x * 64 : x * 64 + 64]

        def product(right):
            for one in range(4):
                left = flipped[one * 512 : one * 512 + 512, :]
                part = jnp.dot(left, right, preferred_element_type=single).astype(bfloat)
                out[one * 4 : one * 4 + 4, 0:128] = part.reshape(4, 128, tile)
            for number, ref in enumerate(extra_refs):
                out[:, 128:144, number * HD : (number + 1) * HD] = jnp.broadcast_to(
                    ref[...].astype(bfloat)[None], (16, 16, HD)
                )

        for number, start in flips.items():
            pl.when(step == start)(lambda number=number: flip(left_refs[number]))
        for ref, (start, stop) in zip(right_refs, spans):
            pl.when((step >= start) & (step < stop))(lambda ref=ref: product(ref[...]))

    def right_spec(start, stop):
        return pl.BlockSpec(
            (depth, tile), lambda i: (0, jnp.minimum(jnp.maximum(i - start, 0), stop - start - 1))
        )

    return pl.pallas_call(
        kernel,
        grid=(count,),
        in_specs=[pl.BlockSpec((depth, height), lambda i: (0, 0)) for _ in lefts]
        + [right_spec(*span) for span in spans]
        + [pl.BlockSpec((1, HD), lambda i: (0, 0)) for _ in extras]
        + ([] if into is None else [ANY]),
        out_specs=pl.BlockSpec((16, rows, tile), lambda i: (0, 0, i + shift_by)),
        out_shape=pltpu.HBM((16, rows, columns), bfloat),
        input_output_aliases={} if into is None else {len(lefts) + len(rights) + len(extras): 0},
        scratch_shapes=[pltpu.VMEM((height, depth), bfloat)],
        compiler_params=pltpu.CompilerParams(
            vmem_limit_bytes=32 * 2**20, dimension_semantics=("arbitrary",)
        ),
        cost_estimate=pl.CostEstimate(
            flops=2 * depth * height * count * tile,
            bytes_accessed=2 * (depth + height) * count * tile + 2 * depth * height,
            transcendentals=0,
        ),
        name="plane_grads",
    )(*lefts, *(right for _, right in rights), *extras, *([] if into is None else [into]))


def columns_of(weight, side, width):
    return lax.dynamic_slice_in_dim(weight, side * width, width, 1)


def rows_of(weight, side, width):
    return lax.dynamic_slice_in_dim(weight, side * width, width, 0)


def in_order(zh, own, other, axis):
    first = jnp.where(zh == 0, own, other)
    second = jnp.where(zh == 0, other, own)
    return jnp.concatenate([first, second], axis=axis)


def gather_plane(block):
    whole = lax.all_gather(block, PLANE, axis=1, tiled=True)
    return whole.reshape(-1, block.shape[-1])


def per_device(
    tokens,
    query_weight,
    key_weight,
    value_weight,
    gate_weight,
    out_weight,
    norm_gain,
    query_gain,
    key_gain,
    inner_gate,
    inner_lift,
    inner_down,
    inner_gain,
    out_grad,
    bucket_len,
    seq_len,
    home_block,
):
    zh = lax.axis_index("zh")
    zl = lax.axis_index("zl")
    c = lax.axis_index("c")
    mine = zl * 2 + c
    width = tokens.shape[1]
    seq_index = zh * 16 + lax.axis_index("y") * 4 + lax.axis_index("x")
    block_own = lax.dynamic_index_in_dim(home_block, seq_index, 0, keepdims=False)
    block_other = lax.dynamic_index_in_dim(home_block, seq_index ^ 16, 0, keepdims=False)
    info = jnp.stack(
        [
            block_own,
            block_other,
            zl,
            c,
            zh,
            bucket_len[0],
            seq_len[0],
            seq_len[1],
            lax.axis_index("y"),
            lax.axis_index("x"),
        ]
    ).astype(jnp.int32)

    lane = jnp.arange(HD, dtype=jnp.int32)

    def head_gain(vector):
        return jnp.where(lane // 4 == seq_index, jnp.tile(vector, 32), 0)

    norm_columns = jnp.pad(jnp.stack([norm_gain, inner_gain], axis=1), ((0, 0), (0, HD - 2)))
    head_rows = jnp.pad(
        jnp.stack([head_gain(query_gain), head_gain(key_gain)], axis=0), ((0, 62), (0, 0))
    ).astype(bfloat)

    def pairs_pack(side):
        return jnp.concatenate(
            [
                columns_of(key_weight, side, HD),
                norm_columns,
                columns_of(value_weight, side, HD),
                head_rows,
            ],
            axis=1,
        )

    def outer_pack(side):
        return jnp.concatenate(
            [
                columns_of(query_weight, side, 256),
                columns_of(gate_weight, side, 256),
                rows_of(out_weight, side, 256).T,
            ],
            axis=1,
        )

    def inner_pack(side):
        gate, lift, down = inner_shards
        return jnp.concatenate(
            [columns_of(gate, side, 768), columns_of(lift, side, 768), rows_of(down, side, 768).T],
            axis=1,
        )

    def pair_up(pack):
        own = pack(zh)
        other = swap(pack(1 - zh), "zh")
        return in_order(zh, own[None], other[None], 0)

    first_block = pair_up(
        lambda side: jnp.concatenate([pairs_pack(side), outer_pack(side)], axis=1)
    )
    index = jnp.arange(512, dtype=jnp.int32)
    half_of = (index >> 7) & 1
    place = jnp.where(half_of == 0, block_own, block_other) * BLOCK + row_place(
        ((index >> 8) << 7) | (index & 127), zl, c
    )
    offset = jnp.where(place >= bucket_len[0], place - bucket_len[0], place)
    freq = jnp.power(THETA, -jnp.arange(HD // 2, dtype=single) * 2.0 / HD)
    angle = offset.astype(single)[:, None] * freq[None, :]
    cosine = jnp.cos(angle)
    sine = jnp.sin(angle)
    cosine = jnp.concatenate([cosine, cosine], axis=1)
    sine = jnp.concatenate([-sine, sine], axis=1)

    first_block, cosine, sine, info, tokens_other = lax.optimization_barrier(
        (first_block, cosine, sine, info, swap(tokens, "zh"))
    )
    pairs_block, outer_block = first_block[:, :, : 4 * HD], first_block[:, :, 4 * HD :]
    outer = gather_plane(outer_block)
    pairs_wide = pairs_block.reshape(HD, 4 * HD)
    weight_pieces, _ = plane_gather(pairs_wide[:, : 2 * HD], pairs_wide[:, 2 * HD :], (), False)
    normed, key_rot, value, k_pre, w_pairs, gains, head_gains = project_pairs(
        info, tokens, tokens_other, cosine, sine, weight_pieces
    )
    key_rot, inner_shards = lax.optimization_barrier(
        (key_rot, (inner_gate, inner_lift, inner_down))
    )
    inner_block = pair_up(inner_pack)
    gain_norm, gain_inner = gains[0:1], gains[1:2]
    gain_query, gain_key = head_gains[0:1], head_gains[1:2]
    w_heads = outer[:, :512]
    w_out = outer[:, 512:]
    query, q_pre, gate_sig = project_query(normed, outer, cosine, sine, head_gains)
    pieces, (inner_block, out_grad_sent) = plane_gather(
        key_rot, value, (inner_block, out_grad), True
    )
    rows_grad = arrange(info, out_grad, swap(out_grad_sent, "zh"))
    inner = gather_plane(inner_block)
    w_gate_lift = inner[:, :1536]
    w_down = inner[:, 1536:]
    query, rows_grad = lax.optimization_barrier((query, rows_grad))
    attended, logs = attend(info, home_block, query, pieces)
    gated = (attended * gate_sig).astype(bfloat)

    def line_product(left, right):
        return line_sum(dot_nt(left[:256], right), dot_nt(left[256:], right))

    inputs = rows_of(tokens, mine, 64).astype(single)
    mixed_in = inputs + line_product(gated, w_out)
    unit_two, factor_two = rms_parts(mixed_in)
    normed_two = line_gather((unit_two * gain_inner).astype(bfloat))
    d_hidden = jnp.dot(rows_grad, w_down, preferred_element_type=single)
    gate_lift = jnp.dot(normed_two, w_gate_lift, preferred_element_type=single)
    gate_val = gate_lift[:, :768]
    lift_val = gate_lift[:, 768:]
    gate_act = jax.nn.sigmoid(gate_val)
    hidden = (gate_val * gate_act * lift_val).astype(bfloat)
    d_gate = (d_hidden * lift_val * gate_act * (1.0 + gate_val * (1.0 - gate_act))).astype(bfloat)
    d_lift = (d_hidden * gate_val * gate_act).astype(bfloat)
    d_gate_lift = jnp.concatenate([d_gate, d_lift], axis=1)

    def inner_grads(needs):
        return plane_grads(
            [normed_two, rows_grad],
            [(0, needs[0]), (0, needs[1]), (1, needs[2])],
            384,
            columns=3072,
        )

    d_normed_two, grad_inner = line_sum_end(
        line_sum_middle(dot_nt(d_gate_lift[:256], w_gate_lift), dot_nt(d_gate_lift[256:], w_gate_lift)),
        (inner_grads, (d_gate, d_lift, hidden)),
    )

    def scatter_plane(grad):
        part = lax.psum_scatter(grad, PLANE, scatter_dimension=0, tiled=False)
        return part.reshape(2, 64, -1)

    d_mixed = rows_grad[:64].astype(single) + rms_back(
        d_normed_two, unit_two, factor_two, gain_inner
    )
    d_attn = line_gather(d_mixed.astype(bfloat))
    d_gated = jnp.dot(d_attn, w_out, preferred_element_type=single)
    d_attended = (d_gated * gate_sig).astype(bfloat)
    d_gate_pre = (d_gated * attended * gate_sig * (1.0 - gate_sig)).astype(bfloat)
    d_q_pre, query_gain_part, d_keys, d_values = attend_back(
        info,
        home_block,
        query,
        d_attended,
        attended,
        logs,
        q_pre,
        cosine,
        sine,
        head_gains,
        pieces,
    )
    grads = plane_grads(
        [normed, d_attn],
        [(0, d_q_pre), (0, d_gate_pre), (1, gated)],
        256,
        columns=3072,
        into=grad_inner,
    )
    d_heads = jnp.concatenate([d_q_pre, d_gate_pre], axis=1)
    result_here = line_sum_middle(dot_nt(hidden[:256], w_down), dot_nt(hidden[256:], w_down))
    d_key, d_value, (grads, result_here, (normed_near, normed_far)) = plane_sum(
        d_keys,
        d_values,
        (grads, result_here, (dot_nt(d_heads[:256], w_heads), dot_nt(d_heads[256:], w_heads))),
    )
    part = scatter_plane(grads)
    k_unit, k_factor = rms_parts(k_pre)
    d_k_turned = d_key * cosine - jnp.roll(d_key, HD // 2, axis=1) * sine
    key_gain_part = jnp.sum(d_k_turned * k_unit, axis=0, keepdims=True)
    d_k_pre = rms_back(d_k_turned, k_unit, k_factor, gain_key).astype(bfloat)
    d_kv_pre = jnp.concatenate([d_k_pre, d_value.astype(bfloat)], axis=1)
    normed_far = (normed_far + dot_nt(d_kv_pre[256:], w_pairs)).astype(bfloat)
    normed_far, d_kv_pre = lax.optimization_barrier((normed_far, d_kv_pre))
    pairs_sent = plane_grads(
        [normed], [(0, d_kv_pre)], 256, rows=144, extras=(query_gain_part, key_gain_part)
    )
    pairs_sent, d_kv_pre = lax.optimization_barrier((pairs_sent, d_kv_pre))
    normed_near = normed_near + dot_nt(d_kv_pre[:256], w_pairs)
    normed_near, result_here = lax.optimization_barrier((normed_near, result_here))
    pairs_got = lax.all_to_all(pairs_sent, PLANE, 0, 0, tiled=True)
    pairs_sum = jnp.sum(pairs_got.astype(single), axis=0)
    pair_part = pairs_sum[:128].reshape(2, 64, 256)
    gain_part = pairs_sum[128]

    d_normed = line_sum(normed_near, normed_far)
    unit_in, factor_in = rms_parts(inputs)
    token_rows = d_mixed + rms_back(d_normed, unit_in, factor_in, gain_norm)
    result_rows = mixed_in + line_sum_end(result_here)

    def both_sides(part):
        own = lax.dynamic_index_in_dim(part, zh, 0, keepdims=False).astype(single)
        sent = lax.dynamic_index_in_dim(part, 1 - zh, 0, keepdims=False).astype(bfloat)
        sent, part = lax.optimization_barrier((sent, part))
        return own, swap(sent, "zh").astype(single), part

    pair_own, pair_got, pair_part = both_sides(pair_part)
    part_own, part_got, part = both_sides(part)

    def shard(own, got, start, count):
        return in_order(zh, own[:, start : start + count], got[:, start : start + count], 1)

    shard_igate = shard(part_own, part_got, 0, 768)
    shard_ilift = shard(part_own, part_got, 768, 768)
    shard_idown = shard(part_own, part_got, 1536, 768).T
    shard_query = shard(part_own, part_got, 2304, 256)
    shard_gate = shard(part_own, part_got, 2560, 256)
    shard_out = shard(part_own, part_got, 2816, 256).T
    shard_key = shard(pair_own, pair_got, 0, 128)
    shard_value = shard(pair_own, pair_got, 128, 128)

    def weighted(block, part):
        return jnp.sum(block.astype(single) * part.astype(single), axis=2)

    norm_part = (
        weighted(outer_block[:, :, :512], part[:, :, 2304:2816])
        + weighted(pairs_block[:, :, :HD], pair_part[:, :, :HD])
        + weighted(pairs_block[:, :, 2 * HD : 3 * HD], pair_part[:, :, HD:])
    ) / pairs_block[:, :, HD].astype(single)
    inner_gain_part = weighted(inner_block[:, :, :1536], part[:, :, :1536]) / pairs_block[
        :, :, HD + 1
    ].astype(single)
    gain_line = jnp.concatenate(
        [
            norm_part.reshape(HD),
            inner_gain_part.reshape(HD),
            gain_part,
        ]
    ).reshape(4, HD)
    gain_line = small_sum(gain_line)
    gain_own = lax.dynamic_index_in_dim(gain_line[:2].reshape(2, 2, 64), zh, 1, keepdims=False)
    gain_sides = lax.dynamic_slice_in_dim(gain_line[2:], seq_index * 4, 4, 1)

    def rounded(rows):
        return lax.reduce_precision(rows, 8, 7).astype(bfloat)

    result = head_gather(rounded(result_rows), mine)
    tokens_grad = head_gather(rounded(token_rows), mine)
    return (
        result,
        tokens_grad,
        shard_query,
        shard_key,
        shard_value,
        shard_gate,
        shard_out,
        gain_own[0],
        gain_sides[0],
        gain_sides[1],
        shard_igate,
        shard_ilift,
        shard_idown,
        gain_own[1],
    )


def solution(mesh):
    fine = Mesh(mesh.devices.reshape(2, 4, 4, 2, 2), ("zh", "y", "x", "zl", "c"))
    seq = ("zh", "y", "x")
    head = ("zl", "c")
    in_specs = (
        P(seq, None),
        P(seq, head),
        P(seq, head),
        P(seq, head),
        P(seq, head),
        P(head, seq),
        P(seq),
        P(seq),
        P(seq),
        P(seq, head),
        P(seq, head),
        P(head, seq),
        P(seq),
        P(seq, None),
        P(),
        P(),
        P(),
    )
    out_specs = (
        P(seq, None),
        P(seq, None),
        P(seq, head),
        P(seq, head),
        P(seq, head),
        P(seq, head),
        P(head, seq),
        P(seq),
        P(seq),
        P(seq),
        P(seq, head),
        P(seq, head),
        P(head, seq),
        P(seq),
    )
    return jax.shard_map(
        per_device, mesh=fine, in_specs=in_specs, out_specs=out_specs, check_vma=False
    )
```

```python
import jax
import jax.numpy as jnp
from jax import lax
from jax.experimental import pallas as pl
from jax.experimental.pallas import tpu as pltpu
from jax.sharding import Mesh
from jax.sharding import PartitionSpec as P

HD = 128
BLOCK = 256
EPS = 1e-06
THETA = 1000000.0
LOG2E = 1.4426950408889634
SCALE = HD ** (-0.5)
PLANE = ("y", "x")
bfloat = jnp.bfloat16
single = jnp.float32


def rms_parts(value):
    factor = lax.rsqrt(jnp.mean(value * value, axis=-1, keepdims=True) + EPS)
    return (value * factor, factor)


def rms_back(grad, unit_val, factor, gain):
    scaled = grad * gain
    return factor * (scaled - unit_val * jnp.mean(unit_val * scaled, axis=-1, keepdims=True))


def swap(value, axis):
    return lax.ppermute(value, axis, [(0, 1), (1, 0)])


def swap_both(value):
    return lax.ppermute(value, ("zh", "zl"), [(0, 3), (1, 2), (2, 1), (3, 0)])


def line_sum(near, far):
    return line_sum_end(line_sum_middle(near, far))


def line_sum_middle(near, far):
    return near + swap(far.astype(bfloat), "c").astype(single)


def line_sum_end(here, beside=None):
    made = None
    if beside is not None:
        here, needs = lax.optimization_barrier((here, beside[1]))
        made = beside[0](needs)
    sent = here.astype(bfloat)
    got = (swap(sent[64:128], "zl"), swap(sent[128:192], "zh"), swap_both(sent[192:256]))
    if beside is not None:
        got, made = lax.optimization_barrier((got, made))
    one, two, three = (piece.astype(single) for piece in got)
    total = (here[:64] + one) + (two + three)
    return total if beside is None else (total, made)


def shift(value, axis, step):
    return lax.ppermute(value, axis, [(i, (i + step) % 4) for i in range(4)])


def plane_gather(one, two, later, ring):
    got = [
        [shift(value, axis, -step) for step in range(1, 4)]
        for value, axis in ((one, "x"), (two, "y"))
    ]
    got, later = lax.optimization_barrier((got, later))
    lines = [jnp.stack([v] + parts, axis=0) for v, parts in zip((one, two), got)]
    if not ring:
        pieces = [
            [line] + [shift(line, axis, -step) for step in range(1, 4)]
            for line, axis in zip(lines, ("y", "x"))
        ]
        return pieces, later
    next_to = [(shift(line, axis, -1), shift(line, axis, 1)) for line, axis in zip(lines, ("y", "x"))]
    next_to = lax.optimization_barrier(next_to)
    return [
        [line, up, shift(up[:2], axis, -1), shift(down[2:], axis, 1), down]
        for line, (up, down), axis in zip(lines, next_to, ("y", "x"))
    ], later


def add_halves(groups):
    def kernel(*refs):
        for number in range(len(groups)):
            one, up, four, down = refs[4 * number : 4 * number + 4]
            first, second = refs[4 * len(groups) + 2 * number : 4 * len(groups) + 2 * number + 2]
            first[0:2] = (one[0:2].astype(single) + up[...].astype(single)).astype(bfloat)
            first[2:4] = one[2:4]
            second[0:2] = four[0:2]
            second[2:4] = (four[2:4].astype(single) + down[...].astype(single)).astype(bfloat)

    outs = pl.pallas_call(
        kernel,
        out_shape=[
            shaped(bfloat, *one.shape) for one, _, _, _ in groups for _ in range(2)
        ],
        in_specs=[VMEM] * (4 * len(groups)),
        out_specs=[VMEM] * (2 * len(groups)),
        compiler_params=pltpu.CompilerParams(vmem_limit_bytes=8 * 2**20),
        cost_estimate=pl.CostEstimate(flops=2**20, bytes_accessed=5 * 2**20, transcendentals=0),
        name="add_halves",
    )(*(part for group in groups for part in group))
    return [tuple(outs[2 * i : 2 * i + 2]) for i in range(len(groups))]


def plane_sum(one, two, first, second):
    both = list(zip((one, two), ("x", "y")))
    across = [(shift(v[2], axis, 1), shift(v[3], axis, -1)) for v, axis in both]
    across, first = lax.optimization_barrier((across, first))
    sent = add_halves([(v[1], up, v[4], down) for (v, _), (up, down) in zip(both, across)])
    got = [(shift(up, axis, 1), shift(down, axis, -1)) for (_, axis), (up, down) in zip(both, sent)]
    got = lax.optimization_barrier(got)
    sums = [
        v[0].astype(single) + (up.astype(single) + down.astype(single))
        for (v, _), (up, down) in zip(both, got)
    ]
    got = [
        [shift(v[step].astype(bfloat), axis, step) for step in range(1, 4)]
        for v, axis in zip(sums, ("y", "x"))
    ]
    got, second = lax.optimization_barrier((got, second))
    sums = [
        (v[0] + parts[0].astype(single)) + (parts[1].astype(single) + parts[2].astype(single))
        for v, parts in zip(sums, got)
    ]
    return sums[0], sums[1], first, second


def line_gather(own):
    near = jnp.concatenate([own, swap(own, "zl"), swap(own, "zh"), swap_both(own)], axis=0)
    return jnp.concatenate([near, swap(near, "c")], axis=0)


def head_sum(value):
    across = lax.ppermute(value, ("zl", "c"), [(0, 3), (1, 2), (2, 1), (3, 0)])
    return (value + swap(value, "c")) + (swap(value, "zl") + across)


def head_gather(own, mine, later=None):
    near = jnp.concatenate([own, swap(own, "zl")], axis=0)
    if later is not None:
        near, later = lax.optimization_barrier((near, later))
    parts = jnp.concatenate([near, swap(near, "c")], axis=0).reshape(4, 64, -1)
    rows = []
    for place in range(4):
        other = place ^ mine
        slot = (other & 1) * 2 + (other >> 1)
        rows.append(lax.dynamic_index_in_dim(parts, slot, 0, keepdims=False))
    rows = jnp.concatenate(rows, axis=0).astype(single)
    return rows if later is None else (rows, later)


def row_place(index, zl, c):
    core = (index >> 7) & 1
    low = (index >> 6) & 1
    return ((low ^ zl) * 2 + (core ^ c)) * 64 + (index & 63)


def block_range(block, cut, ends):
    first = block * BLOCK
    last = first + BLOCK - 1
    low_least = jnp.where(first >= cut, cut, 0)
    low_most = jnp.where(last >= cut, cut, 0)
    high_least = jnp.minimum(first, jnp.where(first >= cut, ends[1], ends[0]))
    start = low_least // BLOCK
    whole = jnp.minimum((low_most + BLOCK - 1) // BLOCK, block + 1)
    whole_end = jnp.maximum((high_least + 1) // BLOCK, whole)
    return start, whole, whole_end, block + 1


def stacked(ref, half):
    near = half * 128
    return jnp.concatenate(
        [
            ref[near : near + 128, 0:HD],
            ref[256 + near : 384 + near, 0:HD],
            ref[near : near + 128, HD : 2 * HD],
            ref[256 + near : 384 + near, HD : 2 * HD],
        ],
        axis=0,
    )


def unstack(ref, half, value):
    near = half * 128
    ref[near : near + 128, 0:HD] = value[0:128]
    ref[256 + near : 384 + near, 0:HD] = value[128:256]
    ref[near : near + 128, HD : 2 * HD] = value[256:384]
    ref[256 + near : 384 + near, HD : 2 * HD] = value[384:512]


def key_rows(ref, one, two, half):
    near = pl.multiple_of(half * 128, 128)
    far = pl.multiple_of(256 + half * 128, 128)
    return jnp.concatenate(
        [ref[one, two, pl.ds(near, 128), :], ref[one, two, pl.ds(far, 128), :]], axis=0
    )


def find_slot(info, where, block):
    slot = where[block]
    down = ((slot >> 2) - info[8]) & 3
    across = (slot - info[9]) & 3
    return down, across, (slot >> 4) ^ info[4]


def bring(pairs, sems):
    copies = [pltpu.make_async_copy(*pair, sems.at[i]) for i, pair in enumerate(pairs)]
    for copy in copies:
        copy.start()
    return copies


def ring_targets(buffer):
    return [
        buffer.at[0],
        buffer.at[1],
        buffer.at[2, pl.ds(0, 2)],
        buffer.at[2, pl.ds(2, 2)],
        buffer.at[3],
    ]


def in_hbm(values):
    return [pltpu.with_memory_space_constraint(value, pltpu.HBM) for value in values]


def turned(value, cosine, sine):
    return value * cosine + pltpu.roll(value, HD // 2, 1) * sine


def unit_of(value):
    factor = lax.rsqrt(jnp.mean(value * value, axis=-1, keepdims=True) + EPS)
    return value * factor, factor


def dot_nt(left, right):
    return lax.dot_general(left, right, (((1,), (1,)), ((), ())), preferred_element_type=single)


def dot_tn(left, right):
    return lax.dot_general(left, right, (((0,), (0,)), ((), ())), preferred_element_type=single)


def find_blocks(home, where):
    for slot in range(32):
        where[home[slot]] = slot


def tile_limits(info, half):
    zl, c, cut = info[2], info[3], info[5]
    ends = (info[6] - 1, cut + info[7] - 1)
    block = info[half]
    place = block * BLOCK + row_place(lax.broadcasted_iota(jnp.int32, (1, 512), 1), zl, c)
    second = place >= cut
    low = jnp.where(second, cut, 0)
    high = jnp.minimum(place, jnp.where(second, ends[1], ends[0]))
    return low, high, block_range(block, cut, ends)


def over_blocks(limits, step):
    start, whole, whole_end, stop = limits
    many = (whole_end - whole) // 4
    lax.fori_loop(start, whole, lambda block, _: step(block, 1, True), None)
    lax.fori_loop(0, many, lambda i, _: step(whole + 4 * i, 4, False), None)
    lax.fori_loop(whole + 4 * many, whole_end, lambda block, _: step(block, 1, False), None)
    lax.fori_loop(whole_end, stop, lambda block, _: step(block, 1, True), None)


def together(parts):
    return parts[0] if len(parts) == 1 else jnp.concatenate(parts, axis=0)


def attend_kernel(info, home, *refs):
    ins, (out, logs) = refs[:11], refs[11:13]
    query, keys, values, where, accum, total, sems = refs[13:]
    copies = bring(
        list(zip(ins, [query] + ring_targets(keys) + ring_targets(values))), sems
    )
    find_blocks(home, where)
    for copy in copies:
        copy.wait()
    key_place = row_place(lax.broadcasted_iota(jnp.int32, (256, 512), 0), info[2], info[3])
    for half in range(2):
        low, high, limits = tile_limits(info, half)
        rows = stacked(query, half)
        accum[...] = jnp.zeros_like(accum)
        total[...] = jnp.zeros_like(total)

        def step(block, count, masked):
            slots = [find_slot(info, where, block + i) for i in range(count)]
            key = together([key_rows(keys, down, across, side) for down, across, side in slots])
            value = together([key_rows(values, across, down, side) for down, across, side in slots])
            weight = jnp.exp2(dot_nt(key, rows) * (SCALE * LOG2E))
            if masked:
                place = key_place + block * BLOCK
                weight = jnp.where((place >= low) & (place <= high), weight, 0.0)
            total[...] += jnp.sum(weight.reshape(-1, 8, 512), axis=0)
            accum[...] += dot_tn(value, weight.astype(bfloat))

        over_blocks(limits, step)
        weights = jnp.sum(total[...], axis=0, keepdims=True)
        logs[half] = jnp.log2(weights)
        unstack(out, half, jnp.transpose(accum[...] / weights))


def attend_back_kernel(info, home, logs, gains, *refs):
    ins, (d_pre, gain_grad) = refs[:16], refs[16:18]
    d_keys, d_values = refs[18:23], refs[23:28]
    query, d_out, out, pre, cosine, sine, keys, values = refs[28:36]
    where, key_sum, value_sum, d_rows, d_query, sems = refs[36:]
    targets = [query, d_out, out, pre, cosine, sine] + ring_targets(keys) + ring_targets(values)
    copies = bring(list(zip(ins, targets)), sems)
    find_blocks(home, where)
    key_place = row_place(lax.broadcasted_iota(jnp.int32, (256, 512), 0), info[2], info[3])

    def clear(index, _):
        for accum in (key_sum, value_sum):
            accum[index] = jnp.zeros(accum.shape[1:], single)

    lax.fori_loop(0, 16, clear, None)
    for copy in copies:
        copy.wait()
    for half in range(2):
        low, high, limits = tile_limits(info, half)
        rows = stacked(query, half)
        grads = stacked(d_out, half)
        delta = jnp.sum(
            jnp.transpose(grads.astype(single) * stacked(out, half)), axis=0, keepdims=True
        )
        log = logs[half]
        d_rows[...] = jnp.zeros_like(d_rows)

        def step(block, count, masked):
            slots = [find_slot(info, where, block + i) for i in range(count)]
            key = together([key_rows(keys, down, across, side) for down, across, side in slots])
            value = together([key_rows(values, across, down, side) for down, across, side in slots])
            prob = jnp.exp2(dot_nt(key, rows) * (SCALE * LOG2E) - log)
            if masked:
                place = key_place + block * BLOCK
                prob = jnp.where((place >= low) & (place <= high), prob, 0.0)
            d_score = (prob * (dot_nt(value, grads) - delta)).astype(bfloat)
            d_value = jnp.dot(prob.astype(bfloat), grads, preferred_element_type=single)
            d_key = jnp.dot(d_score, rows, preferred_element_type=single)
            d_rows[...] += dot_tn(key, d_score)
            for i, (down, across, side) in enumerate(slots):
                near = pl.multiple_of(side * 128, 128)
                far = pl.multiple_of(256 + side * 128, 128)
                for accum, slot, grad in (
                    (key_sum, across * 4 + down, d_key),
                    (value_sum, down * 4 + across, d_value),
                ):
                    accum[slot, pl.ds(near, 128), :] += grad[i * 256 : i * 256 + 128]
                    accum[slot, pl.ds(far, 128), :] += grad[i * 256 + 128 : i * 256 + 256]

        over_blocks(limits, step)
        unstack(d_query, half, jnp.transpose(d_rows[...]) * SCALE)
    for one in range(4):
        for two in range(4):
            number, place = (one, two) if one < 2 else (4, two) if one == 3 else (2 + two // 2, two % 2)
            d_keys[number][place] = (key_sum[one * 4 + two] * SCALE).astype(bfloat)
            d_values[number][place] = value_sum[one * 4 + two].astype(bfloat)
    gain = gains[0:1]
    total = jnp.zeros((1, HD), single)
    for head in range(2):
        columns = slice(head * HD, (head + 1) * HD)
        d_turned = turned(d_query[:, columns], cosine[...], -sine[...])
        unit, factor = unit_of(pre[:, columns])
        total += jnp.sum(d_turned * unit, axis=0, keepdims=True)
        d_pre[:, columns] = rms_back(d_turned, unit, factor, gain).astype(bfloat)
    gain_grad[...] = total


def line_order(info):
    for core in range(2):
        for source in range(2):
            for low in range(2):
                there = ((low ^ info[2]) * 2 + (core ^ info[3])) * 64
                yield core * 4 + source * 2 + low, source, pl.multiple_of(there, 64)


def arrange_kernel(info, own, other, out):
    for place, source, there in line_order(info):
        out[place * 64 : place * 64 + 64, :] = (own, other)[source][pl.ds(there, 64), :]


def project_pairs_kernel(info, cosine, sine, *refs):
    normed, key, value, pre, weights, gains, small, extra, came, own, other, sems = refs[10:]
    copies = bring(list(zip(refs[:10], [own, other] + [came.at[i] for i in range(8)])), sems)
    for copy in copies:
        copy.wait()
    for one in range(4):
        for two in range(4):
            for number, y, x, column in ((one, one, two, 0), (4 + one, two, one, HD)):
                plane = ((y + info[8]) & 3) * 4 + ((x + info[9]) & 3)
                for side in range(2):
                    to = pl.ds(pl.multiple_of(side * 1024 + plane * 64, 64), 64)
                    block = came[number, two, side * 64 : side * 64 + 64, :]
                    weights[to, column : column + HD] = block[:, :HD]
                    extra[to, column : column + HD] = block[:, HD:]
    gains[...] = jnp.transpose(extra[:, 0:HD].astype(single))[0:8]
    total = jnp.zeros((16, HD), single)
    for block in range(32):
        total += extra[block * 64 : block * 64 + 16, HD : 2 * HD].astype(single)
    small[...] = total[0:8]
    gain = gains[0:1]
    for place, source, there in line_order(info):
        unit, _ = unit_of((own, other)[source][pl.ds(there, 64), :].astype(single))
        normed[place * 64 : place * 64 + 64, :] = (unit * gain).astype(bfloat)
    both = jnp.dot(normed[...], weights[...], preferred_element_type=single)
    pre[...] = both[:, :HD]
    unit, _ = unit_of(both[:, :HD])
    key[...] = turned(unit * small[1:2], cosine[...], sine[...]).astype(bfloat)
    value[...] = both[:, HD:].astype(bfloat)


def project_query_kernel(normed, weights, cosine, sine, gains, query, pre, gate_act):
    both = jnp.dot(normed[...], weights[:, 0 : 4 * HD], preferred_element_type=single)
    for head in range(2):
        columns = slice(head * HD, (head + 1) * HD)
        pre[:, columns] = both[:, columns]
        unit, _ = unit_of(both[:, columns])
        query[:, columns] = turned(unit * gains[0:1], cosine[...], sine[...]).astype(bfloat)
    gate_act[...] = jax.nn.sigmoid(both[:, 2 * HD : 4 * HD])


VMEM = pl.BlockSpec(memory_space=pltpu.VMEM)
SMEM = pl.BlockSpec(memory_space=pltpu.SMEM)
ANY = pl.BlockSpec(memory_space=pl.ANY)
HBM = pl.BlockSpec(memory_space=pltpu.HBM)


def shaped(dtype, *shape):
    return jax.ShapeDtypeStruct(shape, dtype)


def arrange(info, own, other):
    return pl.pallas_call(
        arrange_kernel,
        out_shape=shaped(own.dtype, 512, own.shape[1]),
        in_specs=[SMEM, VMEM, VMEM],
        out_specs=VMEM,
        cost_estimate=pl.CostEstimate(flops=0, bytes_accessed=4 * 2**20, transcendentals=0),
        name="arrange",
    )(info, own, other)


def project_pairs(info, own, other, cosine, sine, pieces):
    width = own.shape[1]
    return pl.pallas_call(
        project_pairs_kernel,
        out_shape=(
            shaped(bfloat, 512, width),
            shaped(bfloat, 512, HD),
            shaped(bfloat, 512, HD),
            shaped(single, 512, HD),
            shaped(bfloat, width, 2 * HD),
            shaped(single, 8, width),
            shaped(single, 8, HD),
        ),
        in_specs=[SMEM] + [VMEM] * 2 + [HBM] * 10,
        out_specs=[VMEM] * 7,
        scratch_shapes=[
            pltpu.VMEM((width, 2 * HD), bfloat),
            pltpu.VMEM((8, 4, HD, 2 * HD), bfloat),
            pltpu.VMEM((BLOCK, width), bfloat),
            pltpu.VMEM((BLOCK, width), bfloat),
            pltpu.SemaphoreType.DMA((10,)),
        ],
        compiler_params=pltpu.CompilerParams(vmem_limit_bytes=16 * 2**20),
        cost_estimate=pl.CostEstimate(
            flops=2**30, bytes_accessed=8 * 2**20, transcendentals=2**10
        ),
        name="project_pairs",
    )(info, cosine, sine, *in_hbm([own, other, *pieces[0], *pieces[1]]))


def project_query(normed, weights, cosine, sine, gains):
    return pl.pallas_call(
        project_query_kernel,
        out_shape=(
            shaped(bfloat, 512, 2 * HD),
            shaped(single, 512, 2 * HD),
            shaped(single, 512, 2 * HD),
        ),
        in_specs=[VMEM] * 5,
        out_specs=[VMEM] * 3,
        compiler_params=pltpu.CompilerParams(vmem_limit_bytes=12 * 2**20),
        cost_estimate=pl.CostEstimate(
            flops=2**30, bytes_accessed=8 * 2**20, transcendentals=2**17
        ),
        name="project_query",
    )(normed, weights, cosine, sine, gains)


def attend(info, home, query, pieces):
    return pl.pallas_call(
        attend_kernel,
        out_shape=(shaped(single, 512, 2 * HD), shaped(single, 2, 1, 512)),
        in_specs=[SMEM, SMEM] + [HBM] * 11,
        out_specs=(VMEM, VMEM),
        scratch_shapes=[
            pltpu.VMEM((512, 2 * HD), bfloat),
            pltpu.VMEM((4, 4, 512, HD), bfloat),
            pltpu.VMEM((4, 4, 512, HD), bfloat),
            pltpu.SMEM((32,), jnp.int32),
            pltpu.VMEM((HD, 512), single),
            pltpu.VMEM((8, 512), single),
            pltpu.SemaphoreType.DMA((11,)),
        ],
        compiler_params=pltpu.CompilerParams(vmem_limit_bytes=12 * 2**20),
        cost_estimate=pl.CostEstimate(
            flops=4 * 2**30, bytes_accessed=6 * 2**20, transcendentals=4 * 2**20
        ),
        name="attend",
    )(info, home, *in_hbm([query, *pieces[0], *pieces[1]]))


def attend_back(info, home, query, d_out, out, logs, pre, cosine, sine, gains, pieces):
    outs = pl.pallas_call(
        attend_back_kernel,
        out_shape=[shaped(bfloat, 512, 2 * HD), shaped(single, 1, HD)]
        + [pltpu.HBM((count, 512, HD), bfloat) for count in (4, 4, 2, 2, 4)] * 2,
        in_specs=[SMEM, SMEM, VMEM, VMEM] + [HBM] * 16,
        out_specs=[VMEM] * 12,
        scratch_shapes=[
            pltpu.VMEM((512, 2 * HD), bfloat),
            pltpu.VMEM((512, 2 * HD), bfloat),
            pltpu.VMEM((512, 2 * HD), single),
            pltpu.VMEM((512, 2 * HD), single),
            pltpu.VMEM((512, HD), single),
            pltpu.VMEM((512, HD), single),
            pltpu.VMEM((4, 4, 512, HD), bfloat),
            pltpu.VMEM((4, 4, 512, HD), bfloat),
            pltpu.SMEM((32,), jnp.int32),
            pltpu.VMEM((16, 512, HD), single),
            pltpu.VMEM((16, 512, HD), single),
            pltpu.VMEM((HD, 512), single),
            pltpu.VMEM((512, 2 * HD), single),
            pltpu.SemaphoreType.DMA((16,)),
        ],
        compiler_params=pltpu.CompilerParams(vmem_limit_bytes=28 * 2**20),
        cost_estimate=pl.CostEstimate(
            flops=10 * 2**30, bytes_accessed=12 * 2**20, transcendentals=4 * 2**20
        ),
        name="attend_back",
    )(
        info,
        home,
        logs,
        gains,
        *in_hbm([query, d_out, out, pre, cosine, sine, *pieces[0], *pieces[1]]),
    )
    return outs[0], outs[1], outs[2:7], outs[7:12]


def plane_grads(lefts, rights, tile, rows=128, columns=None, into=None, extras=(), by_x=False):
    starts = []
    count = 0
    for _, right in rights:
        starts.append(count)
        count += right.shape[1] // tile
    spans = list(zip(starts, starts[1:] + [count]))
    depth, height = lefts[0].shape
    columns = columns or count * tile
    shift_by = 0 if into is None else columns // tile - count
    flips = {}
    for (number, _), start in zip(rights, starts):
        flips.setdefault(number, start)

    def kernel(*refs):
        left_refs, right_refs = refs[: len(lefts)], refs[len(lefts) : len(lefts) + len(rights)]
        extra_refs = refs[len(lefts) + len(rights) : len(lefts) + len(rights) + len(extras)]
        out, flipped = refs[-2:]
        step = pl.program_id(0)

        def flip(left):
            for group in range(8):
                side, y = group // 4, group % 4
                turned = jnp.transpose(left[:, group * 256 : group * 256 + 256])
                for x in range(4):
                    first = ((x * 4 + y if by_x else y * 4 + x) * 2 + side) * 64
                    flipped[first : first + 64, :] = turned[x * 64 : x * 64 + 64]

        def product(right):
            for one in range(4):
                left = flipped[one * 512 : one * 512 + 512, :]
                part = jnp.dot(left, right, preferred_element_type=single).astype(bfloat)
                out[one * 4 : one * 4 + 4, 0:128] = part.reshape(4, 128, tile)
            for number, ref in enumerate(extra_refs):
                out[:, 128:144, number * HD : (number + 1) * HD] = jnp.broadcast_to(
                    ref[...].astype(bfloat)[None], (16, 16, HD)
                )

        for number, start in flips.items():
            pl.when(step == start)(lambda number=number: flip(left_refs[number]))
        for ref, (start, stop) in zip(right_refs, spans):
            pl.when((step >= start) & (step < stop))(lambda ref=ref: product(ref[...]))

    def right_spec(start, stop):
        return pl.BlockSpec(
            (depth, tile), lambda i: (0, jnp.minimum(jnp.maximum(i - start, 0), stop - start - 1))
        )

    return pl.pallas_call(
        kernel,
        grid=(count,),
        in_specs=[
            pl.BlockSpec((depth, height), lambda i: (0, 0), pipeline_mode=pl.Buffered(1))
            for _ in lefts
        ]
        + [right_spec(*span) for span in spans]
        + [pl.BlockSpec((1, HD), lambda i: (0, 0)) for _ in extras]
        + ([] if into is None else [ANY]),
        out_specs=pl.BlockSpec((16, rows, tile), lambda i: (0, 0, i + shift_by)),
        out_shape=pltpu.HBM((16, rows, columns), bfloat),
        input_output_aliases={} if into is None else {len(lefts) + len(rights) + len(extras): 0},
        scratch_shapes=[pltpu.VMEM((height, depth), bfloat)],
        compiler_params=pltpu.CompilerParams(
            vmem_limit_bytes=18 * 2**20, dimension_semantics=("arbitrary",)
        ),
        cost_estimate=pl.CostEstimate(
            flops=2 * depth * height * count * tile,
            bytes_accessed=2 * (depth + height) * count * tile + 2 * depth * height,
            transcendentals=0,
        ),
        name="plane_grads",
    )(*lefts, *(right for _, right in rights), *extras, *([] if into is None else [into]))


def columns_of(weight, side, width):
    return lax.dynamic_slice_in_dim(weight, side * width, width, 1)


def rows_of(weight, side, width):
    return lax.dynamic_slice_in_dim(weight, side * width, width, 0)


def in_order(zh, own, other, axis):
    first = jnp.where(zh == 0, own, other)
    second = jnp.where(zh == 0, other, own)
    return jnp.concatenate([first, second], axis=axis)


def gather_plane(block):
    whole = lax.all_gather(block, PLANE, axis=1, tiled=True)
    return whole.reshape(-1, block.shape[-1])


def per_device(
    tokens,
    query_weight,
    key_weight,
    value_weight,
    gate_weight,
    out_weight,
    norm_gain,
    query_gain,
    key_gain,
    inner_gate,
    inner_lift,
    inner_down,
    inner_gain,
    out_grad,
    bucket_len,
    seq_len,
    home_block,
):
    zh = lax.axis_index("zh")
    zl = lax.axis_index("zl")
    c = lax.axis_index("c")
    mine = zl * 2 + c
    width = tokens.shape[1]
    seq_index = zh * 16 + lax.axis_index("y") * 4 + lax.axis_index("x")
    block_own = lax.dynamic_index_in_dim(home_block, seq_index, 0, keepdims=False)
    block_other = lax.dynamic_index_in_dim(home_block, seq_index ^ 16, 0, keepdims=False)
    info = jnp.stack(
        [
            block_own,
            block_other,
            zl,
            c,
            zh,
            bucket_len[0],
            seq_len[0],
            seq_len[1],
            lax.axis_index("y"),
            lax.axis_index("x"),
        ]
    ).astype(jnp.int32)

    lane = jnp.arange(HD, dtype=jnp.int32)

    def head_gain(vector):
        return jnp.where(lane // 4 == seq_index, jnp.tile(vector, 32), 0)

    norm_columns = jnp.pad(jnp.stack([norm_gain, inner_gain], axis=1), ((0, 0), (0, HD - 2)))
    head_rows = jnp.pad(
        jnp.stack([head_gain(query_gain), head_gain(key_gain)], axis=0), ((0, 62), (0, 0))
    ).astype(bfloat)

    def pairs_pack(side):
        return jnp.concatenate(
            [
                columns_of(key_weight, side, HD),
                norm_columns,
                columns_of(value_weight, side, HD),
                head_rows,
            ],
            axis=1,
        )

    def outer_pack(side):
        return jnp.concatenate(
            [
                columns_of(query_weight, side, 256),
                columns_of(gate_weight, side, 256),
                rows_of(out_weight, side, 256).T,
            ],
            axis=1,
        )

    def inner_pack(side):
        gate, lift, down = inner_shards
        return jnp.concatenate(
            [columns_of(gate, side, 768), columns_of(lift, side, 768), rows_of(down, side, 768).T],
            axis=1,
        )

    def pair_up(pack):
        own = pack(zh)
        other = swap(pack(1 - zh), "zh")
        return in_order(zh, own[None], other[None], 0)

    first_block = pair_up(
        lambda side: jnp.concatenate([pairs_pack(side), outer_pack(side)], axis=1)
    )
    index = jnp.arange(512, dtype=jnp.int32)
    half_of = (index >> 7) & 1
    place = jnp.where(half_of == 0, block_own, block_other) * BLOCK + row_place(
        ((index >> 8) << 7) | (index & 127), zl, c
    )
    offset = jnp.where(place >= bucket_len[0], place - bucket_len[0], place)
    freq = jnp.power(THETA, -jnp.arange(HD // 2, dtype=single) * 2.0 / HD)
    angle = offset.astype(single)[:, None] * freq[None, :]
    cosine = jnp.cos(angle)
    sine = jnp.sin(angle)
    cosine = jnp.concatenate([cosine, cosine], axis=1)
    sine = jnp.concatenate([-sine, sine], axis=1)

    first_block, cosine, sine, info = lax.optimization_barrier((first_block, cosine, sine, info))
    tokens_other = swap(tokens, "zh")
    pairs_block, outer_block = first_block[:, :, : 4 * HD], first_block[:, :, 4 * HD :]
    outer = gather_plane(outer_block)
    pairs_wide = pairs_block.reshape(HD, 4 * HD)
    weight_pieces, _ = plane_gather(pairs_wide[:, : 2 * HD], pairs_wide[:, 2 * HD :], (), False)
    normed, key_rot, value, k_pre, w_pairs, gains, head_gains = project_pairs(
        info, tokens, tokens_other, cosine, sine, weight_pieces
    )
    key_rot, inner_shards = lax.optimization_barrier(
        (key_rot, (inner_gate, inner_lift, inner_down))
    )
    inner_block = pair_up(inner_pack)
    gain_norm, gain_inner = gains[0:1], gains[1:2]
    gain_query, gain_key = head_gains[0:1], head_gains[1:2]
    w_heads = outer[:, :512]
    w_out = outer[:, 512:]
    query, q_pre, gate_sig = project_query(normed, outer, cosine, sine, head_gains)
    pieces, (inner_block, out_grad_sent) = plane_gather(
        key_rot, value, (inner_block, out_grad), True
    )
    rows_grad = arrange(info, out_grad, swap(out_grad_sent, "zh"))
    inner = gather_plane(inner_block)
    w_gate_lift = inner[:, :1536]
    w_down = inner[:, 1536:]
    query, rows_grad = lax.optimization_barrier((query, rows_grad))
    attended, logs = attend(info, home_block, query, pieces)
    gated = (attended * gate_sig).astype(bfloat)

    def line_product(left, right):
        return line_sum(dot_nt(left[:256], right), dot_nt(left[256:], right))

    inputs = rows_of(tokens, mine, 64).astype(single)
    mixed_in = inputs + line_product(gated, w_out)
    unit_two, factor_two = rms_parts(mixed_in)
    normed_two = line_gather((unit_two * gain_inner).astype(bfloat))
    d_hidden = jnp.dot(rows_grad, w_down, preferred_element_type=single)
    gate_lift = jnp.dot(normed_two, w_gate_lift, preferred_element_type=single)
    gate_val = gate_lift[:, :768]
    lift_val = gate_lift[:, 768:]
    gate_act = jax.nn.sigmoid(gate_val)
    hidden = (gate_val * gate_act * lift_val).astype(bfloat)
    d_gate = (d_hidden * lift_val * gate_act * (1.0 + gate_val * (1.0 - gate_act))).astype(bfloat)
    d_lift = (d_hidden * gate_val * gate_act).astype(bfloat)
    d_gate_lift = jnp.concatenate([d_gate, d_lift], axis=1)

    def inner_grads(needs):
        return plane_grads(
            [normed_two, rows_grad],
            [(0, needs[0]), (0, needs[1]), (1, needs[2])],
            384,
        )

    d_normed_two, grad_inner = line_sum_end(
        line_sum_middle(dot_nt(d_gate_lift[:256], w_gate_lift), dot_nt(d_gate_lift[256:], w_gate_lift)),
        (inner_grads, (d_gate, d_lift, hidden)),
    )

    def scatter_plane(grad):
        part = lax.psum_scatter(grad, PLANE, scatter_dimension=0, tiled=False)
        return part.reshape(2, 64, -1)

    part = scatter_plane(grad_inner)
    d_mixed = rows_grad[:64].astype(single) + rms_back(
        d_normed_two, unit_two, factor_two, gain_inner
    )
    d_attn = line_gather(d_mixed.astype(bfloat))
    d_gated = jnp.dot(d_attn, w_out, preferred_element_type=single)
    d_attended = (d_gated * gate_sig).astype(bfloat)
    d_gate_pre = (d_gated * attended * gate_sig * (1.0 - gate_sig)).astype(bfloat)

    def rounded(rows):
        return lax.reduce_precision(rows, 8, 7).astype(bfloat)

    def both_sides(part):
        own = lax.dynamic_index_in_dim(part, zh, 0, keepdims=False).astype(single)
        sent = lax.dynamic_index_in_dim(part, 1 - zh, 0, keepdims=False).astype(bfloat)
        sent, part = lax.optimization_barrier((sent, part))
        return own, swap(sent, "zh").astype(single), part

    d_q_pre, query_gain_part, d_keys, d_values = attend_back(
        info,
        home_block,
        query,
        d_attended,
        attended,
        logs,
        q_pre,
        cosine,
        sine,
        head_gains,
        pieces,
    )
    grad_outer = plane_grads(
        [d_attn, normed], [(0, gated), (1, d_gate_pre), (1, d_q_pre)], 256, by_x=True
    )
    d_heads = jnp.concatenate([d_q_pre, d_gate_pre], axis=1)

    d_key, d_value, grad_outer, (normed_near, normed_far) = plane_sum(
        d_keys,
        d_values,
        grad_outer,
        (dot_nt(d_heads[:256], w_heads), dot_nt(d_heads[256:], w_heads)),
    )
    grad_outer, part = lax.optimization_barrier((grad_outer, part))
    rest = lax.psum_scatter(
        grad_outer.reshape(4, 4, 128, -1), "x", scatter_dimension=0, tiled=False
    )
    rest = lax.psum_scatter(rest, "y", scatter_dimension=0, tiled=False).reshape(2, 64, -1)
    k_unit, k_factor = rms_parts(k_pre)
    d_k_turned = d_key * cosine - jnp.roll(d_key, HD // 2, axis=1) * sine
    key_gain_part = jnp.sum(d_k_turned * k_unit, axis=0, keepdims=True)
    d_k_pre = rms_back(d_k_turned, k_unit, k_factor, gain_key).astype(bfloat)
    d_kv_pre = jnp.concatenate([d_k_pre, d_value.astype(bfloat)], axis=1)
    normed_far = (normed_far + dot_nt(d_kv_pre[256:], w_pairs)).astype(bfloat)
    normed_far, d_kv_pre = lax.optimization_barrier((normed_far, d_kv_pre))
    pairs_sent = plane_grads(
        [normed], [(0, d_kv_pre)], 256, rows=144, extras=(query_gain_part, key_gain_part)
    )
    pairs_sent, d_kv_pre = lax.optimization_barrier((pairs_sent, d_kv_pre))
    normed_near = normed_near + dot_nt(d_kv_pre[:256], w_pairs)
    pairs_got = lax.all_to_all(pairs_sent, PLANE, 0, 0, tiled=True)
    here, hidden = lax.optimization_barrier((line_sum_middle(normed_near, normed_far), hidden))
    d_normed = line_sum_end(here)
    result_rows = mixed_in + line_product(hidden, w_down)
    unit_in, factor_in = rms_parts(inputs)
    token_rows = d_mixed + rms_back(d_normed, unit_in, factor_in, gain_norm)

    part_own, part_got, part = both_sides(part)
    pairs_got, rest, token_rows, part_got = lax.optimization_barrier(
        (pairs_got, rest, token_rows, part_got)
    )
    pairs_sum = jnp.sum(pairs_got.astype(single), axis=0)
    result, (pairs_sum, part) = head_gather(rounded(result_rows), mine, (pairs_sum, part))
    gain_part = pairs_sum[128]
    pair_part = pairs_sum[:128].reshape(2, 64, 256)
    tokens_grad = head_gather(rounded(token_rows), mine)

    def weighted(block, part):
        return jnp.sum(block.astype(single) * part.astype(single), axis=2)

    norm_part = (
        weighted(outer_block[:, :, :256], rest[:, :, 512:])
        + weighted(outer_block[:, :, 256:512], rest[:, :, 256:512])
        + weighted(pairs_block[:, :, :HD], pair_part[:, :, :HD])
        + weighted(pairs_block[:, :, 2 * HD : 3 * HD], pair_part[:, :, HD:])
    ) / pairs_block[:, :, HD].astype(single)
    inner_gain_part = weighted(inner_block[:, :, :1536], part[:, :, :1536]) / pairs_block[
        :, :, HD + 1
    ].astype(single)
    gain_line = jnp.concatenate(
        [
            norm_part.reshape(HD),
            inner_gain_part.reshape(HD),
            gain_part,
        ]
    ).reshape(4, HD)
    gain_line = lax.reduce_precision(gain_line, 8, 7)
    last = jnp.concatenate([rest.astype(single), pair_part], axis=2)
    last_own = lax.dynamic_index_in_dim(last, zh, 0, keepdims=False)
    last_sent = lax.dynamic_index_in_dim(last, 1 - zh, 0, keepdims=False)
    last_got = swap(
        jnp.concatenate([last_sent, jnp.pad(gain_line, ((0, 60), (0, 0)))], axis=1).astype(bfloat),
        "zh",
    ).astype(single)
    gain_line = head_sum(gain_line + last_got[:4, 1024:])

    def shard(own, got, start, count):
        return in_order(zh, own[:, start : start + count], got[:, start : start + count], 1)

    shard_igate = shard(part_own, part_got, 0, 768)
    shard_ilift = shard(part_own, part_got, 768, 768)
    shard_idown = shard(part_own, part_got, 1536, 768).T
    shard_out = shard(last_own, last_got, 0, 256).T
    shard_gate = shard(last_own, last_got, 256, 256)
    shard_query = shard(last_own, last_got, 512, 256)
    shard_key = shard(last_own, last_got, 768, 128)
    shard_value = shard(last_own, last_got, 896, 128)

    gain_own = lax.dynamic_index_in_dim(gain_line[:2].reshape(2, 2, 64), zh, 1, keepdims=False)
    gain_sides = lax.dynamic_slice_in_dim(gain_line[2:], seq_index * 4, 4, 1)

    return (
        result,
        tokens_grad,
        shard_query,
        shard_key,
        shard_value,
        shard_gate,
        shard_out,
        gain_own[0],
        gain_sides[0],
        gain_sides[1],
        shard_igate,
        shard_ilift,
        shard_idown,
        gain_own[1],
    )


def solution(mesh):
    fine = Mesh(mesh.devices.reshape(2, 4, 4, 2, 2), ("zh", "y", "x", "zl", "c"))
    seq = ("zh", "y", "x")
    head = ("zl", "c")
    in_specs = (
        P(seq, None),
        P(seq, head),
        P(seq, head),
        P(seq, head),
        P(seq, head),
        P(head, seq),
        P(seq),
        P(seq),
        P(seq),
        P(seq, head),
        P(seq, head),
        P(head, seq),
        P(seq),
        P(seq, None),
        P(),
        P(),
        P(),
    )
    out_specs = (
        P(seq, None),
        P(seq, None),
        P(seq, head),
        P(seq, head),
        P(seq, head),
        P(seq, head),
        P(head, seq),
        P(seq),
        P(seq),
        P(seq),
        P(seq, head),
        P(seq, head),
        P(head, seq),
        P(seq),
    )
    return jax.shard_map(
        per_device, mesh=fine, in_specs=in_specs, out_specs=out_specs, check_vma=False
    )
```

```python
import jax
import jax.numpy as jnp
from jax import lax
from jax.experimental import pallas as pl
from jax.experimental.pallas import tpu as pltpu
from jax.sharding import Mesh
from jax.sharding import PartitionSpec as P

HD = 128
BLOCK = 256
EPS = 1e-06
THETA = 1000000.0
LOG2E = 1.4426950408889634
SCALE = HD ** (-0.5)
PLANE = ("y", "x")
bfloat = jnp.bfloat16
single = jnp.float32


def rms_parts(value):
    factor = lax.rsqrt(jnp.mean(value * value, axis=-1, keepdims=True) + EPS)
    return (value * factor, factor)


def rms_back(grad, unit_val, factor, gain):
    scaled = grad * gain
    return factor * (scaled - unit_val * jnp.mean(unit_val * scaled, axis=-1, keepdims=True))


def swap(value, axis):
    return lax.ppermute(value, axis, [(0, 1), (1, 0)])


def swap_both(value):
    return lax.ppermute(value, ("zh", "zl"), [(0, 3), (1, 2), (2, 1), (3, 0)])


def line_sum(near, far):
    return line_sum_end(line_sum_middle(near, far))


def line_sum_middle(near, far):
    return near + swap(far.astype(bfloat), "c").astype(single)


def line_sum_end(here, beside=None):
    made = None
    if beside is not None:
        here, needs = lax.optimization_barrier((here, beside[1]))
        made = beside[0](needs)
    sent = here.astype(bfloat)
    got = (swap(sent[64:128], "zl"), swap(sent[128:192], "zh"), swap_both(sent[192:256]))
    if beside is not None:
        got, made = lax.optimization_barrier((got, made))
    one, two, three = (piece.astype(single) for piece in got)
    total = (here[:64] + one) + (two + three)
    return total if beside is None else (total, made)


def shift(value, axis, step):
    return lax.ppermute(value, axis, [(i, (i + step) % 4) for i in range(4)])


def plane_gather(one, two, later, ring):
    got = [
        [shift(value, axis, -step) for step in range(1, 4)]
        for value, axis in ((one, "x"), (two, "y"))
    ]
    got, later = lax.optimization_barrier((got, later))
    lines = [jnp.stack([v] + parts, axis=0) for v, parts in zip((one, two), got)]
    if not ring:
        pieces = [
            [line] + [shift(line, axis, -step) for step in range(1, 4)]
            for line, axis in zip(lines, ("y", "x"))
        ]
        return pieces, later
    next_to = [(shift(line, axis, -1), shift(line, axis, 1)) for line, axis in zip(lines, ("y", "x"))]
    return [
        [line, up, shift(up[:2], axis, -1), shift(down[2:], axis, 1), down]
        for line, (up, down), axis in zip(lines, next_to, ("y", "x"))
    ], later


def add_halves(groups):
    def kernel(*refs):
        for number in range(len(groups)):
            one, up, four, down = refs[4 * number : 4 * number + 4]
            first, second = refs[4 * len(groups) + 2 * number : 4 * len(groups) + 2 * number + 2]
            first[0:2] = (one[0:2].astype(single) + up[...].astype(single)).astype(bfloat)
            first[2:4] = one[2:4]
            second[0:2] = four[0:2]
            second[2:4] = (four[2:4].astype(single) + down[...].astype(single)).astype(bfloat)

    outs = pl.pallas_call(
        kernel,
        out_shape=[
            shaped(bfloat, *one.shape) for one, _, _, _ in groups for _ in range(2)
        ],
        in_specs=[VMEM] * (4 * len(groups)),
        out_specs=[VMEM] * (2 * len(groups)),
        compiler_params=pltpu.CompilerParams(vmem_limit_bytes=8 * 2**20),
        cost_estimate=pl.CostEstimate(flops=2**20, bytes_accessed=5 * 2**20, transcendentals=0),
        name="add_halves",
    )(*(part for group in groups for part in group))
    return [tuple(outs[2 * i : 2 * i + 2]) for i in range(len(groups))]


def plane_sum(one, two, first, second):
    both = list(zip((one, two), ("x", "y")))
    across = [(shift(v[2], axis, 1), shift(v[3], axis, -1)) for v, axis in both]
    across, first = lax.optimization_barrier((across, first))
    sent = add_halves([(v[1], up, v[4], down) for (v, _), (up, down) in zip(both, across)])
    got = [(shift(up, axis, 1), shift(down, axis, -1)) for (_, axis), (up, down) in zip(both, sent)]
    got = lax.optimization_barrier(got)
    sums = [
        v[0].astype(single) + (up.astype(single) + down.astype(single))
        for (v, _), (up, down) in zip(both, got)
    ]
    got = [
        [shift(v[step].astype(bfloat), axis, step) for step in range(1, 4)]
        for v, axis in zip(sums, ("y", "x"))
    ]
    got, second = lax.optimization_barrier((got, second))
    sums = [
        (v[0] + parts[0].astype(single)) + (parts[1].astype(single) + parts[2].astype(single))
        for v, parts in zip(sums, got)
    ]
    return sums[0], sums[1], first, second


def line_gather(own):
    near = jnp.concatenate([own, swap(own, "zl"), swap(own, "zh"), swap_both(own)], axis=0)
    return jnp.concatenate([near, swap(near, "c")], axis=0)


def head_sum(value):
    across = lax.ppermute(value, ("zl", "c"), [(0, 3), (1, 2), (2, 1), (3, 0)])
    return (value + swap(value, "c")) + (swap(value, "zl") + across)


def head_gather(own, mine, later=None):
    near = jnp.concatenate([own, swap(own, "zl")], axis=0)
    if later is not None:
        near, later = lax.optimization_barrier((near, later))
    parts = jnp.concatenate([near, swap(near, "c")], axis=0).reshape(4, 64, -1)
    rows = []
    for place in range(4):
        other = place ^ mine
        slot = (other & 1) * 2 + (other >> 1)
        rows.append(lax.dynamic_index_in_dim(parts, slot, 0, keepdims=False))
    rows = jnp.concatenate(rows, axis=0).astype(single)
    return rows if later is None else (rows, later)


def row_place(index, zl, c):
    core = (index >> 7) & 1
    low = (index >> 6) & 1
    return ((low ^ zl) * 2 + (core ^ c)) * 64 + (index & 63)


def block_range(block, cut, ends):
    first = block * BLOCK
    last = first + BLOCK - 1
    low_least = jnp.where(first >= cut, cut, 0)
    low_most = jnp.where(last >= cut, cut, 0)
    high_least = jnp.minimum(first, jnp.where(first >= cut, ends[1], ends[0]))
    start = low_least // BLOCK
    whole = jnp.minimum((low_most + BLOCK - 1) // BLOCK, block + 1)
    whole_end = jnp.maximum((high_least + 1) // BLOCK, whole)
    return start, whole, whole_end, block + 1


def stacked(ref, half):
    near = half * 128
    return jnp.concatenate(
        [
            ref[near : near + 128, 0:HD],
            ref[256 + near : 384 + near, 0:HD],
            ref[near : near + 128, HD : 2 * HD],
            ref[256 + near : 384 + near, HD : 2 * HD],
        ],
        axis=0,
    )


def unstack(ref, half, value):
    near = half * 128
    ref[near : near + 128, 0:HD] = value[0:128]
    ref[256 + near : 384 + near, 0:HD] = value[128:256]
    ref[near : near + 128, HD : 2 * HD] = value[256:384]
    ref[256 + near : 384 + near, HD : 2 * HD] = value[384:512]


def key_rows(ref, one, two, half):
    near = pl.multiple_of(half * 128, 128)
    far = pl.multiple_of(256 + half * 128, 128)
    return jnp.concatenate(
        [ref[one, two, pl.ds(near, 128), :], ref[one, two, pl.ds(far, 128), :]], axis=0
    )


def find_slot(info, where, block):
    slot = where[block]
    down = ((slot >> 2) - info[8]) & 3
    across = (slot - info[9]) & 3
    return down, across, (slot >> 4) ^ info[4]


def bring(pairs, sems):
    copies = [pltpu.make_async_copy(*pair, sems.at[i]) for i, pair in enumerate(pairs)]
    for copy in copies:
        copy.start()
    return copies


def ring_targets(buffer):
    return [
        buffer.at[0],
        buffer.at[1],
        buffer.at[2, pl.ds(0, 2)],
        buffer.at[2, pl.ds(2, 2)],
        buffer.at[3],
    ]


def in_hbm(values):
    return [pltpu.with_memory_space_constraint(value, pltpu.HBM) for value in values]


def turned(value, cosine, sine):
    return value * cosine + pltpu.roll(value, HD // 2, 1) * sine


def unit_of(value):
    factor = lax.rsqrt(jnp.mean(value * value, axis=-1, keepdims=True) + EPS)
    return value * factor, factor


def dot_nt(left, right):
    return lax.dot_general(left, right, (((1,), (1,)), ((), ())), preferred_element_type=single)


def dot_tn(left, right):
    return lax.dot_general(left, right, (((0,), (0,)), ((), ())), preferred_element_type=single)


def find_blocks(home, where):
    for slot in range(32):
        where[home[slot]] = slot


def tile_limits(info, half):
    zl, c, cut = info[2], info[3], info[5]
    ends = (info[6] - 1, cut + info[7] - 1)
    block = info[half]
    place = block * BLOCK + row_place(lax.broadcasted_iota(jnp.int32, (1, 512), 1), zl, c)
    second = place >= cut
    low = jnp.where(second, cut, 0)
    high = jnp.minimum(place, jnp.where(second, ends[1], ends[0]))
    return low, high, block_range(block, cut, ends)


def over_blocks(limits, step):
    start, whole, whole_end, stop = limits
    many = (whole_end - whole) // 4
    lax.fori_loop(start, whole, lambda block, _: step(block, 1, True), None)
    lax.fori_loop(0, many, lambda i, _: step(whole + 4 * i, 4, False), None)
    lax.fori_loop(whole + 4 * many, whole_end, lambda block, _: step(block, 1, False), None)
    lax.fori_loop(whole_end, stop, lambda block, _: step(block, 1, True), None)


def together(parts):
    return parts[0] if len(parts) == 1 else jnp.concatenate(parts, axis=0)


def attend_kernel(info, home, *refs):
    ins, (out, logs) = refs[:11], refs[11:13]
    query, keys, values, where, accum, total, sems = refs[13:]
    copies = bring(
        list(zip(ins, [query] + ring_targets(keys) + ring_targets(values))), sems
    )
    find_blocks(home, where)
    for copy in copies:
        copy.wait()
    key_place = row_place(lax.broadcasted_iota(jnp.int32, (256, 512), 0), info[2], info[3])
    for half in range(2):
        low, high, limits = tile_limits(info, half)
        rows = stacked(query, half)
        accum[...] = jnp.zeros_like(accum)
        total[...] = jnp.zeros_like(total)

        def step(block, count, masked):
            slots = [find_slot(info, where, block + i) for i in range(count)]
            key = together([key_rows(keys, down, across, side) for down, across, side in slots])
            value = together([key_rows(values, across, down, side) for down, across, side in slots])
            weight = jnp.exp2(dot_nt(key, rows) * (SCALE * LOG2E))
            if masked:
                place = key_place + block * BLOCK
                weight = jnp.where((place >= low) & (place <= high), weight, 0.0)
            total[...] += jnp.sum(weight.reshape(-1, 8, 512), axis=0)
            accum[...] += dot_tn(value, weight.astype(bfloat))

        over_blocks(limits, step)
        weights = jnp.sum(total[...], axis=0, keepdims=True)
        logs[half] = jnp.log2(weights)
        unstack(out, half, jnp.transpose(accum[...] / weights))


def attend_back_kernel(info, home, logs, gains, *refs):
    ins, (d_pre, gain_grad) = refs[:16], refs[16:18]
    d_keys, d_values = refs[18:23], refs[23:28]
    query, d_out, out, pre, cosine, sine, keys, values = refs[28:36]
    where, key_sum, value_sum, d_rows, d_query, sems = refs[36:]
    targets = [query, d_out, out, pre, cosine, sine] + ring_targets(keys) + ring_targets(values)
    copies = bring(list(zip(ins, targets)), sems)
    find_blocks(home, where)
    key_place = row_place(lax.broadcasted_iota(jnp.int32, (256, 512), 0), info[2], info[3])

    def clear(index, _):
        for accum in (key_sum, value_sum):
            accum[index] = jnp.zeros(accum.shape[1:], single)

    lax.fori_loop(0, 16, clear, None)
    for copy in copies:
        copy.wait()
    for half in range(2):
        low, high, limits = tile_limits(info, half)
        rows = stacked(query, half)
        grads = stacked(d_out, half)
        delta = jnp.sum(
            jnp.transpose(grads.astype(single) * stacked(out, half)), axis=0, keepdims=True
        )
        log = logs[half]
        d_rows[...] = jnp.zeros_like(d_rows)

        def step(block, count, masked):
            slots = [find_slot(info, where, block + i) for i in range(count)]
            key = together([key_rows(keys, down, across, side) for down, across, side in slots])
            value = together([key_rows(values, across, down, side) for down, across, side in slots])
            prob = jnp.exp2(dot_nt(key, rows) * (SCALE * LOG2E) - log)
            if masked:
                place = key_place + block * BLOCK
                prob = jnp.where((place >= low) & (place <= high), prob, 0.0)
            d_score = (prob * (dot_nt(value, grads) - delta)).astype(bfloat)
            d_value = jnp.dot(prob.astype(bfloat), grads, preferred_element_type=single)
            d_key = jnp.dot(d_score, rows, preferred_element_type=single)
            d_rows[...] += dot_tn(key, d_score)
            for i, (down, across, side) in enumerate(slots):
                near = pl.multiple_of(side * 128, 128)
                far = pl.multiple_of(256 + side * 128, 128)
                for accum, slot, grad in (
                    (key_sum, across * 4 + down, d_key),
                    (value_sum, down * 4 + across, d_value),
                ):
                    accum[slot, pl.ds(near, 128), :] += grad[i * 256 : i * 256 + 128]
                    accum[slot, pl.ds(far, 128), :] += grad[i * 256 + 128 : i * 256 + 256]

        over_blocks(limits, step)
        unstack(d_query, half, jnp.transpose(d_rows[...]) * SCALE)
    for one in range(4):
        for two in range(4):
            number, place = (one, two) if one < 2 else (4, two) if one == 3 else (2 + two // 2, two % 2)
            d_keys[number][place] = (key_sum[one * 4 + two] * SCALE).astype(bfloat)
            d_values[number][place] = value_sum[one * 4 + two].astype(bfloat)
    gain = gains[0:1]
    total = jnp.zeros((1, HD), single)
    for head in range(2):
        columns = slice(head * HD, (head + 1) * HD)
        d_turned = turned(d_query[:, columns], cosine[...], -sine[...])
        unit, factor = unit_of(pre[:, columns])
        total += jnp.sum(d_turned * unit, axis=0, keepdims=True)
        d_pre[:, columns] = rms_back(d_turned, unit, factor, gain).astype(bfloat)
    gain_grad[...] = total


def line_order(info):
    for core in range(2):
        for source in range(2):
            for low in range(2):
                there = ((low ^ info[2]) * 2 + (core ^ info[3])) * 64
                yield core * 4 + source * 2 + low, source, pl.multiple_of(there, 64)


def arrange_kernel(info, own, other, out):
    for place, source, there in line_order(info):
        out[place * 64 : place * 64 + 64, :] = (own, other)[source][pl.ds(there, 64), :]


def project_pairs_kernel(info, cosine, sine, *refs):
    normed, key, value, pre, weights, gains, small, extra, came, own, other, sems = refs[10:]
    copies = bring(list(zip(refs[:10], [own, other] + [came.at[i] for i in range(8)])), sems)
    for copy in copies:
        copy.wait()
    for one in range(4):
        for two in range(4):
            for number, y, x, column in ((one, one, two, 0), (4 + one, two, one, HD)):
                plane = ((y + info[8]) & 3) * 4 + ((x + info[9]) & 3)
                for side in range(2):
                    to = pl.ds(pl.multiple_of(side * 1024 + plane * 64, 64), 64)
                    block = came[number, two, side * 64 : side * 64 + 64, :]
                    weights[to, column : column + HD] = block[:, :HD]
                    extra[to, column : column + HD] = block[:, HD:]
    gains[...] = jnp.transpose(extra[:, 0:HD].astype(single))[0:8]
    total = jnp.zeros((16, HD), single)
    for block in range(32):
        total += extra[block * 64 : block * 64 + 16, HD : 2 * HD].astype(single)
    small[...] = total[0:8]
    gain = gains[0:1]
    for place, source, there in line_order(info):
        unit, _ = unit_of((own, other)[source][pl.ds(there, 64), :].astype(single))
        normed[place * 64 : place * 64 + 64, :] = (unit * gain).astype(bfloat)
    both = jnp.dot(normed[...], weights[...], preferred_element_type=single)
    pre[...] = both[:, :HD]
    unit, _ = unit_of(both[:, :HD])
    key[...] = turned(unit * small[1:2], cosine[...], sine[...]).astype(bfloat)
    value[...] = both[:, HD:].astype(bfloat)


def project_query_kernel(normed, weights, cosine, sine, gains, query, pre, gate_act):
    both = jnp.dot(normed[...], weights[:, 0 : 4 * HD], preferred_element_type=single)
    for head in range(2):
        columns = slice(head * HD, (head + 1) * HD)
        pre[:, columns] = both[:, columns]
        unit, _ = unit_of(both[:, columns])
        query[:, columns] = turned(unit * gains[0:1], cosine[...], sine[...]).astype(bfloat)
    gate_act[...] = jax.nn.sigmoid(both[:, 2 * HD : 4 * HD])


VMEM = pl.BlockSpec(memory_space=pltpu.VMEM)
SMEM = pl.BlockSpec(memory_space=pltpu.SMEM)
ANY = pl.BlockSpec(memory_space=pl.ANY)
HBM = pl.BlockSpec(memory_space=pltpu.HBM)


def shaped(dtype, *shape):
    return jax.ShapeDtypeStruct(shape, dtype)


def arrange(info, own, other):
    return pl.pallas_call(
        arrange_kernel,
        out_shape=shaped(own.dtype, 512, own.shape[1]),
        in_specs=[SMEM, VMEM, VMEM],
        out_specs=VMEM,
        cost_estimate=pl.CostEstimate(flops=0, bytes_accessed=4 * 2**20, transcendentals=0),
        name="arrange",
    )(info, own, other)


def pack(side, key, value, query, gate, out, gains):
    shards = [key, value, query, gate, out]

    def kernel(side_ref, gains, *refs):
        (own, sent), held, sems = refs[5:7], refs[7:12], refs[12]
        for copy in bring(list(zip(refs[:5], held)), sems):
            copy.wait()
        key, value, query, gate, out = held
        for target, zh in ((own, side_ref[0]), (sent, 1 - side_ref[0])):
            narrow = pl.ds(pl.multiple_of(zh * HD, HD), HD)
            wide = pl.ds(pl.multiple_of(zh * 2 * HD, HD), 2 * HD)
            target[:, 0:HD] = key[:, narrow]
            target[:, HD : 2 * HD] = gains[:, 0:HD]
            target[:, 2 * HD : 3 * HD] = value[:, narrow]
            target[:, 3 * HD : 4 * HD] = gains[:, HD : 2 * HD]
            target[:, 4 * HD : 6 * HD] = query[:, wide]
            target[:, 6 * HD : 8 * HD] = gate[:, wide]
            target[:, 8 * HD : 10 * HD] = out[:, wide]

    return pl.pallas_call(
        kernel,
        out_shape=(shaped(bfloat, 64, 10 * HD), shaped(bfloat, 64, 10 * HD)),
        in_specs=[SMEM, VMEM] + [HBM] * 5,
        out_specs=(VMEM, VMEM),
        scratch_shapes=[pltpu.VMEM(shard.shape, bfloat) for shard in shards]
        + [pltpu.SemaphoreType.DMA((5,))],
        compiler_params=pltpu.CompilerParams(vmem_limit_bytes=4 * 2**20),
        cost_estimate=pl.CostEstimate(flops=0, bytes_accessed=2**20, transcendentals=0),
        name="pack",
    )(side, gains, *in_hbm(shards))


def project_pairs(info, own, other, cosine, sine, pieces):
    width = own.shape[1]
    return pl.pallas_call(
        project_pairs_kernel,
        out_shape=(
            shaped(bfloat, 512, width),
            shaped(bfloat, 512, HD),
            shaped(bfloat, 512, HD),
            shaped(single, 512, HD),
            shaped(bfloat, width, 2 * HD),
            shaped(single, 8, width),
            shaped(single, 8, HD),
        ),
        in_specs=[SMEM] + [VMEM] * 2 + [HBM] * 10,
        out_specs=[VMEM] * 7,
        scratch_shapes=[
            pltpu.VMEM((width, 2 * HD), bfloat),
            pltpu.VMEM((8, 4, HD, 2 * HD), bfloat),
            pltpu.VMEM((BLOCK, width), bfloat),
            pltpu.VMEM((BLOCK, width), bfloat),
            pltpu.SemaphoreType.DMA((10,)),
        ],
        compiler_params=pltpu.CompilerParams(vmem_limit_bytes=16 * 2**20),
        cost_estimate=pl.CostEstimate(
            flops=2**30, bytes_accessed=8 * 2**20, transcendentals=2**10
        ),
        name="project_pairs",
    )(info, cosine, sine, *in_hbm([own, other, *pieces[0], *pieces[1]]))


def project_query(normed, weights, cosine, sine, gains):
    return pl.pallas_call(
        project_query_kernel,
        out_shape=(
            shaped(bfloat, 512, 2 * HD),
            shaped(single, 512, 2 * HD),
            shaped(single, 512, 2 * HD),
        ),
        in_specs=[VMEM] * 5,
        out_specs=[VMEM] * 3,
        compiler_params=pltpu.CompilerParams(vmem_limit_bytes=12 * 2**20),
        cost_estimate=pl.CostEstimate(
            flops=2**30, bytes_accessed=8 * 2**20, transcendentals=2**17
        ),
        name="project_query",
    )(normed, weights, cosine, sine, gains)


def attend(info, home, query, pieces):
    return pl.pallas_call(
        attend_kernel,
        out_shape=(shaped(single, 512, 2 * HD), shaped(single, 2, 1, 512)),
        in_specs=[SMEM, SMEM] + [HBM] * 11,
        out_specs=(VMEM, VMEM),
        scratch_shapes=[
            pltpu.VMEM((512, 2 * HD), bfloat),
            pltpu.VMEM((4, 4, 512, HD), bfloat),
            pltpu.VMEM((4, 4, 512, HD), bfloat),
            pltpu.SMEM((32,), jnp.int32),
            pltpu.VMEM((HD, 512), single),
            pltpu.VMEM((8, 512), single),
            pltpu.SemaphoreType.DMA((11,)),
        ],
        compiler_params=pltpu.CompilerParams(vmem_limit_bytes=12 * 2**20),
        cost_estimate=pl.CostEstimate(
            flops=4 * 2**30, bytes_accessed=6 * 2**20, transcendentals=4 * 2**20
        ),
        name="attend",
    )(info, home, *in_hbm([query, *pieces[0], *pieces[1]]))


def attend_back(info, home, query, d_out, out, logs, pre, cosine, sine, gains, pieces):
    outs = pl.pallas_call(
        attend_back_kernel,
        out_shape=[shaped(bfloat, 512, 2 * HD), shaped(single, 1, HD)]
        + [pltpu.HBM((count, 512, HD), bfloat) for count in (4, 4, 2, 2, 4)] * 2,
        in_specs=[SMEM, SMEM, VMEM, VMEM] + [HBM] * 16,
        out_specs=[VMEM] * 12,
        scratch_shapes=[
            pltpu.VMEM((512, 2 * HD), bfloat),
            pltpu.VMEM((512, 2 * HD), bfloat),
            pltpu.VMEM((512, 2 * HD), single),
            pltpu.VMEM((512, 2 * HD), single),
            pltpu.VMEM((512, HD), single),
            pltpu.VMEM((512, HD), single),
            pltpu.VMEM((4, 4, 512, HD), bfloat),
            pltpu.VMEM((4, 4, 512, HD), bfloat),
            pltpu.SMEM((32,), jnp.int32),
            pltpu.VMEM((16, 512, HD), single),
            pltpu.VMEM((16, 512, HD), single),
            pltpu.VMEM((HD, 512), single),
            pltpu.VMEM((512, 2 * HD), single),
            pltpu.SemaphoreType.DMA((16,)),
        ],
        compiler_params=pltpu.CompilerParams(vmem_limit_bytes=28 * 2**20),
        cost_estimate=pl.CostEstimate(
            flops=10 * 2**30, bytes_accessed=12 * 2**20, transcendentals=4 * 2**20
        ),
        name="attend_back",
    )(
        info,
        home,
        logs,
        gains,
        *in_hbm([query, d_out, out, pre, cosine, sine, *pieces[0], *pieces[1]]),
    )
    return outs[0], outs[1], outs[2:7], outs[7:12]


def plane_grads(lefts, rights, tile, rows=128, columns=None, into=None, extras=(), by_x=False):
    starts = []
    count = 0
    for _, right in rights:
        starts.append(count)
        count += right.shape[1] // tile
    spans = list(zip(starts, starts[1:] + [count]))
    depth, height = lefts[0].shape
    columns = columns or count * tile
    shift_by = 0 if into is None else columns // tile - count
    flips = {}
    for (number, _), start in zip(rights, starts):
        flips.setdefault(number, start)

    def kernel(*refs):
        left_refs, right_refs = refs[: len(lefts)], refs[len(lefts) : len(lefts) + len(rights)]
        extra_refs = refs[len(lefts) + len(rights) : len(lefts) + len(rights) + len(extras)]
        out, flipped = refs[-2:]
        step = pl.program_id(0)

        def flip(left):
            for group in range(8):
                side, y = group // 4, group % 4
                turned = jnp.transpose(left[:, group * 256 : group * 256 + 256])
                for x in range(4):
                    first = ((x * 4 + y if by_x else y * 4 + x) * 2 + side) * 64
                    flipped[first : first + 64, :] = turned[x * 64 : x * 64 + 64]

        def product(right):
            for one in range(4):
                left = flipped[one * 512 : one * 512 + 512, :]
                part = jnp.dot(left, right, preferred_element_type=single).astype(bfloat)
                out[one * 4 : one * 4 + 4, 0:128] = part.reshape(4, 128, tile)
            for number, ref in enumerate(extra_refs):
                out[:, 128:144, number * HD : (number + 1) * HD] = jnp.broadcast_to(
                    ref[...].astype(bfloat)[None], (16, 16, HD)
                )

        for number, start in flips.items():
            pl.when(step == start)(lambda number=number: flip(left_refs[number]))
        for ref, (start, stop) in zip(right_refs, spans):
            pl.when((step >= start) & (step < stop))(lambda ref=ref: product(ref[...]))

    def right_spec(start, stop):
        return pl.BlockSpec(
            (depth, tile), lambda i: (0, jnp.minimum(jnp.maximum(i - start, 0), stop - start - 1))
        )

    return pl.pallas_call(
        kernel,
        grid=(count,),
        in_specs=[
            pl.BlockSpec((depth, height), lambda i: (0, 0), pipeline_mode=pl.Buffered(1))
            for _ in lefts
        ]
        + [right_spec(*span) for span in spans]
        + [pl.BlockSpec((1, HD), lambda i: (0, 0)) for _ in extras]
        + ([] if into is None else [ANY]),
        out_specs=pl.BlockSpec((16, rows, tile), lambda i: (0, 0, i + shift_by)),
        out_shape=pltpu.HBM((16, rows, columns), bfloat),
        input_output_aliases={} if into is None else {len(lefts) + len(rights) + len(extras): 0},
        scratch_shapes=[pltpu.VMEM((height, depth), bfloat)],
        compiler_params=pltpu.CompilerParams(
            vmem_limit_bytes=18 * 2**20, dimension_semantics=("arbitrary",)
        ),
        cost_estimate=pl.CostEstimate(
            flops=2 * depth * height * count * tile,
            bytes_accessed=2 * (depth + height) * count * tile + 2 * depth * height,
            transcendentals=0,
        ),
        name="plane_grads",
    )(*lefts, *(right for _, right in rights), *extras, *([] if into is None else [into]))


def columns_of(weight, side, width):
    return lax.dynamic_slice_in_dim(weight, side * width, width, 1)


def rows_of(weight, side, width):
    return lax.dynamic_slice_in_dim(weight, side * width, width, 0)


def in_order(zh, own, other, axis):
    first = jnp.where(zh == 0, own, other)
    second = jnp.where(zh == 0, other, own)
    return jnp.concatenate([first, second], axis=axis)


def gather_plane(block):
    whole = lax.all_gather(block, PLANE, axis=1, tiled=True)
    return whole.reshape(-1, block.shape[-1])


def per_device(
    tokens,
    query_weight,
    key_weight,
    value_weight,
    gate_weight,
    out_weight,
    norm_gain,
    query_gain,
    key_gain,
    inner_gate,
    inner_lift,
    inner_down,
    inner_gain,
    out_grad,
    bucket_len,
    seq_len,
    home_block,
):
    zh = lax.axis_index("zh")
    zl = lax.axis_index("zl")
    c = lax.axis_index("c")
    mine = zl * 2 + c
    width = tokens.shape[1]
    seq_index = zh * 16 + lax.axis_index("y") * 4 + lax.axis_index("x")
    block_own = lax.dynamic_index_in_dim(home_block, seq_index, 0, keepdims=False)
    block_other = lax.dynamic_index_in_dim(home_block, seq_index ^ 16, 0, keepdims=False)
    info = jnp.stack(
        [
            block_own,
            block_other,
            zl,
            c,
            zh,
            bucket_len[0],
            seq_len[0],
            seq_len[1],
            lax.axis_index("y"),
            lax.axis_index("x"),
        ]
    ).astype(jnp.int32)

    lane = jnp.arange(HD, dtype=jnp.int32)

    def head_gain(vector):
        return jnp.where(lane // 4 == seq_index, jnp.tile(vector, 32), 0)

    norm_columns = jnp.pad(jnp.stack([norm_gain, inner_gain], axis=1), ((0, 0), (0, HD - 2)))
    head_rows = jnp.pad(
        jnp.stack([head_gain(query_gain), head_gain(key_gain)], axis=0), ((0, 62), (0, 0))
    ).astype(bfloat)

    def inner_pack(side):
        gate, lift, down = inner_shards
        return jnp.concatenate(
            [columns_of(gate, side, 768), columns_of(lift, side, 768), rows_of(down, side, 768).T],
            axis=1,
        )

    def pair_up(pack):
        own = pack(zh)
        other = swap(pack(1 - zh), "zh")
        return in_order(zh, own[None], other[None], 0)

    own_pack, sent_pack = pack(
        zh.astype(jnp.int32).reshape(1),
        key_weight,
        value_weight,
        query_weight,
        gate_weight,
        out_weight.T,
        jnp.concatenate([norm_columns, head_rows], axis=1),
    )
    first_block = in_order(zh, own_pack[None], swap(sent_pack, "zh")[None], 0)

    index = jnp.arange(512, dtype=jnp.int32)
    half_of = (index >> 7) & 1
    place = jnp.where(half_of == 0, block_own, block_other) * BLOCK + row_place(
        ((index >> 8) << 7) | (index & 127), zl, c
    )
    offset = jnp.where(place >= bucket_len[0], place - bucket_len[0], place)
    freq = jnp.power(THETA, -jnp.arange(HD // 2, dtype=single) * 2.0 / HD)
    angle = offset.astype(single)[:, None] * freq[None, :]
    cosine = jnp.cos(angle)
    sine = jnp.sin(angle)
    cosine = jnp.concatenate([cosine, cosine], axis=1)
    sine = jnp.concatenate([-sine, sine], axis=1)

    first_block, cosine, sine, info = lax.optimization_barrier((first_block, cosine, sine, info))
    tokens_other = swap(tokens, "zh")
    pairs_block, outer_block = first_block[:, :, : 4 * HD], first_block[:, :, 4 * HD :]
    outer = gather_plane(outer_block)
    pairs_wide = pairs_block.reshape(HD, 4 * HD)
    weight_pieces, _ = plane_gather(pairs_wide[:, : 2 * HD], pairs_wide[:, 2 * HD :], (), False)
    normed, key_rot, value, k_pre, w_pairs, gains, head_gains = project_pairs(
        info, tokens, tokens_other, cosine, sine, weight_pieces
    )
    key_rot, inner_shards = lax.optimization_barrier(
        (key_rot, (inner_gate, inner_lift, inner_down))
    )
    inner_block = pair_up(inner_pack)
    gain_norm, gain_inner = gains[0:1], gains[1:2]
    gain_query, gain_key = head_gains[0:1], head_gains[1:2]
    w_heads = outer[:, :512]
    w_out = outer[:, 512:]
    query, q_pre, gate_sig = project_query(normed, outer, cosine, sine, head_gains)
    pieces, (inner_block, out_grad_sent) = plane_gather(
        key_rot, value, (inner_block, out_grad), True
    )
    rows_grad = arrange(info, out_grad, swap(out_grad_sent, "zh"))
    inner = gather_plane(inner_block)
    w_gate_lift = inner[:, :1536]
    w_down = inner[:, 1536:]
    query, rows_grad = lax.optimization_barrier((query, rows_grad))
    attended, logs = attend(info, home_block, query, pieces)
    gated = (attended * gate_sig).astype(bfloat)

    def line_product(left, right):
        return line_sum(dot_nt(left[:256], right), dot_nt(left[256:], right))

    inputs = rows_of(tokens, mine, 64).astype(single)
    mixed_in = inputs + line_product(gated, w_out)
    unit_two, factor_two = rms_parts(mixed_in)
    normed_two = line_gather((unit_two * gain_inner).astype(bfloat))
    d_hidden = jnp.dot(rows_grad, w_down, preferred_element_type=single)
    gate_lift = jnp.dot(normed_two, w_gate_lift, preferred_element_type=single)
    gate_val = gate_lift[:, :768]
    lift_val = gate_lift[:, 768:]
    gate_act = jax.nn.sigmoid(gate_val)
    hidden = (gate_val * gate_act * lift_val).astype(bfloat)
    d_gate = (d_hidden * lift_val * gate_act * (1.0 + gate_val * (1.0 - gate_act))).astype(bfloat)
    d_lift = (d_hidden * gate_val * gate_act).astype(bfloat)
    d_gate_lift = jnp.concatenate([d_gate, d_lift], axis=1)

    def inner_grads(needs):
        return plane_grads(
            [normed_two, rows_grad],
            [(0, needs[0]), (0, needs[1]), (1, needs[2])],
            384,
        )

    d_normed_two, grad_inner = line_sum_end(
        line_sum_middle(dot_nt(d_gate_lift[:256], w_gate_lift), dot_nt(d_gate_lift[256:], w_gate_lift)),
        (inner_grads, (d_gate, d_lift, hidden)),
    )

    def scatter_plane(grad):
        part = lax.psum_scatter(grad, PLANE, scatter_dimension=0, tiled=False)
        return part.reshape(2, 64, -1)

    part = scatter_plane(grad_inner)
    d_mixed = rows_grad[:64].astype(single) + rms_back(
        d_normed_two, unit_two, factor_two, gain_inner
    )
    d_attn = line_gather(d_mixed.astype(bfloat))
    d_gated = jnp.dot(d_attn, w_out, preferred_element_type=single)
    d_attended = (d_gated * gate_sig).astype(bfloat)
    d_gate_pre = (d_gated * attended * gate_sig * (1.0 - gate_sig)).astype(bfloat)

    def rounded(rows):
        return lax.reduce_precision(rows, 8, 7).astype(bfloat)

    def both_sides(part):
        own = lax.dynamic_index_in_dim(part, zh, 0, keepdims=False).astype(single)
        sent = lax.dynamic_index_in_dim(part, 1 - zh, 0, keepdims=False).astype(bfloat)
        sent, part = lax.optimization_barrier((sent, part))
        return own, swap(sent, "zh").astype(single), part

    d_q_pre, query_gain_part, d_keys, d_values = attend_back(
        info,
        home_block,
        query,
        d_attended,
        attended,
        logs,
        q_pre,
        cosine,
        sine,
        head_gains,
        pieces,
    )
    grad_outer = plane_grads(
        [d_attn, normed], [(0, gated), (1, d_gate_pre), (1, d_q_pre)], 256, by_x=True
    )
    d_heads = jnp.concatenate([d_q_pre, d_gate_pre], axis=1)

    d_key, d_value, grad_outer, (normed_near, normed_far) = plane_sum(
        d_keys,
        d_values,
        grad_outer,
        (dot_nt(d_heads[:256], w_heads), dot_nt(d_heads[256:], w_heads)),
    )
    grad_outer, part = lax.optimization_barrier((grad_outer, part))
    rest = lax.psum_scatter(
        grad_outer.reshape(4, 4, 128, -1), "x", scatter_dimension=0, tiled=False
    )
    rest = lax.psum_scatter(rest, "y", scatter_dimension=0, tiled=False).reshape(2, 64, -1)
    k_unit, k_factor = rms_parts(k_pre)
    d_k_turned = d_key * cosine - jnp.roll(d_key, HD // 2, axis=1) * sine
    key_gain_part = jnp.sum(d_k_turned * k_unit, axis=0, keepdims=True)
    d_k_pre = rms_back(d_k_turned, k_unit, k_factor, gain_key).astype(bfloat)
    d_kv_pre = jnp.concatenate([d_k_pre, d_value.astype(bfloat)], axis=1)
    normed_far = (normed_far + dot_nt(d_kv_pre[256:], w_pairs)).astype(bfloat)
    normed_far, d_kv_pre = lax.optimization_barrier((normed_far, d_kv_pre))
    pairs_sent = plane_grads(
        [normed], [(0, d_kv_pre)], 256, rows=144, extras=(query_gain_part, key_gain_part)
    )
    pairs_sent, d_kv_pre = lax.optimization_barrier((pairs_sent, d_kv_pre))
    normed_near = normed_near + dot_nt(d_kv_pre[:256], w_pairs)
    pairs_got = lax.all_to_all(pairs_sent, PLANE, 0, 0, tiled=True)
    here, hidden = lax.optimization_barrier((line_sum_middle(normed_near, normed_far), hidden))
    d_normed = line_sum_end(here)
    result_rows = mixed_in + line_product(hidden, w_down)
    unit_in, factor_in = rms_parts(inputs)
    token_rows = d_mixed + rms_back(d_normed, unit_in, factor_in, gain_norm)

    part_own, part_got, part = both_sides(part)
    pairs_got, rest, token_rows, part_got = lax.optimization_barrier(
        (pairs_got, rest, token_rows, part_got)
    )
    pairs_sum = jnp.sum(pairs_got.astype(single), axis=0)
    result, (pairs_sum, part) = head_gather(rounded(result_rows), mine, (pairs_sum, part))
    gain_part = pairs_sum[128]
    pair_part = pairs_sum[:128].reshape(2, 64, 256)
    tokens_grad = head_gather(rounded(token_rows), mine)

    def weighted(block, part):
        return jnp.sum(block.astype(single) * part.astype(single), axis=2)

    norm_part = (
        weighted(outer_block[:, :, :256], rest[:, :, 512:])
        + weighted(outer_block[:, :, 256:512], rest[:, :, 256:512])
        + weighted(pairs_block[:, :, :HD], pair_part[:, :, :HD])
        + weighted(pairs_block[:, :, 2 * HD : 3 * HD], pair_part[:, :, HD:])
    ) / pairs_block[:, :, HD].astype(single)
    inner_gain_part = weighted(inner_block[:, :, :1536], part[:, :, :1536]) / pairs_block[
        :, :, HD + 1
    ].astype(single)
    gain_line = jnp.concatenate(
        [
            norm_part.reshape(HD),
            inner_gain_part.reshape(HD),
            gain_part,
        ]
    ).reshape(4, HD)
    gain_line = lax.reduce_precision(gain_line, 8, 7)
    last = jnp.concatenate([rest.astype(single), pair_part], axis=2)
    last_own = lax.dynamic_index_in_dim(last, zh, 0, keepdims=False)
    last_sent = lax.dynamic_index_in_dim(last, 1 - zh, 0, keepdims=False)
    last_got = swap(
        jnp.concatenate([last_sent, jnp.pad(gain_line, ((0, 60), (0, 0)))], axis=1).astype(bfloat),
        "zh",
    ).astype(single)
    gain_line = head_sum(gain_line + last_got[:4, 1024:])

    def shard(own, got, start, count):
        return in_order(zh, own[:, start : start + count], got[:, start : start + count], 1)

    shard_igate = shard(part_own, part_got, 0, 768)
    shard_ilift = shard(part_own, part_got, 768, 768)
    shard_idown = shard(part_own, part_got, 1536, 768).T
    shard_out = shard(last_own, last_got, 0, 256).T
    shard_gate = shard(last_own, last_got, 256, 256)
    shard_query = shard(last_own, last_got, 512, 256)
    shard_key = shard(last_own, last_got, 768, 128)
    shard_value = shard(last_own, last_got, 896, 128)

    gain_own = lax.dynamic_index_in_dim(gain_line[:2].reshape(2, 2, 64), zh, 1, keepdims=False)
    gain_sides = lax.dynamic_slice_in_dim(gain_line[2:], seq_index * 4, 4, 1)

    return (
        result,
        tokens_grad,
        shard_query,
        shard_key,
        shard_value,
        shard_gate,
        shard_out,
        gain_own[0],
        gain_sides[0],
        gain_sides[1],
        shard_igate,
        shard_ilift,
        shard_idown,
        gain_own[1],
    )


def solution(mesh):
    fine = Mesh(mesh.devices.reshape(2, 4, 4, 2, 2), ("zh", "y", "x", "zl", "c"))
    seq = ("zh", "y", "x")
    head = ("zl", "c")
    in_specs = (
        P(seq, None),
        P(seq, head),
        P(seq, head),
        P(seq, head),
        P(seq, head),
        P(head, seq),
        P(seq),
        P(seq),
        P(seq),
        P(seq, head),
        P(seq, head),
        P(head, seq),
        P(seq),
        P(seq, None),
        P(),
        P(),
        P(),
    )
    out_specs = (
        P(seq, None),
        P(seq, None),
        P(seq, head),
        P(seq, head),
        P(seq, head),
        P(seq, head),
        P(head, seq),
        P(seq),
        P(seq),
        P(seq),
        P(seq, head),
        P(seq, head),
        P(head, seq),
        P(seq),
    )
    return jax.shard_map(
        per_device, mesh=fine, in_specs=in_specs, out_specs=out_specs, check_vma=False
    )
```

```python
import jax
import jax.numpy as jnp
from jax import lax
from jax.experimental import pallas as pl
from jax.experimental.pallas import tpu as pltpu
from jax.sharding import Mesh
from jax.sharding import PartitionSpec as P

HD = 128
BLOCK = 256
EPS = 1e-06
THETA = 1000000.0
LOG2E = 1.4426950408889634
SCALE = HD ** (-0.5)
PLANE = ("y", "x")
bfloat = jnp.bfloat16
single = jnp.float32


def rms_parts(value):
    factor = lax.rsqrt(jnp.mean(value * value, axis=-1, keepdims=True) + EPS)
    return (value * factor, factor)


def rms_back(grad, unit_val, factor, gain):
    scaled = grad * gain
    return factor * (scaled - unit_val * jnp.mean(unit_val * scaled, axis=-1, keepdims=True))


def swap(value, axis):
    return lax.ppermute(value, axis, [(0, 1), (1, 0)])


def swap_both(value):
    return lax.ppermute(value, ("zh", "zl"), [(0, 3), (1, 2), (2, 1), (3, 0)])


def line_sum(near, far):
    return line_sum_end(line_sum_middle(near, far))


def line_sum_middle(near, far):
    return near + swap(far.astype(bfloat), "c").astype(single)


def line_sum_end(here, beside=None):
    made = None
    if beside is not None:
        here, needs = lax.optimization_barrier((here, beside[1]))
        made = beside[0](needs)
    sent = here.astype(bfloat)
    got = (swap(sent[64:128], "zl"), swap(sent[128:192], "zh"), swap_both(sent[192:256]))
    if beside is not None:
        got, made = lax.optimization_barrier((got, made))
    one, two, three = (piece.astype(single) for piece in got)
    total = (here[:64] + one) + (two + three)
    return total if beside is None else (total, made)


def shift(value, axis, step):
    return lax.ppermute(value, axis, [(i, (i + step) % 4) for i in range(4)])


def plane_gather(one, two, later, ring):
    got = [
        [shift(value, axis, -step) for step in range(1, 4)]
        for value, axis in ((one, "x"), (two, "y"))
    ]
    got, later = lax.optimization_barrier((got, later))
    lines = [jnp.stack([v] + parts, axis=0) for v, parts in zip((one, two), got)]
    if not ring:
        pieces = [
            [line] + [shift(line, axis, -step) for step in range(1, 4)]
            for line, axis in zip(lines, ("y", "x"))
        ]
        return pieces, later
    next_to = [(shift(line, axis, -1), shift(line, axis, 1)) for line, axis in zip(lines, ("y", "x"))]
    return [
        [line, up, shift(up[:2], axis, -1), shift(down[2:], axis, 1), down]
        for line, (up, down), axis in zip(lines, next_to, ("y", "x"))
    ], later


def add_halves(groups):
    def kernel(*refs):
        for number in range(len(groups)):
            one, up, four, down = refs[4 * number : 4 * number + 4]
            first, second = refs[4 * len(groups) + 2 * number : 4 * len(groups) + 2 * number + 2]
            first[0:2] = (one[0:2].astype(single) + up[...].astype(single)).astype(bfloat)
            first[2:4] = one[2:4]
            second[0:2] = four[0:2]
            second[2:4] = (four[2:4].astype(single) + down[...].astype(single)).astype(bfloat)

    outs = pl.pallas_call(
        kernel,
        out_shape=[
            shaped(bfloat, *one.shape) for one, _, _, _ in groups for _ in range(2)
        ],
        in_specs=[VMEM] * (4 * len(groups)),
        out_specs=[VMEM] * (2 * len(groups)),
        compiler_params=pltpu.CompilerParams(vmem_limit_bytes=8 * 2**20),
        cost_estimate=pl.CostEstimate(flops=2**20, bytes_accessed=5 * 2**20, transcendentals=0),
        name="add_halves",
    )(*(part for group in groups for part in group))
    return [tuple(outs[2 * i : 2 * i + 2]) for i in range(len(groups))]


def plane_sum(one, two, first, second):
    both = list(zip((one, two), ("x", "y")))
    across = [(shift(v[2], axis, 1), shift(v[3], axis, -1)) for v, axis in both]
    across, first = lax.optimization_barrier((across, first))
    sent = add_halves([(v[1], up, v[4], down) for (v, _), (up, down) in zip(both, across)])
    got = [(shift(up, axis, 1), shift(down, axis, -1)) for (_, axis), (up, down) in zip(both, sent)]
    got = lax.optimization_barrier(got)
    sums = [
        v[0].astype(single) + (up.astype(single) + down.astype(single))
        for (v, _), (up, down) in zip(both, got)
    ]
    got = [
        [shift(v[step].astype(bfloat), axis, step) for step in range(1, 4)]
        for v, axis in zip(sums, ("y", "x"))
    ]
    got, second = lax.optimization_barrier((got, second))
    sums = [
        (v[0] + parts[0].astype(single)) + (parts[1].astype(single) + parts[2].astype(single))
        for v, parts in zip(sums, got)
    ]
    return sums[0], sums[1], first, second


def line_gather(own):
    near = jnp.concatenate([own, swap(own, "zl"), swap(own, "zh"), swap_both(own)], axis=0)
    return jnp.concatenate([near, swap(near, "c")], axis=0)


def head_sum(value):
    across = lax.ppermute(value, ("zl", "c"), [(0, 3), (1, 2), (2, 1), (3, 0)])
    return (value + swap(value, "c")) + (swap(value, "zl") + across)


def head_gather(own, mine, later=None):
    near = jnp.concatenate([own, swap(own, "zl")], axis=0)
    if later is not None:
        near, later = lax.optimization_barrier((near, later))
    parts = jnp.concatenate([near, swap(near, "c")], axis=0).reshape(4, 64, -1)
    rows = []
    for place in range(4):
        other = place ^ mine
        slot = (other & 1) * 2 + (other >> 1)
        rows.append(lax.dynamic_index_in_dim(parts, slot, 0, keepdims=False))
    rows = jnp.concatenate(rows, axis=0).astype(single)
    return rows if later is None else (rows, later)


def row_place(index, zl, c):
    core = (index >> 7) & 1
    low = (index >> 6) & 1
    return ((low ^ zl) * 2 + (core ^ c)) * 64 + (index & 63)


def block_range(block, cut, ends):
    first = block * BLOCK
    last = first + BLOCK - 1
    low_least = jnp.where(first >= cut, cut, 0)
    low_most = jnp.where(last >= cut, cut, 0)
    high_least = jnp.minimum(first, jnp.where(first >= cut, ends[1], ends[0]))
    start = low_least // BLOCK
    whole = jnp.minimum((low_most + BLOCK - 1) // BLOCK, block + 1)
    whole_end = jnp.maximum((high_least + 1) // BLOCK, whole)
    return start, whole, whole_end, block + 1


def stacked(ref, half):
    near = half * 128
    return jnp.concatenate(
        [
            ref[near : near + 128, 0:HD],
            ref[256 + near : 384 + near, 0:HD],
            ref[near : near + 128, HD : 2 * HD],
            ref[256 + near : 384 + near, HD : 2 * HD],
        ],
        axis=0,
    )


def unstack(ref, half, value):
    near = half * 128
    ref[near : near + 128, 0:HD] = value[0:128]
    ref[256 + near : 384 + near, 0:HD] = value[128:256]
    ref[near : near + 128, HD : 2 * HD] = value[256:384]
    ref[256 + near : 384 + near, HD : 2 * HD] = value[384:512]


def key_rows(ref, one, two, half):
    near = pl.multiple_of(half * 128, 128)
    far = pl.multiple_of(256 + half * 128, 128)
    return jnp.concatenate(
        [ref[one, two, pl.ds(near, 128), :], ref[one, two, pl.ds(far, 128), :]], axis=0
    )


def find_slot(info, where, block):
    slot = where[block]
    down = ((slot >> 2) - info[8]) & 3
    across = (slot - info[9]) & 3
    return down, across, (slot >> 4) ^ info[4]


def bring(pairs, sems):
    copies = [pltpu.make_async_copy(*pair, sems.at[i]) for i, pair in enumerate(pairs)]
    for copy in copies:
        copy.start()
    return copies


def ring_targets(buffer):
    return [
        buffer.at[0],
        buffer.at[1],
        buffer.at[2, pl.ds(0, 2)],
        buffer.at[2, pl.ds(2, 2)],
        buffer.at[3],
    ]


def in_hbm(values):
    return [pltpu.with_memory_space_constraint(value, pltpu.HBM) for value in values]


def turned(value, cosine, sine):
    return value * cosine + pltpu.roll(value, HD // 2, 1) * sine


def unit_of(value):
    factor = lax.rsqrt(jnp.mean(value * value, axis=-1, keepdims=True) + EPS)
    return value * factor, factor


def dot_nt(left, right):
    return lax.dot_general(left, right, (((1,), (1,)), ((), ())), preferred_element_type=single)


def dot_tn(left, right):
    return lax.dot_general(left, right, (((0,), (0,)), ((), ())), preferred_element_type=single)


def find_blocks(home, where):
    for slot in range(32):
        where[home[slot]] = slot


def tile_limits(info, half):
    zl, c, cut = info[2], info[3], info[5]
    ends = (info[6] - 1, cut + info[7] - 1)
    block = info[half]
    place = block * BLOCK + row_place(lax.broadcasted_iota(jnp.int32, (1, 512), 1), zl, c)
    second = place >= cut
    low = jnp.where(second, cut, 0)
    high = jnp.minimum(place, jnp.where(second, ends[1], ends[0]))
    return low, high, block_range(block, cut, ends)


def over_blocks(limits, step):
    start, whole, whole_end, stop = limits
    many = (whole_end - whole) // 4
    lax.fori_loop(start, whole, lambda block, _: step(block, 1, True), None)
    lax.fori_loop(0, many, lambda i, _: step(whole + 4 * i, 4, False), None)
    lax.fori_loop(whole + 4 * many, whole_end, lambda block, _: step(block, 1, False), None)
    lax.fori_loop(whole_end, stop, lambda block, _: step(block, 1, True), None)


def together(parts):
    return parts[0] if len(parts) == 1 else jnp.concatenate(parts, axis=0)


def attend_kernel(info, home, *refs):
    ins, (out, logs) = refs[:11], refs[11:13]
    query, keys, values, where, accum, total, sems = refs[13:]
    copies = bring(
        list(zip(ins, [query] + ring_targets(keys) + ring_targets(values))), sems
    )
    find_blocks(home, where)
    for copy in copies:
        copy.wait()
    key_place = row_place(lax.broadcasted_iota(jnp.int32, (256, 512), 0), info[2], info[3])
    for half in range(2):
        low, high, limits = tile_limits(info, half)
        rows = stacked(query, half)
        accum[...] = jnp.zeros_like(accum)
        total[...] = jnp.zeros_like(total)

        def step(block, count, masked):
            slots = [find_slot(info, where, block + i) for i in range(count)]
            key = together([key_rows(keys, down, across, side) for down, across, side in slots])
            value = together([key_rows(values, across, down, side) for down, across, side in slots])
            weight = jnp.exp2(dot_nt(key, rows) * (SCALE * LOG2E))
            if masked:
                place = key_place + block * BLOCK
                weight = jnp.where((place >= low) & (place <= high), weight, 0.0)
            total[...] += jnp.sum(weight.reshape(-1, 8, 512), axis=0)
            accum[...] += dot_tn(value, weight.astype(bfloat))

        over_blocks(limits, step)
        weights = jnp.sum(total[...], axis=0, keepdims=True)
        logs[half] = jnp.log2(weights)
        unstack(out, half, jnp.transpose(accum[...] / weights))


def attend_back_kernel(info, home, logs, gains, *refs):
    ins, (d_pre, gain_grad) = refs[:16], refs[16:18]
    d_keys, d_values = refs[18:23], refs[23:28]
    query, d_out, out, pre, cosine, sine, keys, values = refs[28:36]
    where, key_sum, value_sum, d_rows, d_query, sems = refs[36:]
    targets = [query, d_out, out, pre, cosine, sine] + ring_targets(keys) + ring_targets(values)
    copies = bring(list(zip(ins, targets)), sems)
    find_blocks(home, where)
    key_place = row_place(lax.broadcasted_iota(jnp.int32, (256, 512), 0), info[2], info[3])

    def clear(index, _):
        for accum in (key_sum, value_sum):
            accum[index] = jnp.zeros(accum.shape[1:], single)

    lax.fori_loop(0, 16, clear, None)
    for copy in copies:
        copy.wait()
    for half in range(2):
        low, high, limits = tile_limits(info, half)
        rows = stacked(query, half)
        grads = stacked(d_out, half)
        delta = jnp.sum(
            jnp.transpose(grads.astype(single) * stacked(out, half)), axis=0, keepdims=True
        )
        log = logs[half]
        d_rows[...] = jnp.zeros_like(d_rows)

        def step(block, count, masked):
            slots = [find_slot(info, where, block + i) for i in range(count)]
            key = together([key_rows(keys, down, across, side) for down, across, side in slots])
            value = together([key_rows(values, across, down, side) for down, across, side in slots])
            prob = jnp.exp2(dot_nt(key, rows) * (SCALE * LOG2E) - log)
            if masked:
                place = key_place + block * BLOCK
                prob = jnp.where((place >= low) & (place <= high), prob, 0.0)
            d_score = (prob * (dot_nt(value, grads) - delta)).astype(bfloat)
            d_value = jnp.dot(prob.astype(bfloat), grads, preferred_element_type=single)
            d_key = jnp.dot(d_score, rows, preferred_element_type=single)
            d_rows[...] += dot_tn(key, d_score)
            for i, (down, across, side) in enumerate(slots):
                near = pl.multiple_of(side * 128, 128)
                far = pl.multiple_of(256 + side * 128, 128)
                for accum, slot, grad in (
                    (key_sum, across * 4 + down, d_key),
                    (value_sum, down * 4 + across, d_value),
                ):
                    accum[slot, pl.ds(near, 128), :] += grad[i * 256 : i * 256 + 128]
                    accum[slot, pl.ds(far, 128), :] += grad[i * 256 + 128 : i * 256 + 256]

        over_blocks(limits, step)
        unstack(d_query, half, jnp.transpose(d_rows[...]) * SCALE)
    for one in range(4):
        for two in range(4):
            number, place = (one, two) if one < 2 else (4, two) if one == 3 else (2 + two // 2, two % 2)
            d_keys[number][place] = (key_sum[one * 4 + two] * SCALE).astype(bfloat)
            d_values[number][place] = value_sum[one * 4 + two].astype(bfloat)
    gain = gains[0:1]
    total = jnp.zeros((1, HD), single)
    for head in range(2):
        columns = slice(head * HD, (head + 1) * HD)
        d_turned = turned(d_query[:, columns], cosine[...], -sine[...])
        unit, factor = unit_of(pre[:, columns])
        total += jnp.sum(d_turned * unit, axis=0, keepdims=True)
        d_pre[:, columns] = rms_back(d_turned, unit, factor, gain).astype(bfloat)
    gain_grad[...] = total


def line_order(info):
    for core in range(2):
        for source in range(2):
            for low in range(2):
                there = ((low ^ info[2]) * 2 + (core ^ info[3])) * 64
                yield core * 4 + source * 2 + low, source, pl.multiple_of(there, 64)


def arrange_kernel(info, own, other, out):
    for place, source, there in line_order(info):
        out[place * 64 : place * 64 + 64, :] = (own, other)[source][pl.ds(there, 64), :]


def project_pairs_kernel(info, cosine, sine, *refs):
    normed, key, value, pre, weights, gains, small, extra, came, own, other, sems = refs[10:]
    copies = bring(list(zip(refs[:10], [own, other] + [came.at[i] for i in range(8)])), sems)
    for copy in copies:
        copy.wait()
    for one in range(4):
        for two in range(4):
            for number, y, x, column in ((one, one, two, 0), (4 + one, two, one, HD)):
                plane = ((y + info[8]) & 3) * 4 + ((x + info[9]) & 3)
                for side in range(2):
                    to = pl.ds(pl.multiple_of(side * 1024 + plane * 64, 64), 64)
                    block = came[number, two, side * 64 : side * 64 + 64, :]
                    weights[to, column : column + HD] = block[:, :HD]
                    extra[to, column : column + HD] = block[:, HD:]
    gains[...] = jnp.transpose(extra[:, 0:HD].astype(single))[0:8]
    total = jnp.zeros((16, HD), single)
    for block in range(32):
        total += extra[block * 64 : block * 64 + 16, HD : 2 * HD].astype(single)
    small[...] = total[0:8]
    gain = gains[0:1]
    for place, source, there in line_order(info):
        unit, _ = unit_of((own, other)[source][pl.ds(there, 64), :].astype(single))
        normed[place * 64 : place * 64 + 64, :] = (unit * gain).astype(bfloat)
    both = jnp.dot(normed[...], weights[...], preferred_element_type=single)
    pre[...] = both[:, :HD]
    unit, _ = unit_of(both[:, :HD])
    key[...] = turned(unit * small[1:2], cosine[...], sine[...]).astype(bfloat)
    value[...] = both[:, HD:].astype(bfloat)


def project_query_kernel(normed, weights, cosine, sine, gains, query, pre, gate_act):
    both = jnp.dot(normed[...], weights[:, 0 : 4 * HD], preferred_element_type=single)
    for head in range(2):
        columns = slice(head * HD, (head + 1) * HD)
        pre[:, columns] = both[:, columns]
        unit, _ = unit_of(both[:, columns])
        query[:, columns] = turned(unit * gains[0:1], cosine[...], sine[...]).astype(bfloat)
    gate_act[...] = jax.nn.sigmoid(both[:, 2 * HD : 4 * HD])


VMEM = pl.BlockSpec(memory_space=pltpu.VMEM)
SMEM = pl.BlockSpec(memory_space=pltpu.SMEM)
ANY = pl.BlockSpec(memory_space=pl.ANY)
HBM = pl.BlockSpec(memory_space=pltpu.HBM)


def shaped(dtype, *shape):
    return jax.ShapeDtypeStruct(shape, dtype)


def arrange(info, own, other):
    return pl.pallas_call(
        arrange_kernel,
        out_shape=shaped(own.dtype, 512, own.shape[1]),
        in_specs=[SMEM, VMEM, VMEM],
        out_specs=VMEM,
        cost_estimate=pl.CostEstimate(flops=0, bytes_accessed=4 * 2**20, transcendentals=0),
        name="arrange",
    )(info, own, other)


def pack(side, key, value, query, gate, out, gains):
    shards = [key, value, query, gate, out]

    def kernel(side_ref, gains, *refs):
        (own, sent), held, sems = refs[5:7], refs[7:12], refs[12]
        for copy in bring(list(zip(refs[:5], held)), sems):
            copy.wait()
        key, value, query, gate, out = held
        for target, zh in ((own, side_ref[0]), (sent, 1 - side_ref[0])):
            narrow = pl.ds(pl.multiple_of(zh * HD, HD), HD)
            wide = pl.ds(pl.multiple_of(zh * 2 * HD, HD), 2 * HD)
            target[:, 0:HD] = key[:, narrow]
            target[:, HD : 2 * HD] = gains[:, 0:HD]
            target[:, 2 * HD : 3 * HD] = value[:, narrow]
            target[:, 3 * HD : 4 * HD] = gains[:, HD : 2 * HD]
            target[:, 4 * HD : 6 * HD] = query[:, wide]
            target[:, 6 * HD : 8 * HD] = gate[:, wide]
            target[:, 8 * HD : 10 * HD] = out[:, wide]

    return pl.pallas_call(
        kernel,
        out_shape=(shaped(bfloat, 64, 10 * HD), shaped(bfloat, 64, 10 * HD)),
        in_specs=[SMEM, VMEM] + [HBM] * 5,
        out_specs=(VMEM, VMEM),
        scratch_shapes=[pltpu.VMEM(shard.shape, bfloat) for shard in shards]
        + [pltpu.SemaphoreType.DMA((5,))],
        compiler_params=pltpu.CompilerParams(vmem_limit_bytes=4 * 2**20),
        cost_estimate=pl.CostEstimate(flops=0, bytes_accessed=2**20, transcendentals=0),
        name="pack",
    )(side, gains, *in_hbm(shards))


def project_pairs(info, own, other, cosine, sine, pieces):
    width = own.shape[1]
    return pl.pallas_call(
        project_pairs_kernel,
        out_shape=(
            shaped(bfloat, 512, width),
            shaped(bfloat, 512, HD),
            shaped(bfloat, 512, HD),
            shaped(single, 512, HD),
            shaped(bfloat, width, 2 * HD),
            shaped(single, 8, width),
            shaped(single, 8, HD),
        ),
        in_specs=[SMEM] + [VMEM] * 2 + [HBM] * 10,
        out_specs=[VMEM] * 7,
        scratch_shapes=[
            pltpu.VMEM((width, 2 * HD), bfloat),
            pltpu.VMEM((8, 4, HD, 2 * HD), bfloat),
            pltpu.VMEM((BLOCK, width), bfloat),
            pltpu.VMEM((BLOCK, width), bfloat),
            pltpu.SemaphoreType.DMA((10,)),
        ],
        compiler_params=pltpu.CompilerParams(vmem_limit_bytes=16 * 2**20),
        cost_estimate=pl.CostEstimate(
            flops=2**30, bytes_accessed=8 * 2**20, transcendentals=2**10
        ),
        name="project_pairs",
    )(info, cosine, sine, *in_hbm([own, other, *pieces[0], *pieces[1]]))


def project_query(normed, weights, cosine, sine, gains):
    return pl.pallas_call(
        project_query_kernel,
        out_shape=(
            shaped(bfloat, 512, 2 * HD),
            shaped(single, 512, 2 * HD),
            shaped(single, 512, 2 * HD),
        ),
        in_specs=[VMEM] * 5,
        out_specs=[VMEM] * 3,
        compiler_params=pltpu.CompilerParams(vmem_limit_bytes=12 * 2**20),
        cost_estimate=pl.CostEstimate(
            flops=2**30, bytes_accessed=8 * 2**20, transcendentals=2**17
        ),
        name="project_query",
    )(normed, weights, cosine, sine, gains)


def attend(info, home, query, pieces):
    return pl.pallas_call(
        attend_kernel,
        out_shape=(shaped(single, 512, 2 * HD), shaped(single, 2, 1, 512)),
        in_specs=[SMEM, SMEM] + [HBM] * 11,
        out_specs=(VMEM, VMEM),
        scratch_shapes=[
            pltpu.VMEM((512, 2 * HD), bfloat),
            pltpu.VMEM((4, 4, 512, HD), bfloat),
            pltpu.VMEM((4, 4, 512, HD), bfloat),
            pltpu.SMEM((32,), jnp.int32),
            pltpu.VMEM((HD, 512), single),
            pltpu.VMEM((8, 512), single),
            pltpu.SemaphoreType.DMA((11,)),
        ],
        compiler_params=pltpu.CompilerParams(vmem_limit_bytes=12 * 2**20),
        cost_estimate=pl.CostEstimate(
            flops=4 * 2**30, bytes_accessed=6 * 2**20, transcendentals=4 * 2**20
        ),
        name="attend",
    )(info, home, *in_hbm([query, *pieces[0], *pieces[1]]))


def attend_back(info, home, query, d_out, out, logs, pre, cosine, sine, gains, pieces):
    outs = pl.pallas_call(
        attend_back_kernel,
        out_shape=[shaped(bfloat, 512, 2 * HD), shaped(single, 1, HD)]
        + [pltpu.HBM((count, 512, HD), bfloat) for count in (4, 4, 2, 2, 4)] * 2,
        in_specs=[SMEM, SMEM, VMEM, VMEM] + [HBM] * 16,
        out_specs=[VMEM] * 12,
        scratch_shapes=[
            pltpu.VMEM((512, 2 * HD), bfloat),
            pltpu.VMEM((512, 2 * HD), bfloat),
            pltpu.VMEM((512, 2 * HD), single),
            pltpu.VMEM((512, 2 * HD), single),
            pltpu.VMEM((512, HD), single),
            pltpu.VMEM((512, HD), single),
            pltpu.VMEM((4, 4, 512, HD), bfloat),
            pltpu.VMEM((4, 4, 512, HD), bfloat),
            pltpu.SMEM((32,), jnp.int32),
            pltpu.VMEM((16, 512, HD), single),
            pltpu.VMEM((16, 512, HD), single),
            pltpu.VMEM((HD, 512), single),
            pltpu.VMEM((512, 2 * HD), single),
            pltpu.SemaphoreType.DMA((16,)),
        ],
        compiler_params=pltpu.CompilerParams(vmem_limit_bytes=28 * 2**20),
        cost_estimate=pl.CostEstimate(
            flops=10 * 2**30, bytes_accessed=12 * 2**20, transcendentals=4 * 2**20
        ),
        name="attend_back",
    )(
        info,
        home,
        logs,
        gains,
        *in_hbm([query, d_out, out, pre, cosine, sine, *pieces[0], *pieces[1]]),
    )
    return outs[0], outs[1], outs[2:7], outs[7:12]


def plane_grads(lefts, rights, tile, rows=128, columns=None, into=None, extras=(), by_x=False):
    starts = []
    count = 0
    for _, right in rights:
        starts.append(count)
        count += right.shape[1] // tile
    spans = list(zip(starts, starts[1:] + [count]))
    depth, height = lefts[0].shape
    columns = columns or count * tile
    shift_by = 0 if into is None else columns // tile - count
    flips = {}
    for (number, _), start in zip(rights, starts):
        flips.setdefault(number, start)

    def kernel(*refs):
        left_refs, right_refs = refs[: len(lefts)], refs[len(lefts) : len(lefts) + len(rights)]
        extra_refs = refs[len(lefts) + len(rights) : len(lefts) + len(rights) + len(extras)]
        out, flipped = refs[-2:]
        step = pl.program_id(0)

        def flip(left):
            for group in range(8):
                side, y = group // 4, group % 4
                turned = jnp.transpose(left[:, group * 256 : group * 256 + 256])
                for x in range(4):
                    first = ((x * 4 + y if by_x else y * 4 + x) * 2 + side) * 64
                    flipped[first : first + 64, :] = turned[x * 64 : x * 64 + 64]

        def product(right):
            for one in range(4):
                left = flipped[one * 512 : one * 512 + 512, :]
                part = jnp.dot(left, right, preferred_element_type=single).astype(bfloat)
                out[one * 4 : one * 4 + 4, 0:128] = part.reshape(4, 128, tile)
            for number, ref in enumerate(extra_refs):
                out[:, 128:144, number * HD : (number + 1) * HD] = jnp.broadcast_to(
                    ref[...].astype(bfloat)[None], (16, 16, HD)
                )

        for number, start in flips.items():
            pl.when(step == start)(lambda number=number: flip(left_refs[number]))
        for ref, (start, stop) in zip(right_refs, spans):
            pl.when((step >= start) & (step < stop))(lambda ref=ref: product(ref[...]))

    def right_spec(start, stop):
        return pl.BlockSpec(
            (depth, tile), lambda i: (0, jnp.minimum(jnp.maximum(i - start, 0), stop - start - 1))
        )

    return pl.pallas_call(
        kernel,
        grid=(count,),
        in_specs=[
            pl.BlockSpec((depth, height), lambda i: (0, 0), pipeline_mode=pl.Buffered(1))
            for _ in lefts
        ]
        + [right_spec(*span) for span in spans]
        + [pl.BlockSpec((1, HD), lambda i: (0, 0)) for _ in extras]
        + ([] if into is None else [ANY]),
        out_specs=pl.BlockSpec((16, rows, tile), lambda i: (0, 0, i + shift_by)),
        out_shape=pltpu.HBM((16, rows, columns), bfloat),
        input_output_aliases={} if into is None else {len(lefts) + len(rights) + len(extras): 0},
        scratch_shapes=[pltpu.VMEM((height, depth), bfloat)],
        compiler_params=pltpu.CompilerParams(
            vmem_limit_bytes=18 * 2**20, dimension_semantics=("arbitrary",)
        ),
        cost_estimate=pl.CostEstimate(
            flops=2 * depth * height * count * tile,
            bytes_accessed=2 * (depth + height) * count * tile + 2 * depth * height,
            transcendentals=0,
        ),
        name="plane_grads",
    )(*lefts, *(right for _, right in rights), *extras, *([] if into is None else [into]))


def columns_of(weight, side, width):
    return lax.dynamic_slice_in_dim(weight, side * width, width, 1)


def rows_of(weight, side, width):
    return lax.dynamic_slice_in_dim(weight, side * width, width, 0)


def in_order(zh, own, other, axis):
    first = jnp.where(zh == 0, own, other)
    second = jnp.where(zh == 0, other, own)
    return jnp.concatenate([first, second], axis=axis)


def gather_plane(block):
    whole = lax.all_gather(block, PLANE, axis=1, tiled=True)
    return whole.reshape(-1, block.shape[-1])


def per_device(
    tokens,
    query_weight,
    key_weight,
    value_weight,
    gate_weight,
    out_weight,
    norm_gain,
    query_gain,
    key_gain,
    inner_gate,
    inner_lift,
    inner_down,
    inner_gain,
    out_grad,
    bucket_len,
    seq_len,
    home_block,
):
    zh = lax.axis_index("zh")
    zl = lax.axis_index("zl")
    c = lax.axis_index("c")
    mine = zl * 2 + c
    width = tokens.shape[1]
    seq_index = zh * 16 + lax.axis_index("y") * 4 + lax.axis_index("x")
    block_own = lax.dynamic_index_in_dim(home_block, seq_index, 0, keepdims=False)
    block_other = lax.dynamic_index_in_dim(home_block, seq_index ^ 16, 0, keepdims=False)
    info = jnp.stack(
        [
            block_own,
            block_other,
            zl,
            c,
            zh,
            bucket_len[0],
            seq_len[0],
            seq_len[1],
            lax.axis_index("y"),
            lax.axis_index("x"),
        ]
    ).astype(jnp.int32)

    lane = jnp.arange(HD, dtype=jnp.int32)

    def head_gain(vector):
        return jnp.where(lane // 4 == seq_index, jnp.tile(vector, 32), 0)

    norm_columns = jnp.pad(jnp.stack([norm_gain, inner_gain], axis=1), ((0, 0), (0, HD - 2)))
    head_rows = jnp.pad(
        jnp.stack([head_gain(query_gain), head_gain(key_gain)], axis=0), ((0, 62), (0, 0))
    ).astype(bfloat)

    def inner_pack(side):
        gate, lift, down = inner_shards
        return jnp.concatenate(
            [columns_of(gate, side, 768), columns_of(lift, side, 768), rows_of(down, side, 768).T],
            axis=1,
        )

    def pair_up(pack):
        own = pack(zh)
        other = swap(pack(1 - zh), "zh")
        return in_order(zh, own[None], other[None], 0)

    own_pack, sent_pack = pack(
        zh.astype(jnp.int32).reshape(1),
        key_weight,
        value_weight,
        query_weight,
        gate_weight,
        out_weight.T,
        jnp.concatenate([norm_columns, head_rows], axis=1),
    )
    first_block = in_order(zh, own_pack[None], swap(sent_pack, "zh")[None], 0)

    index = jnp.arange(512, dtype=jnp.int32)
    half_of = (index >> 7) & 1
    place = jnp.where(half_of == 0, block_own, block_other) * BLOCK + row_place(
        ((index >> 8) << 7) | (index & 127), zl, c
    )
    offset = jnp.where(place >= bucket_len[0], place - bucket_len[0], place)
    freq = jnp.power(THETA, -jnp.arange(HD // 2, dtype=single) * 2.0 / HD)
    angle = offset.astype(single)[:, None] * freq[None, :]
    cosine = jnp.cos(angle)
    sine = jnp.sin(angle)
    cosine = jnp.concatenate([cosine, cosine], axis=1)
    sine = jnp.concatenate([-sine, sine], axis=1)

    first_block, cosine, sine, info = lax.optimization_barrier((first_block, cosine, sine, info))
    tokens_other = swap(tokens, "zh")
    pairs_block, outer_block = first_block[:, :, : 4 * HD], first_block[:, :, 4 * HD :]
    outer = gather_plane(outer_block)
    pairs_wide = pairs_block.reshape(HD, 4 * HD)
    weight_pieces, _ = plane_gather(pairs_wide[:, : 2 * HD], pairs_wide[:, 2 * HD :], (), False)
    normed, key_rot, value, k_pre, w_pairs, gains, head_gains = project_pairs(
        info, tokens, tokens_other, cosine, sine, weight_pieces
    )
    key_rot, inner_shards = lax.optimization_barrier(
        (key_rot, (inner_gate, inner_lift, inner_down))
    )
    inner_block = pair_up(inner_pack)
    gain_norm, gain_inner = gains[0:1], gains[1:2]
    gain_query, gain_key = head_gains[0:1], head_gains[1:2]
    w_heads = outer[:, :512]
    w_out = outer[:, 512:]
    query, q_pre, gate_sig = project_query(normed, outer, cosine, sine, head_gains)
    pieces, (inner_block, out_grad_sent) = plane_gather(
        key_rot, value, (inner_block, out_grad), True
    )
    rows_grad = arrange(info, out_grad, swap(out_grad_sent, "zh"))
    inner = gather_plane(inner_block)
    w_gate_lift = inner[:, :1536]
    w_down = inner[:, 1536:]
    query, rows_grad = lax.optimization_barrier((query, rows_grad))
    attended, logs = attend(info, home_block, query, pieces)
    gated = (attended * gate_sig).astype(bfloat)

    def line_product(left, right):
        return line_sum(dot_nt(left[:256], right), dot_nt(left[256:], right))

    inputs = rows_of(tokens, mine, 64).astype(single)
    mixed_in = inputs + line_product(gated, w_out)
    unit_two, factor_two = rms_parts(mixed_in)
    normed_two = line_gather((unit_two * gain_inner).astype(bfloat))
    d_hidden = jnp.dot(rows_grad, w_down, preferred_element_type=single)
    gate_lift = jnp.dot(normed_two, w_gate_lift, preferred_element_type=single)
    gate_val = gate_lift[:, :768]
    lift_val = gate_lift[:, 768:]
    gate_act = jax.nn.sigmoid(gate_val)
    hidden = (gate_val * gate_act * lift_val).astype(bfloat)
    d_gate = (d_hidden * lift_val * gate_act * (1.0 + gate_val * (1.0 - gate_act))).astype(bfloat)
    d_lift = (d_hidden * gate_val * gate_act).astype(bfloat)
    d_gate_lift = jnp.concatenate([d_gate, d_lift], axis=1)

    def inner_grads(needs):
        return plane_grads(
            [normed_two, rows_grad],
            [(0, needs[0]), (0, needs[1]), (1, needs[2])],
            384,
        )

    d_normed_two, grad_inner = line_sum_end(
        line_sum_middle(dot_nt(d_gate_lift[:256], w_gate_lift), dot_nt(d_gate_lift[256:], w_gate_lift)),
        (inner_grads, (d_gate, d_lift, hidden)),
    )

    def scatter_plane(grad):
        part = lax.psum_scatter(grad, PLANE, scatter_dimension=0, tiled=False)
        return part.reshape(2, 64, -1)

    part = scatter_plane(grad_inner)
    d_mixed = rows_grad[:64].astype(single) + rms_back(
        d_normed_two, unit_two, factor_two, gain_inner
    )
    d_attn = line_gather(d_mixed.astype(bfloat))
    d_gated = jnp.dot(d_attn, w_out, preferred_element_type=single)
    d_attended = (d_gated * gate_sig).astype(bfloat)
    d_gate_pre = (d_gated * attended * gate_sig * (1.0 - gate_sig)).astype(bfloat)

    def rounded(rows):
        return lax.reduce_precision(rows, 8, 7).astype(bfloat)

    def both_sides(part):
        own = lax.dynamic_index_in_dim(part, zh, 0, keepdims=False).astype(single)
        sent = lax.dynamic_index_in_dim(part, 1 - zh, 0, keepdims=False).astype(bfloat)
        sent, part = lax.optimization_barrier((sent, part))
        return own, swap(sent, "zh").astype(single), part

    d_q_pre, query_gain_part, d_keys, d_values = attend_back(
        info,
        home_block,
        query,
        d_attended,
        attended,
        logs,
        q_pre,
        cosine,
        sine,
        head_gains,
        pieces,
    )
    grad_outer = plane_grads(
        [d_attn, normed], [(0, gated), (1, d_gate_pre), (1, d_q_pre)], 256, by_x=True
    )
    d_heads = jnp.concatenate([d_q_pre, d_gate_pre], axis=1)

    d_key, d_value, grad_outer, (normed_near, normed_far) = plane_sum(
        d_keys,
        d_values,
        grad_outer,
        (dot_nt(d_heads[:256], w_heads), dot_nt(d_heads[256:], w_heads)),
    )
    grad_outer, part = lax.optimization_barrier((grad_outer, part))
    rest = lax.psum_scatter(
        grad_outer.reshape(4, 4, 128, -1), "x", scatter_dimension=0, tiled=False
    )
    own_y = lax.axis_index("y")
    rest = [
        lax.dynamic_index_in_dim(rest, (own_y + step) & 3, 0, keepdims=False) for step in range(4)
    ]
    rest = [rest[0]] + [shift(rest[step], "y", step) for step in range(1, 4)]
    k_unit, k_factor = rms_parts(k_pre)
    d_k_turned = d_key * cosine - jnp.roll(d_key, HD // 2, axis=1) * sine
    key_gain_part = jnp.sum(d_k_turned * k_unit, axis=0, keepdims=True)
    d_k_pre = rms_back(d_k_turned, k_unit, k_factor, gain_key).astype(bfloat)
    d_kv_pre = jnp.concatenate([d_k_pre, d_value.astype(bfloat)], axis=1)
    normed_far = (normed_far + dot_nt(d_kv_pre[256:], w_pairs)).astype(bfloat)
    normed_far, d_kv_pre = lax.optimization_barrier((normed_far, d_kv_pre))
    pairs_sent = plane_grads(
        [normed], [(0, d_kv_pre)], 256, rows=144, extras=(query_gain_part, key_gain_part)
    )
    pairs_sent, d_kv_pre = lax.optimization_barrier((pairs_sent, d_kv_pre))
    normed_near = normed_near + dot_nt(d_kv_pre[:256], w_pairs)
    pairs_got = lax.all_to_all(pairs_sent, PLANE, 0, 0, tiled=True)
    here, hidden = lax.optimization_barrier((line_sum_middle(normed_near, normed_far), hidden))
    d_normed = line_sum_end(here)
    result_rows = mixed_in + line_product(hidden, w_down)
    unit_in, factor_in = rms_parts(inputs)
    token_rows = d_mixed + rms_back(d_normed, unit_in, factor_in, gain_norm)

    part_own, part_got, part = both_sides(part)
    pairs_got, rest, token_rows, part_got = lax.optimization_barrier(
        (pairs_got, rest, token_rows, part_got)
    )
    one, two, three, four = (value.astype(single) for value in rest)
    rest = ((one + two) + (three + four)).reshape(2, 64, -1)
    pairs_sum = jnp.sum(pairs_got.astype(single), axis=0)
    result, (pairs_sum, part) = head_gather(rounded(result_rows), mine, (pairs_sum, part))
    gain_part = pairs_sum[128]
    pair_part = pairs_sum[:128].reshape(2, 64, 256)
    tokens_grad = head_gather(rounded(token_rows), mine)

    def weighted(block, part):
        return jnp.sum(block.astype(single) * part.astype(single), axis=2)

    norm_part = (
        weighted(outer_block[:, :, :256], rest[:, :, 512:])
        + weighted(outer_block[:, :, 256:512], rest[:, :, 256:512])
        + weighted(pairs_block[:, :, :HD], pair_part[:, :, :HD])
        + weighted(pairs_block[:, :, 2 * HD : 3 * HD], pair_part[:, :, HD:])
    ) / pairs_block[:, :, HD].astype(single)
    inner_gain_part = weighted(inner_block[:, :, :1536], part[:, :, :1536]) / pairs_block[
        :, :, HD + 1
    ].astype(single)
    gain_line = jnp.concatenate(
        [
            norm_part.reshape(HD),
            inner_gain_part.reshape(HD),
            gain_part,
        ]
    ).reshape(4, HD)
    gain_line = lax.reduce_precision(gain_line, 8, 7)
    last = jnp.concatenate([rest.astype(single), pair_part], axis=2)
    last_own = lax.dynamic_index_in_dim(last, zh, 0, keepdims=False)
    last_sent = lax.dynamic_index_in_dim(last, 1 - zh, 0, keepdims=False)
    last_got = swap(
        jnp.concatenate([last_sent, jnp.pad(gain_line, ((0, 60), (0, 0)))], axis=1).astype(bfloat),
        "zh",
    ).astype(single)
    gain_line = head_sum(gain_line + last_got[:4, 1024:])

    def shard(own, got, start, count):
        return in_order(zh, own[:, start : start + count], got[:, start : start + count], 1)

    shard_igate = shard(part_own, part_got, 0, 768)
    shard_ilift = shard(part_own, part_got, 768, 768)
    shard_idown = shard(part_own, part_got, 1536, 768).T
    shard_out = shard(last_own, last_got, 0, 256).T
    shard_gate = shard(last_own, last_got, 256, 256)
    shard_query = shard(last_own, last_got, 512, 256)
    shard_key = shard(last_own, last_got, 768, 128)
    shard_value = shard(last_own, last_got, 896, 128)

    gain_own = lax.dynamic_index_in_dim(gain_line[:2].reshape(2, 2, 64), zh, 1, keepdims=False)
    gain_sides = lax.dynamic_slice_in_dim(gain_line[2:], seq_index * 4, 4, 1)

    return (
        result,
        tokens_grad,
        shard_query,
        shard_key,
        shard_value,
        shard_gate,
        shard_out,
        gain_own[0],
        gain_sides[0],
        gain_sides[1],
        shard_igate,
        shard_ilift,
        shard_idown,
        gain_own[1],
    )


def solution(mesh):
    fine = Mesh(mesh.devices.reshape(2, 4, 4, 2, 2), ("zh", "y", "x", "zl", "c"))
    seq = ("zh", "y", "x")
    head = ("zl", "c")
    in_specs = (
        P(seq, None),
        P(seq, head),
        P(seq, head),
        P(seq, head),
        P(seq, head),
        P(head, seq),
        P(seq),
        P(seq),
        P(seq),
        P(seq, head),
        P(seq, head),
        P(head, seq),
        P(seq),
        P(seq, None),
        P(),
        P(),
        P(),
    )
    out_specs = (
        P(seq, None),
        P(seq, None),
        P(seq, head),
        P(seq, head),
        P(seq, head),
        P(seq, head),
        P(head, seq),
        P(seq),
        P(seq),
        P(seq),
        P(seq, head),
        P(seq, head),
        P(head, seq),
        P(seq),
    )
    return jax.shard_map(
        per_device, mesh=fine, in_specs=in_specs, out_specs=out_specs, check_vma=False
    )
```
